32 devices in a mesh: pages: 8 (over z, x), blk: 4 (over y, core).
Axes of the slice: x: 2, y: 2, z: 4, core: 2. Of those that a mesh axis runs over, the one named last changes fastest.
Arguments:
- hidden: bfloat16 [8, 512, 768], P('pages', 'blk'), may hold values from -6 to 6
- boxes: int32 [8, 512, 2], P('pages', 'blk'), may hold values from 0 to 255
- lengths: int32 [8], P('pages'), may hold values from 40 to 512, as said below
- w_qkv: bfloat16 [768, 2304], P(('pages', 'blk')), may hold values from -0.21875 to 0.21875
- b_qkv: bfloat16 [2304], P(('pages', 'blk')), may hold values from -1.1953125 to 1.1953125
- w_relq: bfloat16 [768, 768], P(('pages', 'blk')), may hold values from -0.21875 to 0.21875
- w_relk: bfloat16 [768, 768], P(('pages', 'blk')), may hold values from -0.21875 to 0.21875
- w_out: bfloat16 [768, 768], P(('pages', 'blk')), may hold values from -0.875 to 0.875
- b_out: bfloat16 [768], P(('pages', 'blk')), may hold values from -1.1953125 to 1.1953125
- ln1_gain: bfloat16 [768], P(('pages', 'blk')), may hold values from 0.5 to 1.5
- ln1_bias: bfloat16 [768], P(('pages', 'blk')), may hold values from -1.1953125 to 1.1953125
- w_up: bfloat16 [768, 3072], P(('pages', 'blk')), may hold values from -0.21875 to 0.21875
- b_up: bfloat16 [3072], P(('pages', 'blk')), may hold values from -1.1953125 to 1.1953125
- w_down: bfloat16 [3072, 768], P(('pages', 'blk')), may hold values from -0.21875 to 0.21875
- b_down: bfloat16 [768], P(('pages', 'blk')), may hold values from -1.1953125 to 1.1953125
- ln2_gain: bfloat16 [768], P(('pages', 'blk')), may hold values from 0.5 to 1.5
- ln2_bias: bfloat16 [768], P(('pages', 'blk')), may hold values from -1.1953125 to 1.1953125
- cotangent: bfloat16 [8, 512, 768], P('pages', 'blk'), may hold values from -6 to 6
Outputs:
- output: bfloat16 [8, 512, 768], P('pages', 'blk')
- grad_hidden: bfloat16 [8, 512, 768], P('pages', 'blk')
- grad_w_qkv: float32 [768, 2304], P(('pages', 'blk'))
- grad_b_qkv: float32 [2304], P(('pages', 'blk'))
- grad_w_relq: float32 [768, 768], P(('pages', 'blk'))
- grad_w_relk: float32 [768, 768], P(('pages', 'blk'))
- grad_w_out: float32 [768, 768], P(('pages', 'blk'))
- grad_b_out: float32 [768], P(('pages', 'blk'))
- grad_ln1_gain: float32 [768], P(('pages', 'blk'))
- grad_ln1_bias: float32 [768], P(('pages', 'blk'))
- grad_w_up: float32 [768, 3072], P(('pages', 'blk'))
- grad_b_up: float32 [3072], P(('pages', 'blk'))
- grad_w_down: float32 [3072, 768], P(('pages', 'blk'))
- grad_b_down: float32 [768], P(('pages', 'blk'))
- grad_ln2_gain: float32 [768], P(('pages', 'blk'))
- grad_ln2_bias: float32 [768], P(('pages', 'blk'))
The draws below stay inside these ranges and needn't reach their ends.
Inputs may be any that keep to these rules, and one draw needn't show every extreme that they name: `lengths`: exactly one page has all 512 slots real; the others have fewer than 512.
All inputs are finite; a program needn't handle non-finite values.
Results may differ from the reference program's by a relative error of at most 0.025.
Values may be sent and summed in bfloat16 or wider, within the bound.
A program may use at most 256 MiB of HBM per device.

```python
import math
import jax
import jax.numpy as jnp
from jax import lax

D = 768
HEAD_DIM = 64
FF = 3072
FREQ = 192
PAGE = 512
MIN_LEN = 40
PAGES = 8


def draw_lengths(key, part):
    key = jax.random.fold_in(key, 7)
    base_key, pick_key = jax.random.split(key)
    drawn_lens = jax.random.randint(base_key, (PAGES,), MIN_LEN, PAGE)
    chosen = jax.random.randint(pick_key, (), 0, PAGES)
    full_page = jnp.arange(PAGES) == chosen
    return jnp.where(full_page, PAGE, drawn_lens).astype(jnp.int32)


def place_ends(entries, key, least, top_value):
    spot = [jax.random.randint(jax.random.fold_in(key, axis), (), 0, length) for axis, length in enumerate(entries.shape)]
    widest = entries.shape.index(max(entries.shape))
    next_to = spot[:widest] + [(spot[widest] + 1) % entries.shape[widest]] + spot[widest + 1:]
    return entries.at[tuple(spot)].set(least).at[tuple(next_to)].set(top_value)


def with_spikes(drawn, rng, source, target, shards_of, factor):
    def block_of(position):
        return (jnp.arange(drawn.shape[position]) // (drawn.shape[position] // shards_of)).reshape((-1,) + (1,) * (drawn.ndim - 1 - position))

    one_side = jax.random.permutation(rng, shards_of)[block_of(target)]
    far = (block_of(target) + shards_of // 2) % shards_of
    return jnp.where((block_of(source) == one_side) | (block_of(source) == far), factor * drawn, drawn)


def block_scale(rng, shape, cuts, least, largest):
    def one(axis_at, blocks):
        heights = jax.random.uniform(jax.random.fold_in(jax.random.fold_in(rng, 6), axis_at), (blocks,), jnp.float32, least / len(cuts), largest / len(cuts))
        return jnp.repeat(jnp.exp(heights), shape[axis_at] // blocks).reshape((-1,) + (1,) * (len(shape) - axis_at - 1))

    level = one(*cuts[0])
    for cut in cuts[1:]:
        level = level * one(*cut)
    return level


def noise(rng, extent, scale, most, shards=(), kind=jnp.bfloat16):
    level = block_scale(rng, extent, shards, -0.22, 0.18) if shards else 1.0
    values = jax.random.normal(rng, extent, jnp.float32) * scale * level
    return jnp.minimum(jnp.maximum(values, -most), most).astype(kind)


def bell_draw_with(rng, extent, scale, limit, cuts, heavy, held_as=jnp.bfloat16):
    entries = scale * jax.random.normal(rng, extent, jnp.float32)
    if cuts:
        entries = entries * block_scale(rng, extent, cuts, -0.22, 0.18)
    return jnp.clip(with_spikes(entries, jax.random.fold_in(rng, 3), *heavy), -limit, limit).astype(held_as)


def setup_inputs(seed: int = 0) -> dict:
    key_list = jax.random.split(jax.random.key(seed), 19)
    return {
        "hidden": noise(key_list[0], (PAGES, PAGE, D), 1.0, 6.0, ((0, 8), (1, 4))),
        "boxes": place_ends(jax.random.randint(key_list[1], (PAGES, PAGE, 2), 0, 256), jax.random.fold_in(key_list[1], 1), 0, 255).astype(jnp.int32),
        "lengths": draw_lengths(jax.random.fold_in(key_list[18], 71), 0),
        "w_qkv": noise(key_list[3], (D, 3 * D), D ** -0.5, 0.21875, ((0, 32),)),
        "b_qkv": noise(key_list[4], (3 * D,), 0.2, 1.1953125, ((0, 32),)),
        "w_relq": noise(key_list[5], (4 * FREQ, D), (4 * FREQ) ** -0.5, 0.21875, ((0, 32),)),
        "w_relk": noise(key_list[6], (4 * FREQ, D), (4 * FREQ) ** -0.5, 0.21875, ((0, 32),)),
        "w_out": noise(key_list[7], (D, D), (D // 16) ** -0.5, 0.875, ((0, 32),)),
        "b_out": noise(key_list[8], (D,), 0.2, 1.1953125, ((0, 32),)),
        "ln1_gain": jnp.clip(1.0 + 0.1 * jax.random.normal(key_list[9], (D,), jnp.float32), 0.5, 1.5).astype(jnp.bfloat16),
        "ln1_bias": noise(key_list[10], (D,), 0.2, 1.1953125, ((0, 32),)),
        "w_up": noise(key_list[11], (D, FF), D ** -0.5, 0.21875, ((0, 32),)),
        "b_up": noise(key_list[12], (FF,), 0.2, 1.1953125, ((0, 32),)),
        "w_down": noise(key_list[13], (FF, D), (FF // 4) ** -0.5, 0.21875, ((0, 32),)),
        "b_down": noise(key_list[14], (D,), 0.2, 1.1953125, ((0, 32),)),
        "ln2_gain": jnp.clip(1.0 + 0.1 * jax.random.normal(key_list[15], (D,), jnp.float32), 0.5, 1.5).astype(jnp.bfloat16),
        "ln2_bias": noise(key_list[16], (D,), 0.2, 1.1953125, ((0, 32),)),
        "cotangent": bell_draw_with(key_list[17], (PAGES, PAGE, D), 1.0, 6.0, ((0, 8), (1, 4)), (0, 2, 8, 2.0)),
    }


@jax.custom_vjp
def low(v):
    return lax.optimization_barrier(v.astype(jnp.bfloat16)).astype(jnp.float32)

@jax.custom_vjp
def low_back(v):
    return v

def low_keep(v):
    return (low(v), None)

def low_pass(kept, grad):
    return (grad,)

def back_keep(v):
    return (v, None)

def back_low(kept, grad):
    return (low(grad),)
low.defvjp(low_keep, low_pass)
low_back.defvjp(back_keep, back_low)
precise = lax.Precision.HIGHEST

def box_features(boxes):
    ladder = jnp.arange(FREQ).astype(jnp.float32)
    rates = jnp.exp(ladder * (-math.log(10000.0) / FREQ))
    coords = boxes.astype(jnp.float32)
    angles = jnp.concatenate([coords[..., 0:1] * rates, coords[..., 1:2] * rates], axis=-1)
    return jnp.concatenate([jnp.cos(angles), jnp.sin(angles)], axis=-1)

def turn_query(rel_vals, cos_part, sin_part):
    middle = rel_vals.shape[-1] // 2
    lead_part, tail_part = (rel_vals[..., :middle], rel_vals[..., middle:])
    cos_wide = cos_part[..., None, :]
    sin_wide = sin_part[..., None, :]
    return jnp.concatenate([lead_part * cos_wide + tail_part * sin_wide, lead_part * sin_wide - tail_part * cos_wide], axis=-1)

def turn_key(rel_vals, cos_part, sin_part):
    middle = rel_vals.shape[-1] // 2
    lead_part, tail_part = (rel_vals[..., :middle], rel_vals[..., middle:])
    cos_wide = cos_part[..., None, :]
    sin_wide = sin_part[..., None, :]
    return jnp.concatenate([lead_part * cos_wide - tail_part * sin_wide, lead_part * sin_wide + tail_part * cos_wide], axis=-1)

def normalize(values, gain, shift):
    centre = values - lax.optimization_barrier(jnp.mean(values, axis=-1, keepdims=True))
    spread = lax.optimization_barrier(jnp.mean(centre * centre, axis=-1, keepdims=True))
    return centre * lax.rsqrt(spread + 1e-12) * gain + shift

def page_layer(hidden_part, box_part, length_part, weight_set):
    w_qkv, b_qkv, w_relq, w_relk, w_out, b_out, ln1_gain, ln1_bias, w_up, b_up, w_down, b_down, ln2_gain, ln2_bias = weight_set
    group_size, page_len, width = hidden_part.shape
    heads = width // HEAD_DIM
    span = 2 * FREQ
    feats = low(box_features(box_part))
    cos_part, sin_part = (feats[..., :span], feats[..., span:])
    qkv = jnp.einsum('gtd,de->gte', hidden_part, w_qkv, precision=precise) + b_qkv
    qkv = low_back(low(qkv))
    queries = qkv[..., :width].reshape(group_size, page_len, heads, HEAD_DIM)
    key_rows = qkv[..., width:2 * width].reshape(group_size, page_len, heads, HEAD_DIM)
    value_rows = qkv[..., 2 * width:].reshape(group_size, page_len, heads, HEAD_DIM)
    rel_in = jnp.einsum('gthc,rhc->gthr', queries, w_relq.reshape(2 * span, heads, HEAD_DIM), precision=precise)
    query_rel = low(turn_query(low_back(rel_in), cos_part, sin_part))
    key_in = jnp.einsum('gthc,rhc->gthr', key_rows, w_relk.reshape(2 * span, heads, HEAD_DIM), precision=precise)
    key_rel = low(turn_key(low_back(key_in), cos_part, sin_part))
    scores = jnp.einsum('gqhc,gkhc->ghqk', queries, key_rows, precision=precise)
    scores = scores + jnp.einsum('gqhr,gkr->ghqk', query_rel, feats, precision=precise)
    scores = scores + jnp.einsum('gqr,gkhr->ghqk', feats, key_rel, precision=precise)
    scores = low_back(scores * 0.125)
    usable = (jnp.arange(page_len)[None, :] < length_part[:, None])[:, None, None, :]
    masked = jnp.where(usable, scores, -1e+30)
    row_max = lax.optimization_barrier(jnp.max(masked, axis=-1, keepdims=True))
    exp_terms = jnp.where(usable, jnp.exp(masked - row_max), 0.0)
    attention = low(exp_terms / lax.optimization_barrier(jnp.sum(exp_terms, axis=-1, keepdims=True)))
    context = jnp.einsum('ghqk,gkhc->gqhc', attention, value_rows, precision=precise)
    ctx_low = low_back(low(context.reshape(group_size, page_len, width)))
    attn_out = low_back(jnp.einsum('gtd,de->gte', ctx_low, w_out, precision=precise) + b_out)
    normed_one = normalize(hidden_part + attn_out, ln1_gain, ln1_bias)
    middle_rows = low_back(jnp.einsum('gtd,de->gte', low(normed_one), w_up, precision=precise) + b_up)
    activated = low(jax.nn.gelu(middle_rows, approximate=False))
    branch_out = low_back(jnp.einsum('gtd,de->gte', activated, w_down, precision=precise) + b_down)
    return normalize(normed_one + branch_out, ln2_gain, ln2_bias)

def reference(hidden, boxes, lengths, w_qkv, b_qkv, w_relq, w_relk, w_out, b_out, ln1_gain, ln1_bias, w_up, b_up, w_down, b_down, ln2_gain, ln2_bias, cotangent):
    weight_set = (w_qkv.astype(jnp.float32), b_qkv.astype(jnp.float32), w_relq.astype(jnp.float32), w_relk.astype(jnp.float32), w_out.astype(jnp.float32), b_out.astype(jnp.float32), ln1_gain.astype(jnp.float32), ln1_bias.astype(jnp.float32), w_up.astype(jnp.float32), b_up.astype(jnp.float32), w_down.astype(jnp.float32), b_down.astype(jnp.float32), ln2_gain.astype(jnp.float32), ln2_bias.astype(jnp.float32))
    group_size = math.gcd(PAGES, 8)
    group_count = PAGES // group_size
    hidden_all = hidden.astype(jnp.float32).reshape(group_count, group_size, PAGE, D)
    box_all = boxes.reshape(group_count, group_size, PAGE, 2)
    length_all = lengths.reshape(group_count, group_size)

    def forward(hidden_in, weights_in):

        def one_group(carry, pieces):
            return (carry, page_layer(pieces[0], pieces[1], pieces[2], weights_in))
        _, outputs = lax.scan(jax.checkpoint(one_group), jnp.zeros((), jnp.float32), (hidden_in, box_all, length_all))
        return outputs
    outputs, pullback = jax.vjp(forward, hidden_all, weight_set)
    grad_in, grads = pullback(cotangent.astype(jnp.float32).reshape(group_count, group_size, PAGE, D))
    return (outputs.reshape(PAGES, PAGE, D).astype(jnp.bfloat16), grad_in.reshape(PAGES, PAGE, D).astype(jnp.bfloat16), grads[0], grads[1], grads[2], grads[3], grads[4], grads[5], grads[6], grads[7], grads[8], grads[9], grads[10], grads[11], grads[12], grads[13])
```

```python
import functools
import math

import jax
import jax.numpy as jnp
from jax import lax
from jax.experimental import pallas as pl
from jax.experimental.pallas import tpu as pltpu
from jax.sharding import PartitionSpec as P

HEAD_DIM = 64
FREQ = 192
GRID_Z = 4
GRID_X = 2
GROUP = GRID_Z * GRID_X
BLK = 4
MESH = pl.DeviceIdType.MESH
F32 = jnp.float32
BF16 = jnp.bfloat16
VMEM_BYTES = 56 << 20


def mm(left, right):
    return jnp.dot(left, right, preferred_element_type=F32)


def mm_t(left, right):
    return lax.dot_general(left, right, (((1,), (1,)), ((), ())), preferred_element_type=F32)


def tmm(left, right):
    return lax.dot_general(left, right, (((0,), (0,)), ((), ())), preferred_element_type=F32)


class Place:
    def __init__(self, spread):
        pages = lax.axis_index("pages")
        self.spread = spread
        self.hi = pages // spread
        self.lo = pages % spread
        self.z = self.hi // GRID_X
        self.x = self.hi % GRID_X
        self.b = lax.axis_index("blk")
        self.pages = pages
        self.sib = self.b + 1 - 2 * (self.b % 2)
        self.across = (self.b + 2) % BLK
        self.diag = (self.sib + 2) % BLK

    def at(self, z, x):
        return ((z * GRID_X + x) * self.spread + self.lo, self.b)

    def in_page(self, b):
        return (self.pages, b)

    def blk_peers(self):
        return (self.sib, self.across, self.diag)

    def z_at(self, step):
        return (self.z + step) % GRID_Z


def remote(src, dst, send, recv, device):
    return pltpu.make_async_remote_copy(
        src_ref=src, dst_ref=dst, send_sem=send, recv_sem=recv, device_id=device, device_id_type=MESH
    )


def meet(devices):
    barrier = pltpu.get_barrier_semaphore()
    for device in devices:
        pl.semaphore_signal(barrier, inc=1, device_id=device, device_id_type=MESH)
    pl.semaphore_wait(barrier, len(devices))


class BlkGather:
    def __init__(self, place, dst, send, recv):
        self.place, self.dst = place, dst
        b, across = place.b, place.across
        self.to_sib = remote(dst.at[b], dst.at[b], send.at[0], recv.at[0], place.in_page(place.sib))
        self.to_across = remote(dst.at[b], dst.at[b], send.at[1], recv.at[1], place.in_page(across))
        self.forward = remote(
            dst.at[across], dst.at[across], send.at[2], recv.at[2], place.in_page(place.sib)
        )

    def start(self):
        self.to_across.start()
        self.to_sib.start()

    def wait_sib(self):
        self.to_sib.wait_recv()

    def wait_across(self):
        self.to_across.wait_recv()
        self.forward.start()

    def wait_diag(self):
        self.forward.wait_recv()

    def finish(self):
        self.to_sib.wait_send()
        self.to_across.wait_send()
        self.forward.wait_send()


class BlkReduce:
    def __init__(self, place, parts, near, far, send, recv):
        self.place, self.parts, self.near, self.far = place, parts, near, far
        sib, across = place.sib, place.across
        self.sib_far = remote(
            parts.at[place.diag], near.at[1], send.at[0], recv.at[0], place.in_page(sib)
        )
        self.sib_near = remote(parts.at[sib], near.at[0], send.at[1], recv.at[1], place.in_page(sib))
        self.cross = remote(near.at[1], far, send.at[2], recv.at[2], place.in_page(across))

    def send_cross(self):
        self.sib_far.wait_recv()
        both = self.parts[self.place.across].astype(F32) + self.near[1].astype(F32)
        self.near[1] = both.astype(BF16)
        self.cross.start()

    def total(self, own):
        self.sib_near.wait_recv()
        partial = own + self.near[0].astype(F32)
        self.cross.wait_recv()
        return partial + self.far[...].astype(F32)

    def finish(self):
        self.sib_far.wait_send()
        self.sib_near.wait_send()
        self.cross.wait_send()


def gather_kernel(
    spread,
    pack_a,
    pack_b,
    down,
    hidden,
    box,
    vec,
    all_a,
    all_b,
    all_c,
    all_hid,
    all_box,
    all_out,
    vec_sum,
    land_a,
    land_b,
    land_vec,
    all_vec,
    aa_send,
    aa_recv,
    z_send,
    z_recv,
    x_send,
    x_recv,
    bg_send,
    bg_recv,
):
    place = Place(spread)
    peers = place.blk_peers()
    meet(
        [place.in_page(peer) for peer in peers]
        + [place.at(place.z, 1 - place.x)]
        + [place.at(place.z_at(step), place.x) for step in range(1, GRID_Z)]
    )

    def exchange(which, pack, land):
        copies = []
        for slot, peer in enumerate(peers):
            copies.append(
                remote(
                    pack.at[peer],
                    land.at[slot],
                    aa_send.at[which, slot],
                    aa_recv.at[which, slot],
                    place.in_page(peer),
                )
            )
            copies[-1].start()
        return copies

    def spread_out(which, whole):
        copies = []
        own = whole.at[place.hi]
        copies.append(
            remote(own, own, x_send.at[which, 0], x_recv.at[which, 0], place.at(place.z, 1 - place.x))
        )
        for step in range(1, GRID_Z):
            copies.append(
                remote(
                    own,
                    own,
                    z_send.at[which, step - 1],
                    z_recv.at[which, step - 1],
                    place.at(place.z_at(step), place.x),
                )
            )
        for copy in copies:
            copy.start()
        return copies

    def pass_on(which, whole, copies):
        more = []
        for step in range(1, GRID_Z):
            copies[step].wait_recv()
            came = whole.at[place.z_at(GRID_Z - step) * GRID_X + place.x]
            more.append(
                remote(
                    came,
                    came,
                    x_send.at[which, step],
                    x_recv.at[which, step],
                    place.at(place.z, 1 - place.x),
                )
            )
            more[-1].start()
        return more

    def settle(copies, more):
        copies[0].wait_recv()
        for copy in more:
            copy.wait_recv()
        for copy in copies + more:
            copy.wait_send()

    swap_a = exchange(0, pack_a, land_a)
    swap_vec = exchange(1, vec, land_vec)
    all_hid[place.b] = hidden[...]
    all_box[place.b] = box[...]
    gather_hid = BlkGather(place, all_hid, bg_send.at[0], bg_recv.at[0])
    gather_box = BlkGather(place, all_box, bg_send.at[1], bg_recv.at[1])
    gather_box.start()
    gather_hid.start()
    swap_b = exchange(2, pack_b, land_b)
    all_c[place.hi] = down[...]
    def join(pack, land, copies, whole):
        for copy in copies:
            copy.wait_recv()
        held = [pack[place.b].astype(F32)] + [land[slot].astype(F32) for slot in range(3)]
        owners = [place.b] + list(peers)
        parts = []
        for blk in range(BLK):
            part = held[0]
            for other in range(1, BLK):
                part = jnp.where(owners[other] == blk, held[other], part)
            parts.append(part)
        whole[place.hi] = jnp.concatenate(parts, axis=0).astype(BF16)

    join(pack_a, land_a, swap_a, all_a)
    sent_a = spread_out(0, all_a)
    for copy in swap_vec:
        copy.wait_recv()
    whole_vec = vec[place.b].astype(F32)
    for slot in range(3):
        whole_vec = whole_vec + land_vec[slot].astype(F32)
    all_vec[place.hi] = whole_vec.astype(BF16)
    sent_vec = spread_out(3, all_vec)
    sent_c = spread_out(2, all_c)
    join(pack_b, land_b, swap_b, all_b)
    sent_b = spread_out(1, all_b)

    gather_box.wait_across()
    gather_hid.wait_across()
    more_a = pass_on(0, all_a, sent_a)
    more_vec = pass_on(3, all_vec, sent_vec)
    settle(sent_a, more_a)
    own_out = jnp.concatenate([all_a[shard][:, 960:1152] for shard in range(GROUP)], axis=0)
    all_out[place.b] = own_out
    gather_out = BlkGather(place, all_out, bg_send.at[2], bg_recv.at[2])
    gather_out.start()
    more_b = pass_on(1, all_b, sent_b)
    gather_out.wait_across()
    more_c = pass_on(2, all_c, sent_c)
    settle(sent_vec, more_vec)
    total = all_vec[0].astype(F32)
    for shard in range(1, GROUP):
        total = total + all_vec[shard].astype(F32)
    vec_sum[...] = total
    settle(sent_c, more_c)
    settle(sent_b, more_b)
    for gather in (gather_box, gather_hid, gather_out):
        gather.wait_sib()
        gather.wait_diag()
        gather.finish()
    for copy in swap_a + swap_vec + swap_b:
        copy.wait_send()


def vmem_call(kernel, outs, scratch, name, collective=None, smem=()):
    def run(*operands):
        params = dict(vmem_limit_bytes=VMEM_BYTES)
        if collective is not None:
            params.update(collective_id=collective, has_side_effects=True)
        return pl.pallas_call(
            kernel,
            name=name,
            out_shape=[jax.ShapeDtypeStruct(shape, kind) for shape, kind in outs],
            in_specs=[
                pl.BlockSpec(memory_space=pltpu.SMEM if i in smem else pltpu.VMEM)
                for i in range(len(operands))
            ],
            out_specs=[pl.BlockSpec(memory_space=pltpu.VMEM) for _ in outs],
            scratch_shapes=scratch,
            compiler_params=pltpu.CompilerParams(**params),
        )(*operands)

    return run


def attend_kernel(
    lengths, w_a, hid, box, vec, qkv, ctx, probs, feats, relq, relk, qrel, krel
):
    tokens, width = hid.shape
    span = 2 * FREQ
    places = lax.broadcasted_iota(jnp.int32, (256, FREQ), 0).astype(F32)
    ladder = lax.broadcasted_iota(jnp.int32, (256, FREQ), 1).astype(F32)
    angles = places * jnp.exp(ladder * (-math.log(10000.0) / FREQ))
    cosines, sines, blank = jnp.cos(angles), jnp.sin(angles), jnp.zeros((256, FREQ), F32)
    table = jnp.concatenate(
        [
            jnp.concatenate([cosines, blank, sines, blank], axis=1),
            jnp.concatenate([blank, cosines, blank, sines], axis=1),
        ],
        axis=0,
    ).astype(BF16)
    slots = lax.broadcasted_iota(jnp.int32, (256, tokens // BLK), 0)
    for blk in range(BLK):
        hot = jnp.concatenate(
            [
                jnp.where(slots == box[blk][0:1, :], 1.0, 0.0),
                jnp.where(slots == box[blk][1:2, :], 1.0, 0.0),
            ],
            axis=0,
        ).astype(BF16)
        feats[blk * 128 : (blk + 1) * 128, :] = tmm(hot, table).astype(BF16)

    bias = vec[0:1, : 9 * HEAD_DIM]
    for blk in range(BLK):
        rows = slice(blk * 128, (blk + 1) * 128)
        low = (mm(hid[rows, :], w_a[:, : 9 * HEAD_DIM]) + bias).astype(BF16)
        for part in range(9):
            qkv[part, rows, :] = low[:, part * HEAD_DIM : (part + 1) * HEAD_DIM]
    for head in range(3):
        start = 9 * HEAD_DIM + head * HEAD_DIM
        relq[head] = w_a[:, start : start + HEAD_DIM]
        relk[head] = w_a[:, start + 3 * HEAD_DIM : start + 4 * HEAD_DIM]

    usable = lax.broadcasted_iota(jnp.int32, (128, tokens), 1) < lengths[0]

    for head in range(3):

        def turn(blk, carry):
            rows = pl.ds(pl.multiple_of(blk * 128, 128), 128)
            cos_part = feats[rows, :span].astype(F32)
            sin_part = feats[rows, span:].astype(F32)
            u = mm_t(qkv[head, rows, :], relq[head])
            u1, u2 = u[:, :span], u[:, span:]
            qrel[rows, :span] = (u1 * cos_part + u2 * sin_part).astype(BF16)
            qrel[rows, span:] = (u1 * sin_part - u2 * cos_part).astype(BF16)
            v = mm_t(qkv[3 + head, rows, :], relk[head])
            v1, v2 = v[:, :span], v[:, span:]
            krel[rows, :span] = (v1 * cos_part - v2 * sin_part).astype(BF16)
            krel[rows, span:] = (v1 * sin_part + v2 * cos_part).astype(BF16)
            return carry

        lax.fori_loop(0, BLK, turn, 0)

        def rows_of(blk, carry):
            rows = pl.ds(pl.multiple_of(blk * 128, 128), 128)
            scores = mm_t(qrel[rows, :], feats[...])
            scores = scores + mm_t(feats[rows, :], krel[...])
            scores = scores + mm_t(qkv[head, rows, :], qkv[3 + head])
            masked = jnp.where(usable, scores * 0.125, -1e30)
            raised = jnp.exp(masked - jnp.max(masked, axis=-1, keepdims=True))
            prob = raised / jnp.sum(raised, axis=-1, keepdims=True)
            probs[head, rows, :] = prob
            ctx[rows, head * HEAD_DIM : (head + 1) * HEAD_DIM] = mm(
                prob.astype(BF16), qkv[6 + head]
            ).astype(BF16)
            return carry

        lax.fori_loop(0, BLK, rows_of, 0)


def centred(values):
    mean = jnp.mean(values, axis=-1, keepdims=True)
    centre = values - mean
    scale = lax.rsqrt(jnp.mean(centre * centre, axis=-1, keepdims=True) + 1e-12)
    return centre * scale, scale


def norm_back(grad_hat, hat, scale):
    first = jnp.mean(grad_hat, axis=-1, keepdims=True)
    second = jnp.mean(grad_hat * hat, axis=-1, keepdims=True)
    return scale * (grad_hat - first - hat * second)


def column_sum(values):
    return jnp.sum(values, axis=0, keepdims=True)


def middle_kernel(
    spread,
    ctx,
    hid,
    cot,
    vec,
    w_out,
    w_up,
    w_down,
    out,
    g_one_out,
    g_ctx,
    grad_out,
    grad_up,
    grad_down,
    grad_vec,
    ctx_own,
    ctx_all,
    normed_all,
    act,
    slope,
    parts_one,
    near_one,
    far_one,
    branch_all,
    parts_two,
    near_two,
    far_two,
    g_attn_own,
    g_attn_cols,
    g_ctx_own,
    ca_send,
    ca_recv,
    bg_send,
    bg_recv,
    br_send,
    br_recv,
):
    place = Place(spread)
    b = place.b
    peers = place.blk_peers()
    order = (b, place.sib, place.across, place.diag)
    width = hid.shape[1]
    third = 3 * HEAD_DIM
    meet([place.in_page(peer) for peer in peers])

    def exchange(which, source_of, target):
        copies = []
        for slot, peer in enumerate(peers):
            copies.append(
                remote(
                    source_of(peer),
                    target.at[b],
                    ca_send.at[which, slot],
                    ca_recv.at[which, slot],
                    place.in_page(peer),
                )
            )
            copies[-1].start()
        return copies

    def recv_all(copies):
        for copy in copies:
            copy.wait_recv()

    swap_ctx = exchange(0, lambda peer: ctx.at[peer], ctx_own)
    spread_ctx = exchange(1, lambda peer: ctx, ctx_all)
    ctx_own[b] = ctx[b]
    ctx_all[b] = ctx[...]
    recv_all(swap_ctx)
    own = jnp.concatenate([ctx_own[blk] for blk in range(BLK)], axis=1)
    attn = jnp.concatenate([mm(own, w_out[blk]) for blk in range(BLK)], axis=1) + vec[2:3, :]
    hat_one, scale_one = centred(hid[...].astype(F32) + attn)
    gain_one = vec[3:4, :]
    normed = hat_one * gain_one + vec[4:5, :]
    normed_all[b] = normed.astype(BF16)
    gather = BlkGather(place, normed_all, bg_send.at[0], bg_recv.at[0])
    gather.start()
    reduce = BlkReduce(place, parts_one, near_one, far_one, br_send.at[0], br_recv.at[0])
    own_branch = None
    for step, blk in enumerate(order):
        if step == 1:
            gather.wait_sib()
        elif step == 2:
            gather.wait_across()
        elif step == 3:
            gather.wait_diag()
        middle = mm(normed_all[blk], w_up[...]) + vec[1:2, :]
        half = 0.5 * (1.0 + lax.erf(middle * math.sqrt(0.5)))
        act[blk] = (middle * half).astype(BF16)
        slope[blk] = half + middle * jnp.exp(-0.5 * middle * middle) * (1.0 / math.sqrt(2.0 * math.pi))
        part = mm(act[blk], w_down[...])
        if step == 0:
            own_branch = part
        else:
            parts_one[blk] = part.astype(BF16)
        if step == 1:
            reduce.sib_near.start()
        elif step == 3:
            reduce.sib_far.start()
    reduce.send_cross()
    gather.finish()
    branch = reduce.total(own_branch) + vec[5:6, :]
    reduce.finish()
    hat_two, scale_two = centred(normed + branch)
    gain_two = vec[6:7, :]
    out[...] = (hat_two * gain_two + vec[7:8, :]).astype(BF16)
    cot_wide = cot[...].astype(F32)
    grad_vec[6:7, :] = column_sum(cot_wide * hat_two)
    grad_vec[7:8, :] = column_sum(cot_wide)
    g_two = norm_back(cot_wide * gain_two, hat_two, scale_two)
    g_branch = g_two.astype(BF16)
    branch_all[b] = g_branch
    gather = BlkGather(place, branch_all, bg_send.at[1], bg_recv.at[1])
    gather.start()
    grad_vec[5:6, :] = column_sum(g_branch.astype(F32))
    reduce = BlkReduce(place, parts_two, near_two, far_two, br_send.at[1], br_recv.at[1])
    up_bias = jnp.zeros((1, width), F32)
    for step, blk in enumerate(order):
        if step == 1:
            gather.wait_sib()
        elif step == 2:
            gather.wait_across()
        elif step == 3:
            gather.wait_diag()
        g_middle = (mm_t(branch_all[blk], w_down[...]) * slope[blk]).astype(BF16)
        up_bias = up_bias + column_sum(g_middle.astype(F32))
        slope[blk] = g_middle.astype(F32)
        part = mm_t(g_middle, w_up[...])
        if step == 0:
            own_branch = part
        else:
            parts_two[blk] = part.astype(BF16)
        if step == 1:
            reduce.sib_near.start()
        elif step == 3:
            reduce.sib_far.start()
    grad_vec[1:2, :] = up_bias
    reduce.send_cross()
    gather.finish()

    act_rows = act.reshape(4 * act.shape[1], act.shape[2])
    branch_rows = branch_all.reshape(4 * act.shape[1], width)
    normed_rows = normed_all.reshape(4 * act.shape[1], width)
    slope_rows = slope.reshape(4 * act.shape[1], act.shape[2])

    def down_rows(at, carry):
        cols = pl.ds(pl.multiple_of(at * 128, 128), 128)
        grad_down[cols, :] = tmm(act_rows[:, cols], branch_rows[...]).astype(BF16)
        return carry

    lax.fori_loop(0, act.shape[2] // 128, down_rows, 0)

    g_normed = g_two + reduce.total(own_branch)
    reduce.finish()
    grad_vec[3:4, :] = column_sum(g_normed * hat_one)
    grad_vec[4:5, :] = column_sum(g_normed)
    g_one = norm_back(g_normed * gain_one, hat_one, scale_one)
    g_one_out[...] = g_one
    g_attn = g_one.astype(BF16)
    grad_vec[2:3, :] = column_sum(g_attn.astype(F32))
    for blk in range(BLK):
        cols = g_attn[:, blk * third : (blk + 1) * third]
        g_attn_own[blk] = cols
    swap_attn = exchange(2, lambda peer: g_attn_own.at[peer], g_attn_cols)
    g_attn_cols[b] = g_attn_own[b]
    g_ctx_wide = jnp.zeros(g_one.shape, F32)
    for blk in range(BLK):
        g_ctx_wide = g_ctx_wide + mm_t(g_attn_own[blk], w_out[blk])
    for blk in range(BLK):
        g_ctx_own[blk] = g_ctx_wide[:, blk * third : (blk + 1) * third].astype(BF16)
    swap_back = exchange(3, lambda peer: g_ctx_own.at[peer], g_ctx)
    g_ctx[b] = g_ctx_own[b]

    g_middle_low = slope_rows[...].astype(BF16)

    act[...] = g_middle_low.reshape(act.shape)

    def up_rows(at, carry):
        cols = pl.ds(pl.multiple_of(at * 128, 128), 128)
        grad_up[cols, :] = tmm(normed_rows[:, cols], act_rows[...]).astype(BF16)
        return carry

    lax.fori_loop(0, width // 128, up_rows, 0)
    recv_all(swap_attn)
    recv_all(spread_ctx)
    columns = g_attn_cols.reshape(4 * act.shape[1], third)[...]
    for blk in range(BLK):
        heads = ctx_all[blk].reshape(4 * act.shape[1], third)
        grad_out[blk * third : (blk + 1) * third, :] = tmm(heads, columns).astype(BF16)
    recv_all(swap_back)
    for copy in swap_ctx + spread_ctx + swap_attn + swap_back:
        copy.wait_send()
    grad_vec[0:1, :] = jnp.zeros((1, width), F32)


def attend_back_kernel(
    w_a,
    hid,
    qkv,
    ctx,
    g_ctx,
    probs,
    feats,
    relq,
    relk,
    grad_a,
    part_hid,
    grad_bias,
    g_scores,
    p_low,
    g_turned_q,
    g_turned_k,
    g_heads,
    go_heads,
    g_qkv,
):
    tokens, width = hid.shape
    span = 2 * FREQ
    nine = 9 * HEAD_DIM
    for head in range(3):
        lanes = slice(head * HEAD_DIM, (head + 1) * HEAD_DIM)
        go_heads[...] = g_ctx[:, lanes]

        def query_rows(blk, carry):
            rows = pl.ds(pl.multiple_of(blk * 128, 128), 128)
            go = go_heads[rows, :]
            delta = jnp.sum(
                go.astype(F32) * ctx[rows, lanes].astype(F32), axis=-1, keepdims=True
            )
            prob = probs[head, rows, :]
            p_low[rows, :] = prob.astype(BF16)
            ds = (prob * (mm_t(go, qkv[6 + head]) - delta)).astype(BF16)
            g_scores[rows, :] = ds
            turned = 0.125 * mm(ds, feats[...])
            a1, a2 = turned[:, :span], turned[:, span:]
            cos_part = feats[rows, :span].astype(F32)
            sin_part = feats[rows, span:].astype(F32)
            g_turned_q[rows, :span] = (a1 * cos_part + a2 * sin_part).astype(BF16)
            g_turned_q[rows, span:] = (a1 * sin_part - a2 * cos_part).astype(BF16)
            gq = 0.125 * mm(ds, qkv[3 + head]) + mm(g_turned_q[rows, :], relq[head])
            g_heads[head, rows, :] = gq.astype(BF16)
            return carry

        lax.fori_loop(0, BLK, query_rows, 0)

        def key_rows(blk, carry):
            rows = pl.ds(pl.multiple_of(blk * 128, 128), 128)
            ds = g_scores[:, rows]
            turned = 0.125 * tmm(ds, feats[...])
            b1, b2 = turned[:, :span], turned[:, span:]
            cos_part = feats[rows, :span].astype(F32)
            sin_part = feats[rows, span:].astype(F32)
            g_turned_k[rows, :span] = (b1 * cos_part + b2 * sin_part).astype(BF16)
            g_turned_k[rows, span:] = (b2 * cos_part - b1 * sin_part).astype(BF16)
            gk = 0.125 * tmm(ds, qkv[head]) + mm(g_turned_k[rows, :], relk[head])
            g_heads[3 + head, rows, :] = gk.astype(BF16)
            g_heads[6 + head, rows, :] = tmm(p_low[:, rows], go_heads[...]).astype(BF16)
            return carry

        lax.fori_loop(0, BLK, key_rows, 0)
        start = nine + head * HEAD_DIM
        grad_a[:, start : start + HEAD_DIM] = tmm(g_turned_q[...], qkv[head]).astype(BF16)
        start = start + 3 * HEAD_DIM
        grad_a[:, start : start + HEAD_DIM] = tmm(g_turned_k[...], qkv[3 + head]).astype(BF16)
    g_qkv[...] = jnp.concatenate([g_heads[part] for part in range(9)], axis=1)
    grad_bias[0:1, :nine] = column_sum(g_qkv[...].astype(F32))
    grad_bias[0:1, nine:] = jnp.zeros((1, width - nine), F32)
    for blk in range(BLK):
        part_hid[blk] = mm_t(g_qkv[blk * 128 : (blk + 1) * 128, :], w_a[:, :nine]).astype(BF16)

    def weight_rows(at, carry):
        cols = pl.ds(pl.multiple_of(at * 128, 128), 128)
        grad_a[cols, :nine] = tmm(hid[:, cols], g_qkv[...]).astype(BF16)
        return carry

    lax.fori_loop(0, width // 128, weight_rows, 0)


def reduce_kernel(
    spread,
    grad_a,
    grad_b,
    grad_c,
    part_hid,
    g_one,
    sum_a,
    sum_b,
    sum_c,
    grad_hid,
    pair_a,
    pair_b,
    pair_c,
    line_a,
    line_b,
    line_c,
    cut_a,
    cut_b,
    near,
    far,
    x_send,
    x_recv,
    z_send,
    z_recv,
    aa_send,
    aa_recv,
    br_send,
    br_recv,
):
    place = Place(spread)
    peers = place.blk_peers()
    meet(
        [place.in_page(peer) for peer in peers]
        + [place.at(place.z, 1 - place.x)]
        + [place.at(place.z_at(step), place.x) for step in range(1, GRID_Z)]
    )
    chunks = ((grad_c, pair_c, line_c), (grad_b, pair_b, line_b), (grad_a, pair_a, line_a))

    def shard(step, x):
        return place.z_at(step) * GRID_X + x

    def to_partner(which):
        grad, pair, _ = chunks[which]
        copies = []
        for step in range(GRID_Z):
            copies.append(
                remote(
                    grad.at[shard(step, 1 - place.x)],
                    pair.at[step],
                    x_send.at[which, step],
                    x_recv.at[which, step],
                    place.at(place.z, 1 - place.x),
                )
            )
        for step in (1, 2, 3, 0):
            copies[step].start()
        return copies

    def to_line(which, copies):
        grad, pair, line = chunks[which]
        more = []
        for step in range(1, GRID_Z):
            copies[step].wait_recv()
            both = grad[shard(step, place.x)].astype(F32) + pair[step].astype(F32)
            pair[step] = both.astype(BF16)
            more.append(
                remote(
                    pair.at[step],
                    line.at[step - 1],
                    z_send.at[which, step - 1],
                    z_recv.at[which, step - 1],
                    place.at(place.z_at(step), place.x),
                )
            )
            more[-1].start()
        return more

    def total(which, copies, more):
        grad, pair, line = chunks[which]
        copies[0].wait_recv()
        value = grad[shard(0, place.x)].astype(F32) + pair[0].astype(F32)
        for step in range(1, GRID_Z):
            more[step - 1].wait_recv()
            value = value + line[step - 1].astype(F32)
        return value

    def cut(which, value, pieces, target):
        rows = value.shape[0] // BLK
        for blk in range(BLK):
            pieces[blk] = value[blk * rows : (blk + 1) * rows, :].astype(BF16)
        target[place.b] = pieces[place.b]
        copies = []
        for slot, peer in enumerate(peers):
            copies.append(
                remote(
                    pieces.at[peer],
                    target.at[place.b],
                    aa_send.at[which, slot],
                    aa_recv.at[which, slot],
                    place.in_page(peer),
                )
            )
            copies[-1].start()
        return copies

    first = [to_partner(which) for which in range(3)]
    reduce = BlkReduce(place, part_hid, near, far, br_send, br_recv)
    reduce.sib_far.start()
    reduce.sib_near.start()
    second = [to_line(0, first[0])]
    reduce.send_cross()
    second.append(to_line(1, first[1]))
    own = part_hid[place.b].astype(F32) + g_one[...]
    grad_hid[...] = reduce.total(own).astype(BF16)
    reduce.finish()
    second.append(to_line(2, first[2]))
    sum_c[...] = total(0, first[0], second[0])
    last = cut(0, total(1, first[1], second[1]), cut_b, sum_b)
    last = last + cut(1, total(2, first[2], second[2]), cut_a, sum_a)
    for copy in last:
        copy.wait_recv()
        copy.wait_send()
    for copies in first + second:
        for copy in copies:
            copy.wait_send()


def on_device(
    hidden,
    boxes,
    lengths,
    w_qkv,
    b_qkv,
    w_relq,
    w_relk,
    w_out,
    b_out,
    ln1_gain,
    ln1_bias,
    w_up,
    b_up,
    w_down,
    b_down,
    ln2_gain,
    ln2_bias,
    cotangent,
):
    page_count = lax.axis_size("pages")
    spread = page_count // GROUP
    b = lax.axis_index("blk")
    hi = lax.axis_index("pages") // spread
    _, tok, width = hidden.shape
    third = 3 * HEAD_DIM
    groups = [[h * spread + low for low in range(spread)] for h in range(GROUP)]

    def grow(rows):
        if spread == 1:
            return rows
        rows = lax.all_gather(rows, "blk", axis=0, tiled=True)
        rows = lax.all_gather(rows, "pages", axis=0, tiled=True, axis_index_groups=groups)
        count = rows.shape[0] // BLK
        return lax.dynamic_slice_in_dim(rows, b * count, count, 0)

    def shrink(rows):
        if spread == 1:
            return rows
        rows = lax.all_gather(rows, "blk", axis=0, tiled=True)
        rows = lax.psum_scatter(
            rows, "pages", scatter_dimension=0, tiled=True, axis_index_groups=groups
        )
        count = rows.shape[0] // BLK
        return lax.dynamic_slice_in_dim(rows, b * count, count, 0)

    w_qkv, w_relq, w_relk, w_out, w_up, w_down = map(
        grow, (w_qkv, w_relq, w_relk, w_out, w_up, w_down)
    )
    b_qkv, b_up, b_out, ln1_gain, ln1_bias, b_down, ln2_gain, ln2_bias = map(
        grow, (b_qkv, b_up, b_out, ln1_gain, ln1_bias, b_down, ln2_gain, ln2_bias)
    )
    rows = w_qkv.shape[0]
    shard = BLK * rows
    ff_part = w_up.shape[1] // (GROUP * BLK)

    def by_head(weight):
        return weight.reshape(rows, BLK, third).transpose(1, 0, 2)

    pack_a = jnp.concatenate(
        [
            w_qkv.reshape(rows, 3, BLK, third).transpose(2, 0, 1, 3).reshape(BLK, rows, 3 * third),
            by_head(w_relq),
            by_head(w_relk),
            by_head(w_out),
        ],
        axis=-1,
    )
    pack_b = (
        w_up.reshape(rows, GROUP, BLK, ff_part)
        .transpose(2, 0, 1, 3)
        .reshape(BLK, rows, GROUP * ff_part)
    )
    here = (lax.iota(jnp.int32, GROUP * BLK) == hi * BLK + b).astype(BF16)
    spot = here[:, None]
    own_bias = (spot * b_qkv[None, :]).reshape(3, BLK, third).transpose(1, 0, 2)
    own_bias = own_bias.reshape(BLK, 3 * third)
    own_bias = jnp.pad(own_bias, ((0, 0), (0, width - 3 * third)))
    up_spot = (spot * b_up[None, :]).reshape(GROUP, BLK, ff_part).transpose(1, 0, 2)
    up_spot = up_spot.reshape(BLK, GROUP * ff_part)
    plain = jnp.stack([b_out, ln1_gain, ln1_bias, b_down, ln2_gain, ln2_bias])
    plain = (spot[None] * plain[:, None, :]).reshape(6, width)
    vec = jnp.concatenate(
        [
            own_bias[:, None, :],
            up_spot[:, None, :],
            jnp.broadcast_to(plain[None], (BLK, 6, width)),
            jnp.zeros((BLK, 8, width), BF16),
        ],
        axis=1,
    )
    box = jnp.pad(boxes[0].T, ((0, 6), (0, 0)))

    hid = hidden[0]
    sem = pltpu.SemaphoreType.DMA
    cols_a, cols_b = pack_a.shape[-1], pack_b.shape[-1]
    all_a, all_b, all_c, all_hid, all_box, all_out, vec_sum = vmem_call(
        functools.partial(gather_kernel, spread),
        [
            ((GROUP, shard, cols_a), BF16),
            ((GROUP, shard, cols_b), BF16),
            ((GROUP, shard, width), BF16),
            ((BLK, tok, width), BF16),
            ((BLK, 8, tok), jnp.int32),
            ((BLK, GROUP * shard, third), BF16),
            ((16, width), F32),
        ],
        [
            pltpu.VMEM((3, rows, cols_a), BF16),
            pltpu.VMEM((3, rows, cols_b), BF16),
            pltpu.VMEM((3, 16, width), BF16),
            pltpu.VMEM((GROUP, 16, width), BF16),
            sem((3, 3)),
            sem((3, 3)),
            sem((4, 3)),
            sem((4, 3)),
            sem((4, 4)),
            sem((4, 4)),
            sem((3, 3)),
            sem((3, 3)),
        ],
        "gather",
        collective=1,
    )(pack_a, pack_b, w_down, hid, box, vec)
    w_a = all_a.reshape(GROUP * shard, cols_a)
    w_b = all_b.reshape(GROUP * shard, cols_b)
    w_c = all_c.reshape(GROUP * shard, width)
    hid_page = all_hid.reshape(BLK * tok, width)
    tokens = BLK * tok

    qkv, ctx, probs, feats, relq, relk = vmem_call(
        attend_kernel,
        [
            ((9, tokens, HEAD_DIM), BF16),
            ((tokens, third), BF16),
            ((3, tokens, tokens), F32),
            ((tokens, width), BF16),
            ((3, width, HEAD_DIM), BF16),
            ((3, width, HEAD_DIM), BF16),
        ],
        [pltpu.VMEM((tokens, width), BF16), pltpu.VMEM((tokens, width), BF16)],
        "attend",
        smem=(0,),
    )(lengths, w_a, hid_page, all_box, vec_sum)

    block = pltpu.VMEM((BLK, tok, width), BF16)
    thirds = pltpu.VMEM((BLK, tok, third), BF16)
    two, one = pltpu.VMEM((2, tok, width), BF16), pltpu.VMEM((tok, width), BF16)
    out, g_one, g_ctx, grad_out, grad_b, grad_c, grad_vec = vmem_call(
        functools.partial(middle_kernel, spread),
        [
            ((tok, width), BF16),
            ((tok, width), F32),
            ((BLK, tok, third), BF16),
            ((GROUP * shard, third), BF16),
            ((GROUP * shard, cols_b), BF16),
            ((GROUP * shard, width), BF16),
            ((8, width), F32),
        ],
        [
            thirds,
            pltpu.VMEM((BLK, BLK, tok, third), BF16),
            block,
            pltpu.VMEM((BLK, tok, cols_b), BF16),
            pltpu.VMEM((BLK, tok, cols_b), F32),
            block,
            two,
            one,
            block,
            block,
            two,
            one,
            thirds,
            thirds,
            thirds,
            sem((4, 3)),
            sem((4, 3)),
            sem((2, 3)),
            sem((2, 3)),
            sem((2, 3)),
            sem((2, 3)),
        ],
        "middle",
        collective=2,
    )(ctx.reshape(BLK, tok, third), hid, cotangent[0], vec_sum, all_out, w_b, w_c)

    grad_a, part_hid, grad_bias = vmem_call(
        attend_back_kernel,
        [
            ((width, 5 * third), BF16),
            ((BLK, tok, width), BF16),
            ((1, width), F32),
        ],
        [
            pltpu.VMEM((tokens, tokens), BF16),
            pltpu.VMEM((tokens, tokens), BF16),
            pltpu.VMEM((tokens, width), BF16),
            pltpu.VMEM((tokens, width), BF16),
            pltpu.VMEM((9, tokens, HEAD_DIM), BF16),
            pltpu.VMEM((tokens, HEAD_DIM), BF16),
            pltpu.VMEM((tokens, 3 * third), BF16),
        ],
        "attend_back",
    )(w_a, hid_page, qkv, ctx, g_ctx.reshape(tokens, third), probs, feats, relq, relk)
    grad_a = jnp.concatenate([grad_a, grad_out], axis=1).reshape(GROUP, shard, cols_a)

    sum_a, sum_b, sum_c, grad_hid = vmem_call(
        functools.partial(reduce_kernel, spread),
        [
            ((BLK, rows, cols_a), BF16),
            ((BLK, rows, cols_b), BF16),
            ((shard, width), F32),
            ((tok, width), BF16),
        ],
        [
            pltpu.VMEM((GRID_Z, shard, cols_a), BF16),
            pltpu.VMEM((GRID_Z, shard, cols_b), BF16),
            pltpu.VMEM((GRID_Z, shard, width), BF16),
            pltpu.VMEM((GRID_Z - 1, shard, cols_a), BF16),
            pltpu.VMEM((GRID_Z - 1, shard, cols_b), BF16),
            pltpu.VMEM((GRID_Z - 1, shard, width), BF16),
            pltpu.VMEM((BLK, rows, cols_a), BF16),
            pltpu.VMEM((BLK, rows, cols_b), BF16),
            two,
            one,
            sem((3, 4)),
            sem((3, 4)),
            sem((3, 3)),
            sem((3, 3)),
            sem((2, 3)),
            sem((2, 3)),
            sem((3,)),
            sem((3,)),
        ],
        "reduce",
        collective=3,
    )(
        grad_a,
        grad_b.reshape(GROUP, shard, cols_b),
        grad_c.reshape(GROUP, shard, width),
        part_hid,
        g_one,
    )

    def heads_back(cols):
        return cols.transpose(1, 0, 2).reshape(rows, BLK * third).astype(F32)

    grad_qkv = sum_a[:, :, : 3 * third].reshape(BLK, rows, 3, third).transpose(1, 2, 0, 3)
    grad_qkv = grad_qkv.reshape(rows, 3 * BLK * third).astype(F32)
    grad_relq = heads_back(sum_a[:, :, 3 * third : 4 * third])
    grad_relk = heads_back(sum_a[:, :, 4 * third : 5 * third])
    grad_w_out = heads_back(sum_a[:, :, 5 * third :])
    grad_up = sum_b.reshape(BLK, rows, GROUP, ff_part).transpose(1, 2, 0, 3)
    grad_up = grad_up.reshape(rows, GROUP * BLK * ff_part).astype(F32)

    mine = (lax.iota(jnp.int32, BLK) == b).astype(F32)
    count = page_count * BLK
    bias_parts = grad_bias[0, : 3 * third].reshape(3, 1, third) * mine[None, :, None]
    up_parts = grad_vec[1].reshape(GROUP, 1, ff_part) * mine[None, :, None]
    owned = jnp.concatenate(
        [bias_parts.reshape(count, -1), up_parts.reshape(count, -1)]
        + [grad_vec[row].reshape(count, -1) for row in range(2, 8)],
        axis=1,
    )
    vectors = lax.psum_scatter(owned, ("pages", "blk"), scatter_dimension=0, tiled=True)[0]
    sizes = [3 * BLK * third // count, GROUP * BLK * ff_part // count] + [width // count] * 6
    cuts = [sum(sizes[:at]) for at in range(len(sizes) + 1)]
    g_bias, g_up, g_out, g_gain1, g_shift1, g_down, g_gain2, g_shift2 = [
        vectors[cuts[at] : cuts[at + 1]] for at in range(8)
    ]
    return (
        out[None],
        grad_hid[None],
        shrink(grad_qkv),
        g_bias,
        shrink(grad_relq),
        shrink(grad_relk),
        shrink(grad_w_out),
        g_out,
        g_gain1,
        g_shift1,
        shrink(grad_up),
        g_up,
        shrink(sum_c),
        g_down,
        g_gain2,
        g_shift2,
    )


def solution(mesh):
    rows = P(("pages", "blk"), None)
    vector = P(("pages", "blk"))
    tokens = P("pages", "blk", None)
    return jax.shard_map(
        on_device,
        mesh=mesh,
        in_specs=(
            tokens,
            tokens,
            P("pages"),
            rows,
            vector,
            rows,
            rows,
            rows,
            vector,
            vector,
            vector,
            rows,
            vector,
            rows,
            vector,
            vector,
            vector,
            tokens,
        ),
        out_specs=(
            tokens,
            tokens,
            rows,
            vector,
            rows,
            rows,
            rows,
            vector,
            vector,
            vector,
            rows,
            vector,
            rows,
            vector,
            vector,
            vector,
        ),
        check_vma=False,
    )
```

```python
import functools
import math

import jax
import jax.numpy as jnp
from jax import lax
from jax.experimental import pallas as pl
from jax.experimental.pallas import tpu as pltpu
from jax.sharding import PartitionSpec as P

HEAD_DIM = 64
FREQ = 192
GRID_Z = 4
GRID_X = 2
GROUP = GRID_Z * GRID_X
BLK = 4
MESH = pl.DeviceIdType.MESH
F32 = jnp.float32
BF16 = jnp.bfloat16
VMEM_BYTES = 56 << 20


def mm(left, right):
    return jnp.dot(left, right, preferred_element_type=F32)


def mm_t(left, right):
    return lax.dot_general(left, right, (((1,), (1,)), ((), ())), preferred_element_type=F32)


def tmm(left, right):
    return lax.dot_general(left, right, (((0,), (0,)), ((), ())), preferred_element_type=F32)


class Place:
    def __init__(self, spread):
        pages = lax.axis_index("pages")
        self.spread = spread
        self.hi = pages // spread
        self.lo = pages % spread
        self.z = self.hi // GRID_X
        self.x = self.hi % GRID_X
        self.b = lax.axis_index("blk")
        self.pages = pages
        self.sib = self.b + 1 - 2 * (self.b % 2)
        self.across = (self.b + 2) % BLK
        self.diag = (self.sib + 2) % BLK

    def at(self, z, x):
        return ((z * GRID_X + x) * self.spread + self.lo, self.b)

    def in_page(self, b):
        return (self.pages, b)

    def blk_peers(self):
        return (self.sib, self.across, self.diag)

    def z_at(self, step):
        return (self.z + step) % GRID_Z


def remote(src, dst, send, recv, device):
    return pltpu.make_async_remote_copy(
        src_ref=src, dst_ref=dst, send_sem=send, recv_sem=recv, device_id=device, device_id_type=MESH
    )


def meet(devices):
    barrier = pltpu.get_barrier_semaphore()
    for device in devices:
        pl.semaphore_signal(barrier, inc=1, device_id=device, device_id_type=MESH)
    pl.semaphore_wait(barrier, len(devices))


class BlkGather:
    def __init__(self, place, dst, send, recv):
        self.place, self.dst = place, dst
        b, across = place.b, place.across
        self.to_sib = remote(dst.at[b], dst.at[b], send.at[0], recv.at[0], place.in_page(place.sib))
        self.to_across = remote(dst.at[b], dst.at[b], send.at[1], recv.at[1], place.in_page(across))
        self.forward = remote(
            dst.at[across], dst.at[across], send.at[2], recv.at[2], place.in_page(place.sib)
        )

    def start(self):
        self.to_across.start()
        self.to_sib.start()

    def wait_sib(self):
        self.to_sib.wait_recv()

    def wait_across(self):
        self.to_across.wait_recv()
        self.forward.start()

    def wait_diag(self):
        self.forward.wait_recv()

    def finish(self):
        self.to_sib.wait_send()
        self.to_across.wait_send()
        self.forward.wait_send()


class BlkReduce:
    def __init__(self, place, parts, near, far, send, recv):
        self.place, self.parts, self.near, self.far = place, parts, near, far
        sib, across = place.sib, place.across
        self.sib_far = remote(
            parts.at[place.diag], near.at[1], send.at[0], recv.at[0], place.in_page(sib)
        )
        self.sib_near = remote(parts.at[sib], near.at[0], send.at[1], recv.at[1], place.in_page(sib))
        self.cross = remote(near.at[1], far, send.at[2], recv.at[2], place.in_page(across))

    def send_cross(self):
        self.sib_far.wait_recv()
        both = self.parts[self.place.across].astype(F32) + self.near[1].astype(F32)
        self.near[1] = both.astype(BF16)
        self.cross.start()

    def total(self, own):
        self.sib_near.wait_recv()
        partial = own + self.near[0].astype(F32)
        self.cross.wait_recv()
        return partial + self.far[...].astype(F32)

    def finish(self):
        self.sib_far.wait_send()
        self.sib_near.wait_send()
        self.cross.wait_send()


def vmem_call(kernel, outs, scratch, name, collective=None, smem=()):
    def run(*operands):
        params = dict(vmem_limit_bytes=VMEM_BYTES)
        if collective is not None:
            params.update(collective_id=collective, has_side_effects=True)
        return pl.pallas_call(
            kernel,
            name=name,
            out_shape=[jax.ShapeDtypeStruct(shape, kind) for shape, kind in outs],
            in_specs=[
                pl.BlockSpec(memory_space=pltpu.SMEM if i in smem else pltpu.VMEM)
                for i in range(len(operands))
            ],
            out_specs=[pl.BlockSpec(memory_space=pltpu.VMEM) for _ in outs],
            scratch_shapes=scratch,
            compiler_params=pltpu.CompilerParams(**params),
        )(*operands)

    return run


HEADS = 3
HEAD_COLS = 6 * HEAD_DIM
A_CHUNKS, B_CHUNKS, C_CHUNKS = (0, 1, 2), (3, 4), (5, 6)
CHUNKS = 7
VEC = 7
SPAN = 2 * FREQ


def centred(values):
    mean = jnp.mean(values, axis=-1, keepdims=True)
    centre = values - mean
    scale = lax.rsqrt(jnp.mean(centre * centre, axis=-1, keepdims=True) + 1e-12)
    return centre * scale, scale


def norm_back(grad_hat, hat, scale):
    first = jnp.mean(grad_hat, axis=-1, keepdims=True)
    second = jnp.mean(grad_hat * hat, axis=-1, keepdims=True)
    return scale * (grad_hat - first - hat * second)


def column_sum(values):
    return jnp.sum(values, axis=0, keepdims=True)


def block_rows(blk):
    return pl.ds(pl.multiple_of(blk * 128, 128), 128)


def layer_kernel(
    spread,
    lengths,
    w_qkv,
    w_relq,
    w_relk,
    w_out,
    w_up,
    w_down,
    hidden,
    cot,
    box,
    vec,
    out,
    grad_hid,
    sums,
    sum_c,
    vec_out,
    weights,
    grads,
    pair,
    line,
    cut,
    pack_a,
    pack_b,
    land_a,
    land_b,
    land_vec,
    all_vec,
    all_hid,
    all_box,
    all_out,
    vec_sum,
    table,
    feats,
    qkv,
    relq,
    relk,
    qrel,
    krel,
    probs,
    ctx,
    ctx_own,
    ctx_all,
    normed_all,
    act,
    slope,
    branch_all,
    g_middle,
    parts,
    near,
    far,
    g_attn_own,
    g_attn_cols,
    g_ctx_own,
    g_ctx,
    go_heads,
    g_scores,
    p_low,
    g_heads,
    g_qkv,
    gvec,
    gvec_all,
    gvec_page,
    ag_x,
    ag_z,
    rs_x,
    rs_z,
    in_swap,
    gather_sem,
    reduce_sem,
    mid_swap,
    out_swap,
):
    place = Place(spread)
    b = place.b
    peers = place.blk_peers()
    order = (b, place.sib, place.across, place.diag)
    partner = place.at(place.z, 1 - place.x)
    width = hidden.shape[1]
    tokens = BLK * hidden.shape[0]
    third = HEADS * HEAD_DIM
    ff_part = w_up.shape[1] // (GROUP * BLK)
    sends = []


    def shard_at(step, x):
        return place.z_at(step) * GRID_X + x

    def start(copy):
        copy.start()
        sends.append(copy)
        return copy

    class Spread:
        def __init__(self, whole, index, sem_x, sem_z):
            self.whole, self.index, self.sem_x, self.sem_z = whole, index, sem_x, sem_z

        def begin(self):
            own = self.whole.at[place.hi]
            self.along = []
            for step in range(1, GRID_Z):
                self.along.append(
                    start(
                        remote(
                            own,
                            own,
                            self.sem_z.at[0, self.index, step - 1],
                            self.sem_z.at[1, self.index, step - 1],
                            place.at(place.z_at(step), place.x),
                        )
                    )
                )
            self.over = [self._over(own, 0)]

        def _over(self, ref, slot):
            return start(
                remote(
                    ref,
                    ref,
                    self.sem_x.at[0, self.index, slot],
                    self.sem_x.at[1, self.index, slot],
                    partner,
                )
            )

        def pass_on(self):
            for step in range(1, GRID_Z):
                self.along[step - 1].wait_recv()
                self.over.append(self._over(self.whole.at[shard_at(GRID_Z - step, place.x)], step))

        def settle(self):
            for copy in self.over:
                copy.wait_recv()

    class Sum:
        def __init__(self, index):
            self.index = index
            self.grad = grads.at[index]

        def begin(self):
            self.over = []
            for step in (1, 2, 3, 0):
                self.over.append(
                    start(
                        remote(
                            self.grad.at[shard_at(step, 1 - place.x)],
                            pair.at[self.index, step],
                            rs_x.at[0, self.index, step],
                            rs_x.at[1, self.index, step],
                            partner,
                        )
                    )
                )

        def pass_on(self):
            self.along = []
            for step in range(1, GRID_Z):
                self.over[step - 1].wait_recv()
                both = self.grad[shard_at(step, place.x)].astype(F32) + pair[
                    self.index, step
                ].astype(F32)
                pair[self.index, step] = both.astype(BF16)
                self.along.append(
                    start(
                        remote(
                            pair.at[self.index, step],
                            line.at[self.index, step - 1],
                            rs_z.at[0, self.index, step - 1],
                            rs_z.at[1, self.index, step - 1],
                            place.at(place.z_at(step), place.x),
                        )
                    )
                )

        def settle(self):
            index = self.index
            self.over[3].wait_recv()
            value = self.grad[shard_at(0, place.x)].astype(F32) + pair[index, 0].astype(F32)
            for step in range(1, GRID_Z):
                self.along[step - 1].wait_recv()
                value = value + line[index, step - 1].astype(F32)
            if index in C_CHUNKS:
                at = (index - C_CHUNKS[0]) * HEAD_COLS
                sum_c[:, at : at + HEAD_COLS] = value
                return []
            rows = value.shape[0] // BLK
            for blk in range(BLK):
                cut[index, blk] = value[blk * rows : (blk + 1) * rows, :].astype(BF16)
            sums[index, b] = cut[index, b]
            return [
                start(
                    remote(
                        cut.at[index, peer],
                        sums.at[index, b],
                        out_swap.at[0, index, slot],
                        out_swap.at[1, index, slot],
                        place.in_page(peer),
                    )
                )
                for slot, peer in enumerate(peers)
            ]

    def swap(sem, which, source_of, target):
        return [
            start(
                remote(
                    source_of(peer),
                    target.at[b],
                    sem.at[0, which, slot],
                    sem.at[1, which, slot],
                    place.in_page(peer),
                )
            )
            for slot, peer in enumerate(peers)
        ]

    def arrive(copies):
        for copy in copies:
            copy.wait_recv()

    def blk_gather(which, dst):
        return BlkGather(place, dst, gather_sem.at[0, which], gather_sem.at[1, which])

    def blk_reduce(which):
        return BlkReduce(
            place,
            parts.at[which],
            near.at[which],
            far.at[which],
            reduce_sem.at[0, which],
            reduce_sem.at[1, which],
        )


    for blk in range(BLK):
        for head in range(HEADS):
            at = blk * third + head * HEAD_DIM
            lanes = slice(at, at + HEAD_DIM)
            columns = [
                w_qkv[:, part * width + at : part * width + at + HEAD_DIM] for part in range(3)
            ]
            columns = columns + [w_relq[:, lanes], w_relk[:, lanes], w_out[:, lanes]]
            pack_a[blk, :, head * HEAD_COLS : (head + 1) * HEAD_COLS] = jnp.concatenate(
                columns, axis=1
            )
        pack_b[blk] = jnp.concatenate(
            [
                w_up[:, (page * BLK + blk) * ff_part : (page * BLK + blk + 1) * ff_part]
                for page in range(GROUP)
            ],
            axis=1,
        )
    all_hid[b] = hidden[...]
    all_box[b] = box[...]
    for half, index in enumerate(C_CHUNKS):
        weights[index, place.hi] = w_down[:, half * HEAD_COLS : (half + 1) * HEAD_COLS]

    meet(
        [place.in_page(peer) for peer in peers]
        + [partner]
        + [place.at(place.z_at(step), place.x) for step in range(1, GRID_Z)]
    )
    chunk = [Spread(weights.at[index], index, ag_x, ag_z) for index in range(CHUNKS)]
    chunk.append(Spread(all_vec, VEC, ag_x, ag_z))
    swap_a = swap(in_swap, 0, lambda peer: pack_a.at[peer], land_a)
    swap_vec = swap(in_swap, 1, lambda peer: vec.at[peer], land_vec)
    gather_box = blk_gather(0, all_box)
    gather_hid = blk_gather(1, all_hid)
    gather_box.start()
    gather_hid.start()
    chunk[5].begin()
    swap_b = swap(in_swap, 2, lambda peer: pack_b.at[peer], land_b)

    places = lax.broadcasted_iota(jnp.int32, (256, FREQ), 0).astype(F32)
    ladder = lax.broadcasted_iota(jnp.int32, (256, FREQ), 1).astype(F32)
    angles = places * jnp.exp(ladder * (-math.log(10000.0) / FREQ))
    cosines, sines, blank = jnp.cos(angles), jnp.sin(angles), jnp.zeros((256, FREQ), F32)
    table[0:256, :] = jnp.concatenate([cosines, blank, sines, blank], axis=1).astype(BF16)
    table[256:512, :] = jnp.concatenate([blank, cosines, blank, sines], axis=1).astype(BF16)

    land_a[b] = pack_a[b]
    arrive(swap_a)
    joined = jnp.concatenate([land_a[blk].astype(F32) for blk in range(BLK)], axis=0).astype(BF16)
    for head in range(HEADS):
        weights[head, place.hi] = joined[:, head * HEAD_COLS : (head + 1) * HEAD_COLS]
    chunk[0].begin()
    land_vec[b] = vec[b]
    arrive(swap_vec)
    all_vec[place.hi] = (
        land_vec[0].astype(F32)
        + land_vec[1].astype(F32)
        + land_vec[2].astype(F32)
        + land_vec[3].astype(F32)
    ).astype(BF16)
    chunk[VEC].begin()
    gather_box.wait_across()
    gather_hid.wait_across()
    chunk[1].begin()

    gather_box.wait_sib()
    gather_box.wait_diag()
    slots = lax.broadcasted_iota(jnp.int32, (256, tokens // BLK), 0)
    for blk in range(BLK):
        hot = jnp.concatenate(
            [
                jnp.where(slots == all_box[blk][0:1, :], 1.0, 0.0),
                jnp.where(slots == all_box[blk][1:2, :], 1.0, 0.0),
            ],
            axis=0,
        ).astype(BF16)
        feats[blk * 128 : (blk + 1) * 128, :] = tmm(hot, table[...]).astype(BF16)
    land_b[b] = pack_b[b]
    arrive(swap_b)
    joined = jnp.concatenate([land_b[blk].astype(F32) for blk in range(BLK)], axis=0).astype(BF16)
    for half, index in enumerate(B_CHUNKS):
        weights[index, place.hi] = joined[:, half * HEAD_COLS : (half + 1) * HEAD_COLS]
    chunk[5].pass_on()
    chunk[2].begin()
    chunk[VEC].pass_on()
    chunk[0].pass_on()
    chunk[3].begin()
    gather_hid.wait_sib()
    gather_hid.wait_diag()
    chunk[VEC].settle()
    total = all_vec[0].astype(F32)
    for shard in range(1, GROUP):
        total = total + all_vec[shard].astype(F32)
    vec_sum[...] = total

    rows_whole = GROUP * weights.shape[2]
    whole = weights.reshape(CHUNKS, rows_whole, HEAD_COLS)
    hid = all_hid.reshape(tokens, width)
    usable = lax.broadcasted_iota(jnp.int32, (128, tokens), 1) < lengths[0]

    def head_forward(head):
        bias = vec_sum[0:1, head * 3 * HEAD_DIM : (head + 1) * 3 * HEAD_DIM]

        def project(blk, carry):
            rows = block_rows(blk)
            low = (mm(hid[rows, :], whole[head, :, : 3 * HEAD_DIM]) + bias).astype(BF16)
            for part in range(3):
                qkv[3 * part + head, rows, :] = low[:, part * HEAD_DIM : (part + 1) * HEAD_DIM]
            return carry

        lax.fori_loop(0, BLK, project, 0)
        relq[head] = whole[head, :, 3 * HEAD_DIM : 4 * HEAD_DIM]
        relk[head] = whole[head, :, 4 * HEAD_DIM : 5 * HEAD_DIM]
        all_out[b, :, head * HEAD_DIM : (head + 1) * HEAD_DIM] = whole[
            head, :, 5 * HEAD_DIM : 6 * HEAD_DIM
        ]
        yield

        def turn(blk, carry):
            rows = block_rows(blk)
            cos_part = feats[rows, :SPAN].astype(F32)
            sin_part = feats[rows, SPAN:].astype(F32)
            u = mm_t(qkv[head, rows, :], relq[head])
            u1, u2 = u[:, :SPAN], u[:, SPAN:]
            qrel[rows, :SPAN] = (u1 * cos_part + u2 * sin_part).astype(BF16)
            qrel[rows, SPAN:] = (u1 * sin_part - u2 * cos_part).astype(BF16)
            v = mm_t(qkv[3 + head, rows, :], relk[head])
            v1, v2 = v[:, :SPAN], v[:, SPAN:]
            krel[rows, :SPAN] = (v1 * cos_part - v2 * sin_part).astype(BF16)
            krel[rows, SPAN:] = (v1 * sin_part + v2 * cos_part).astype(BF16)
            return carry

        lax.fori_loop(0, BLK, turn, 0)
        yield

        def rows_of(blk, carry):
            rows = block_rows(blk)
            scores = mm_t(qrel[rows, :], feats[...])
            scores = scores + mm_t(feats[rows, :], krel[...])
            scores = scores + mm_t(qkv[head, rows, :], qkv[3 + head])
            masked = jnp.where(usable, scores * 0.125, -1e30)
            raised = jnp.exp(masked - jnp.max(masked, axis=-1, keepdims=True))
            prob = raised / jnp.sum(raised, axis=-1, keepdims=True)
            probs[head, rows, :] = prob
            ctx[blk, :, head * HEAD_DIM : (head + 1) * HEAD_DIM] = mm(
                prob.astype(BF16), qkv[6 + head]
            ).astype(BF16)
            return carry

        lax.fori_loop(0, 2, rows_of, 0)
        yield
        lax.fori_loop(2, BLK, rows_of, 0)
        yield

    def run(generator, events):
        at = 0
        for _ in generator:
            for event in events.get(at, ()):
                event()
            at += 1

    chunk[0].settle()
    run(head_forward(0), {1: (chunk[1].pass_on, chunk[4].begin)})
    chunk[1].settle()
    run(head_forward(1), {1: (chunk[2].pass_on, chunk[6].begin)})
    chunk[2].settle()
    gather_out = blk_gather(2, all_out)

    def out_there():
        gather_out.start()

    def out_passed():
        gather_out.wait_across()

    run(
        head_forward(2),
        {0: (out_there,), 1: (chunk[3].pass_on,), 3: (out_passed, chunk[4].pass_on)},
    )

    swap_ctx = swap(mid_swap, 0, lambda peer: ctx.at[peer], ctx_own)
    ctx_own[b] = ctx[b]
    gather_out.wait_sib()
    gather_out.wait_diag()
    arrive(swap_ctx)
    own = jnp.concatenate([ctx_own[blk] for blk in range(BLK)], axis=1)
    attn = jnp.concatenate([mm(own, all_out[blk]) for blk in range(BLK)], axis=1) + vec_sum[2:3, :]
    hat_one, scale_one = centred(hidden[...].astype(F32) + attn)
    gain_one = vec_sum[3:4, :]
    normed = hat_one * gain_one + vec_sum[4:5, :]
    normed_all[b] = normed.astype(BF16)
    gather_normed = blk_gather(3, normed_all)
    gather_normed.start()
    chunk[6].pass_on()
    chunk[3].settle()
    chunk[4].settle()
    reduce_one = blk_reduce(0)

    def up(blk):
        for half, index in enumerate(B_CHUNKS):
            lanes = slice(half * HEAD_COLS, (half + 1) * HEAD_COLS)
            middle = mm(normed_all[blk], whole[index]) + vec_sum[1:2, lanes]
            gate = 0.5 * (1.0 + lax.erf(middle * math.sqrt(0.5)))
            act[blk, :, lanes] = (middle * gate).astype(BF16)
            bell = jnp.exp(-0.5 * middle * middle) * (1.0 / math.sqrt(2.0 * math.pi))
            slope[blk, :, lanes] = gate + middle * bell

    def down(blk):
        return jnp.concatenate([mm(act[blk], whole[index]) for index in C_CHUNKS], axis=1)

    up(b)
    gather_normed.wait_sib()
    up(place.sib)
    chunk[5].settle()
    chunk[6].settle()
    gather_normed.wait_across()
    parts[0, place.sib] = down(place.sib).astype(BF16)
    reduce_one.sib_near.start()
    up(place.across)
    parts[0, place.across] = down(place.across).astype(BF16)
    gather_normed.wait_diag()
    up(place.diag)
    parts[0, place.diag] = down(place.diag).astype(BF16)
    reduce_one.sib_far.start()
    own_branch = down(b)
    reduce_one.send_cross()
    branch = reduce_one.total(own_branch) + vec_sum[5:6, :]

    hat_two, scale_two = centred(normed + branch)
    gain_two = vec_sum[6:7, :]
    cot_wide = cot[...].astype(F32)
    g_two = norm_back(cot_wide * gain_two, hat_two, scale_two)
    branch_all[b] = g_two.astype(BF16)
    gather_branch = blk_gather(4, branch_all)
    gather_branch.start()
    out[...] = (hat_two * gain_two + vec_sum[7:8, :]).astype(BF16)
    gvec[6:7, :] = column_sum(cot_wide * hat_two)
    gvec[7:8, :] = column_sum(cot_wide)
    gvec[5:6, :] = column_sum(branch_all[b].astype(F32))
    gvec[8:16, :] = jnp.zeros((8, width), F32)
    reduce_two = blk_reduce(1)

    def back(blk):
        slab = mm_t(branch_all[blk, :, :HEAD_COLS], whole[C_CHUNKS[0]])
        slab = slab + mm_t(branch_all[blk, :, HEAD_COLS:], whole[C_CHUNKS[1]])
        low = (slab * slope[blk]).astype(BF16)
        g_middle[blk] = low
        part = mm_t(low[:, :HEAD_COLS], whole[B_CHUNKS[0]])
        return part + mm_t(low[:, HEAD_COLS:], whole[B_CHUNKS[1]])

    own_normed = back(b)
    gather_branch.wait_sib()
    parts[1, place.sib] = back(place.sib).astype(BF16)
    reduce_two.sib_near.start()
    gather_branch.wait_across()
    parts[1, place.across] = back(place.across).astype(BF16)
    gather_branch.wait_diag()
    parts[1, place.diag] = back(place.diag).astype(BF16)
    reduce_two.sib_far.start()

    act_rows = act.reshape(tokens, act.shape[2])
    branch_rows = branch_all.reshape(tokens, width)
    normed_rows = normed_all.reshape(tokens, width)
    middle_rows = g_middle.reshape(tokens, act.shape[2])
    flat_grads = grads.reshape(CHUNKS, rows_whole, HEAD_COLS)

    def weight_grad(index, left, right):
        def step(at, carry):
            cols = pl.ds(pl.multiple_of(at * 256, 256), 256)
            flat_grads[index, cols, :] = tmm(left[:, cols], right()).astype(BF16)
            return carry

        lax.fori_loop(0, rows_whole // 256, step, 0)

    summed = [Sum(index) for index in range(CHUNKS)]
    weight_grad(5, act_rows, lambda: branch_rows[:, :HEAD_COLS])
    summed[5].begin()
    reduce_two.send_cross()
    weight_grad(6, act_rows, lambda: branch_rows[:, HEAD_COLS:])
    summed[6].begin()
    weight_grad(3, normed_rows, lambda: middle_rows[:, :HEAD_COLS])
    weight_grad(4, normed_rows, lambda: middle_rows[:, HEAD_COLS:])
    gvec[1:2, :] = column_sum(middle_rows[...].astype(F32))
    g_normed = g_two + reduce_two.total(own_normed)

    g_one = norm_back(g_normed * gain_one, hat_one, scale_one)
    g_attn = g_one.astype(BF16)
    for blk in range(BLK):
        g_attn_own[blk] = g_attn[:, blk * third : (blk + 1) * third]
    wide = mm_t(g_attn_own[0], all_out[0])
    for blk in range(1, BLK):
        wide = wide + mm_t(g_attn_own[blk], all_out[blk])
    for blk in range(BLK):
        g_ctx_own[blk] = wide[:, blk * third : (blk + 1) * third].astype(BF16)
    swap_back = swap(mid_swap, 1, lambda peer: g_ctx_own.at[peer], g_ctx)
    g_ctx[b] = g_ctx_own[b]
    gvec[3:4, :] = column_sum(g_normed * hat_one)
    gvec[4:5, :] = column_sum(g_normed)
    gvec[2:3, :] = column_sum(g_attn.astype(F32))
    summed[5].pass_on()
    summed[3].begin()
    arrive(swap_back)
    swap_attn = swap(mid_swap, 2, lambda peer: g_attn_own.at[peer], g_attn_cols)
    g_attn_cols[b] = g_attn_own[b]
    spread_ctx = swap(mid_swap, 3, lambda peer: ctx, ctx_all)
    ctx_all[b] = ctx[...]

    g_ctx_rows = g_ctx.reshape(tokens, third)
    ctx_rows = ctx.reshape(tokens, third)

    def head_backward(head):
        lanes = slice(head * HEAD_DIM, (head + 1) * HEAD_DIM)
        go_heads[...] = g_ctx_rows[:, lanes]

        def query_rows(blk, carry):
            rows = block_rows(blk)
            go = go_heads[rows, :]
            delta = jnp.sum(
                go.astype(F32) * ctx_rows[rows, lanes].astype(F32), axis=-1, keepdims=True
            )
            prob = probs[head, rows, :]
            p_low[rows, :] = prob.astype(BF16)
            ds = (prob * (mm_t(go, qkv[6 + head]) - delta)).astype(BF16)
            g_scores[rows, :] = ds
            turned = 0.125 * mm(ds, feats[...])
            a1, a2 = turned[:, :SPAN], turned[:, SPAN:]
            cos_part = feats[rows, :SPAN].astype(F32)
            sin_part = feats[rows, SPAN:].astype(F32)
            qrel[rows, :SPAN] = (a1 * cos_part + a2 * sin_part).astype(BF16)
            qrel[rows, SPAN:] = (a1 * sin_part - a2 * cos_part).astype(BF16)
            gq = 0.125 * mm(ds, qkv[3 + head]) + mm(qrel[rows, :], relq[head])
            g_heads[0, rows, :] = gq.astype(BF16)
            return carry

        lax.fori_loop(0, 2, query_rows, 0)
        yield
        lax.fori_loop(2, BLK, query_rows, 0)
        yield

        def key_rows(blk, carry):
            rows = block_rows(blk)
            ds = g_scores[:, rows]
            turned = 0.125 * tmm(ds, feats[...])
            b1, b2 = turned[:, :SPAN], turned[:, SPAN:]
            cos_part = feats[rows, :SPAN].astype(F32)
            sin_part = feats[rows, SPAN:].astype(F32)
            krel[rows, :SPAN] = (b1 * cos_part + b2 * sin_part).astype(BF16)
            krel[rows, SPAN:] = (b2 * cos_part - b1 * sin_part).astype(BF16)
            gk = 0.125 * tmm(ds, qkv[head]) + mm(krel[rows, :], relk[head])
            g_heads[1, rows, :] = gk.astype(BF16)
            g_heads[2, rows, :] = tmm(p_low[:, rows], go_heads[...]).astype(BF16)
            return carry

        lax.fori_loop(0, 2, key_rows, 0)
        yield
        lax.fori_loop(2, BLK, key_rows, 0)
        yield
        g_qkv[head] = jnp.concatenate([g_heads[part] for part in range(3)], axis=1)
        gvec[0:1, head * third : (head + 1) * third] = column_sum(g_qkv[head].astype(F32))

        def chunk_rows(at, carry):
            cols = pl.ds(pl.multiple_of(at * 256, 256), 256)
            flat_grads[head, cols, :] = jnp.concatenate(
                [
                    tmm(hid[:, cols], g_qkv[head]),
                    tmm(qrel[:, cols], qkv[head]),
                    tmm(krel[:, cols], qkv[3 + head]),
                    tmm(
                        ctx_flat(at), g_attn_cols_rows[:, lanes]
                    ),
                ],
                axis=1,
            ).astype(BF16)
            return carry

        for at in range(rows_whole // 256):
            chunk_rows(at, 0)
        yield

    g_attn_cols_rows = g_attn_cols.reshape(tokens, third)

    def ctx_flat(at):
        pieces, start_col = [], at * 256
        while start_col < (at + 1) * 256:
            owner = start_col // third
            stop = min((owner + 1) * third, (at + 1) * 256)
            pieces.append(
                ctx_all.reshape(BLK, tokens, third)[
                    owner, :, start_col - owner * third : stop - owner * third
                ]
            )
            start_col = stop
        return jnp.concatenate(pieces, axis=1)

    def cross_there():
        arrive(swap_attn)
        arrive(spread_ctx)

    finals = []

    def settle(index):
        def done():
            finals.extend(summed[index].settle())

        return done

    gvec[0:1, 3 * third :] = jnp.zeros((1, width - 3 * third), F32)
    run(
        head_backward(0),
        {
            1: (summed[6].pass_on, summed[4].begin),
            3: (cross_there,),
            4: (summed[3].pass_on, settle(5), summed[0].begin),
        },
    )
    run(
        head_backward(1),
        {
            2: (summed[4].pass_on, settle(6)),
            4: (summed[1].begin,),
        },
    )
    run(
        head_backward(2),
        {
            1: (summed[0].pass_on, settle(3)),
            4: (summed[2].begin,),
        },
    )
    gvec_all[place.hi] = gvec[...].astype(BF16)
    vec_back = Spread(gvec_all, VEC, rs_x, rs_z)
    vec_back.begin()
    reduce_hid = blk_reduce(2)

    def part_hid(blk):
        total = mm_t(g_qkv[0, block_rows(blk), :], whole[0, :, :third])
        for head in range(1, HEADS):
            total = total + mm_t(g_qkv[head, block_rows(blk), :], whole[head, :, :third])
        return total

    parts[2, place.diag] = part_hid(place.diag).astype(BF16)
    reduce_hid.sib_far.start()
    parts[2, place.across] = part_hid(place.across).astype(BF16)
    reduce_hid.send_cross()
    parts[2, place.sib] = part_hid(place.sib).astype(BF16)
    reduce_hid.sib_near.start()
    own_hid = part_hid(b) + g_one
    settle(4)()
    summed[1].pass_on()
    vec_back.pass_on()
    vec_back.settle()
    total = gvec_all[0].astype(F32)
    for shard in range(1, GROUP):
        total = total + gvec_all[shard].astype(F32)
    gvec_page[b] = total
    gather_vec = blk_gather(5, gvec_page)
    gather_vec.start()
    grad_hid[...] = reduce_hid.total(own_hid).astype(BF16)
    gather_vec.wait_across()
    settle(0)()
    summed[2].pass_on()
    settle(1)()
    gather_vec.wait_sib()
    gather_vec.wait_diag()
    vec_out[...] = gvec_page[...]
    settle(2)()
    arrive(finals)
    for copy in sends:
        copy.wait_send()
    for reduce in (reduce_one, reduce_two, reduce_hid):
        reduce.finish()
    for gather in (gather_box, gather_hid, gather_out, gather_normed, gather_branch, gather_vec):
        gather.finish()


def on_device(
    hidden,
    boxes,
    lengths,
    w_qkv,
    b_qkv,
    w_relq,
    w_relk,
    w_out,
    b_out,
    ln1_gain,
    ln1_bias,
    w_up,
    b_up,
    w_down,
    b_down,
    ln2_gain,
    ln2_bias,
    cotangent,
):
    page_count = lax.axis_size("pages")
    spread = page_count // GROUP
    b = lax.axis_index("blk")
    hi = lax.axis_index("pages") // spread
    _, tok, width = hidden.shape
    third = 3 * HEAD_DIM
    groups = [[h * spread + low for low in range(spread)] for h in range(GROUP)]

    def grow(rows):
        if spread == 1:
            return rows
        rows = lax.all_gather(rows, "blk", axis=0, tiled=True)
        rows = lax.all_gather(rows, "pages", axis=0, tiled=True, axis_index_groups=groups)
        count = rows.shape[0] // BLK
        return lax.dynamic_slice_in_dim(rows, b * count, count, 0)

    def shrink(rows):
        if spread == 1:
            return rows
        rows = lax.all_gather(rows, "blk", axis=0, tiled=True)
        rows = lax.psum_scatter(
            rows, "pages", scatter_dimension=0, tiled=True, axis_index_groups=groups
        )
        count = rows.shape[0] // BLK
        return lax.dynamic_slice_in_dim(rows, b * count, count, 0)

    w_qkv, w_relq, w_relk, w_out, w_up, w_down = map(
        grow, (w_qkv, w_relq, w_relk, w_out, w_up, w_down)
    )
    b_qkv, b_up, b_out, ln1_gain, ln1_bias, b_down, ln2_gain, ln2_bias = map(
        grow, (b_qkv, b_up, b_out, ln1_gain, ln1_bias, b_down, ln2_gain, ln2_bias)
    )
    rows = w_qkv.shape[0]
    shard = BLK * rows
    ff_part = w_up.shape[1] // (GROUP * BLK)

    here = (lax.iota(jnp.int32, GROUP * BLK) == hi * BLK + b).astype(BF16)
    spot = here[:, None]
    own_bias = (spot * b_qkv[None, :]).reshape(3, BLK, HEADS, HEAD_DIM).transpose(1, 2, 0, 3)
    own_bias = own_bias.reshape(BLK, 3 * third)
    own_bias = jnp.pad(own_bias, ((0, 0), (0, width - 3 * third)))
    up_spot = (spot * b_up[None, :]).reshape(GROUP, BLK, ff_part).transpose(1, 0, 2)
    up_spot = up_spot.reshape(BLK, GROUP * ff_part)
    plain = jnp.stack([b_out, ln1_gain, ln1_bias, b_down, ln2_gain, ln2_bias])
    plain = (spot[None] * plain[:, None, :]).reshape(6, width)
    vec = jnp.concatenate(
        [
            own_bias[:, None, :],
            up_spot[:, None, :],
            jnp.broadcast_to(plain[None], (BLK, 6, width)),
            jnp.zeros((BLK, 8, width), BF16),
        ],
        axis=1,
    )
    box = jnp.pad(boxes[0].T, ((0, 6), (0, 0)))

    tokens = BLK * tok
    sem = pltpu.SemaphoreType.DMA

    def held(*shape, kind=BF16):
        return pltpu.VMEM(shape, kind)

    outs = [
        ((tok, width), BF16),
        ((tok, width), BF16),
        ((5, BLK, rows, HEAD_COLS), BF16),
        ((shard, width), F32),
        ((BLK, 16, width), F32),
    ]
    scratch = dict(
        weights=held(CHUNKS, GROUP, shard, HEAD_COLS),
        grads=held(CHUNKS, GROUP, shard, HEAD_COLS),
        pair=held(CHUNKS, GRID_Z, shard, HEAD_COLS),
        line=held(CHUNKS, GRID_Z - 1, shard, HEAD_COLS),
        cut=held(5, BLK, rows, HEAD_COLS),
        pack_a=held(BLK, rows, 3 * HEAD_COLS),
        pack_b=held(BLK, rows, GROUP * ff_part),
        land_a=held(BLK, rows, 3 * HEAD_COLS),
        land_b=held(BLK, rows, GROUP * ff_part),
        land_vec=held(BLK, 16, width),
        all_vec=held(GROUP, 16, width),
        all_hid=held(BLK, tok, width),
        all_box=held(BLK, 8, tok, kind=jnp.int32),
        all_out=held(BLK, GROUP * shard, third),
        vec_sum=held(16, width, kind=F32),
        table=held(512, width),
        feats=held(tokens, width),
        qkv=held(9, tokens, HEAD_DIM),
        relq=held(3, width, HEAD_DIM),
        relk=held(3, width, HEAD_DIM),
        qrel=held(tokens, width),
        krel=held(tokens, width),
        probs=held(3, tokens, tokens, kind=F32),
        ctx=held(BLK, tok, third),
        ctx_own=held(BLK, tok, third),
        ctx_all=held(BLK, BLK, tok, third),
        normed_all=held(BLK, tok, width),
        act=held(BLK, tok, GROUP * ff_part),
        slope=held(BLK, tok, GROUP * ff_part, kind=F32),
        branch_all=held(BLK, tok, width),
        g_middle=held(BLK, tok, GROUP * ff_part),
        parts=held(3, BLK, tok, width),
        near=held(3, 2, tok, width),
        far=held(3, tok, width),
        g_attn_own=held(BLK, tok, third),
        g_attn_cols=held(BLK, tok, third),
        g_ctx_own=held(BLK, tok, third),
        g_ctx=held(BLK, tok, third),
        go_heads=held(tokens, HEAD_DIM),
        g_scores=held(tokens, tokens),
        p_low=held(tokens, tokens),
        g_heads=held(3, tokens, HEAD_DIM),
        g_qkv=held(3, tokens, third),
        gvec=held(16, width, kind=F32),
        gvec_all=held(GROUP, 16, width),
        gvec_page=held(BLK, 16, width, kind=F32),
        ag_x=sem((2, CHUNKS + 1, 4)),
        ag_z=sem((2, CHUNKS + 1, 3)),
        rs_x=sem((2, CHUNKS + 1, 4)),
        rs_z=sem((2, CHUNKS + 1, 3)),
        in_swap=sem((2, 3, 3)),
        gather_sem=sem((2, 6, 3)),
        reduce_sem=sem((2, 3, 3)),
        mid_swap=sem((2, 4, 3)),
        out_swap=sem((2, 5, 3)),
    )
    out, grad_hid, sums, sum_c, vec_out = vmem_call(
        functools.partial(layer_kernel, spread),
        outs,
        list(scratch.values()),
        "layer",
        collective=1,
        smem=(0,),
    )(
        lengths,
        w_qkv,
        w_relq,
        w_relk,
        w_out,
        w_up,
        w_down,
        hidden[0],
        cotangent[0],
        box,
        vec,
    )

    heads = sums[:HEADS].reshape(HEADS, BLK, rows, 6, HEAD_DIM)

    def columns(part):
        return heads[:, :, :, part].transpose(2, 1, 0, 3).reshape(rows, BLK * third).astype(F32)

    grad_qkv = heads[:, :, :, :3].transpose(2, 3, 1, 0, 4).reshape(rows, 3 * BLK * third)
    grad_qkv = grad_qkv.astype(F32)
    grad_relq, grad_relk, grad_w_out = columns(3), columns(4), columns(5)
    grad_up = sums[HEADS:].reshape(2, BLK, rows, GROUP // 2, ff_part).transpose(2, 0, 3, 1, 4)
    grad_up = grad_up.reshape(rows, GROUP * BLK * ff_part).astype(F32)

    place = lax.axis_index("pages") * BLK + b
    if spread > 1:
        vec_out = lax.psum(vec_out, "pages", axis_index_groups=groups)
    summed = jnp.sum(vec_out[:, 2:8], axis=0)
    bias_all = vec_out[:, 0, : 3 * third].reshape(BLK, HEADS, 3, HEAD_DIM).transpose(2, 0, 1, 3)
    up_all = vec_out[:, 1].reshape(BLK, GROUP, ff_part).transpose(1, 0, 2)
    count = page_count * BLK
    whole = jnp.concatenate(
        [bias_all.reshape(count, -1), up_all.reshape(count, -1)]
        + [summed[row].reshape(count, -1) for row in range(6)],
        axis=1,
    )
    vectors = lax.dynamic_slice_in_dim(whole, place, 1, 0)[0]
    sizes = [3 * BLK * third // count, GROUP * BLK * ff_part // count] + [width // count] * 6
    cuts = [sum(sizes[:at]) for at in range(len(sizes) + 1)]
    g_bias, g_up, g_out, g_gain1, g_shift1, g_down, g_gain2, g_shift2 = [
        vectors[cuts[at] : cuts[at + 1]] for at in range(8)
    ]
    return (
        out[None],
        grad_hid[None],
        shrink(grad_qkv),
        g_bias,
        shrink(grad_relq),
        shrink(grad_relk),
        shrink(grad_w_out),
        g_out,
        g_gain1,
        g_shift1,
        shrink(grad_up),
        g_up,
        shrink(sum_c),
        g_down,
        g_gain2,
        g_shift2,
    )


def solution(mesh):
    rows = P(("pages", "blk"), None)
    vector = P(("pages", "blk"))
    tokens = P("pages", "blk", None)
    return jax.shard_map(
        on_device,
        mesh=mesh,
        in_specs=(
            tokens,
            tokens,
            P("pages"),
            rows,
            vector,
            rows,
            rows,
            rows,
            vector,
            vector,
            vector,
            rows,
            vector,
            rows,
            vector,
            vector,
            vector,
            tokens,
        ),
        out_specs=(
            tokens,
            tokens,
            rows,
            vector,
            rows,
            rows,
            rows,
            vector,
            vector,
            vector,
            rows,
            vector,
            rows,
            vector,
            vector,
            vector,
        ),
        check_vma=False,
    )
```

```python
import functools
import math

import jax
import jax.numpy as jnp
from jax import lax
from jax.experimental import pallas as pl
from jax.experimental.pallas import tpu as pltpu
from jax.sharding import PartitionSpec as P

HEAD_DIM = 64
FREQ = 192
GRID_Z = 4
GRID_X = 2
GROUP = GRID_Z * GRID_X
BLK = 4
MESH = pl.DeviceIdType.MESH
F32 = jnp.float32
BF16 = jnp.bfloat16
VMEM_BYTES = 56 << 20


def mm(left, right):
    return jnp.dot(left, right, preferred_element_type=F32)


def mm_t(left, right):
    return lax.dot_general(left, right, (((1,), (1,)), ((), ())), preferred_element_type=F32)


def tmm(left, right):
    return lax.dot_general(left, right, (((0,), (0,)), ((), ())), preferred_element_type=F32)


class Place:
    def __init__(self, spread):
        pages = lax.axis_index("pages")
        self.spread = spread
        self.hi = pages // spread
        self.lo = pages % spread
        self.z = self.hi // GRID_X
        self.x = self.hi % GRID_X
        self.b = lax.axis_index("blk")
        self.pages = pages
        self.sib = self.b + 1 - 2 * (self.b % 2)
        self.across = (self.b + 2) % BLK
        self.diag = (self.sib + 2) % BLK

    def at(self, z, x):
        return ((z * GRID_X + x) * self.spread + self.lo, self.b)

    def in_page(self, b):
        return (self.pages, b)

    def blk_peers(self):
        return (self.sib, self.across, self.diag)

    def z_at(self, step):
        return (self.z + step) % GRID_Z


def copy_to(src, dst, send, recv, device):
    return pltpu.make_async_remote_copy(
        src_ref=src, dst_ref=dst, send_sem=send, recv_sem=recv, device_id=device, device_id_type=MESH
    )


def remote(src, dst, send, recv, device):
    return copy_to(src, dst, send, recv, device)


class Hop:
    def __init__(self, here, make):
        self.here, self.make = here, make

    def start(self):
        @pl.when(self.here)
        def _():
            self.make().start()

    def wait_send(self):
        @pl.when(self.here)
        def _():
            self.make().wait_send()


def greet(devices):
    barrier = pltpu.get_barrier_semaphore()
    for device in devices:
        pl.semaphore_signal(barrier, inc=1, device_id=device, device_id_type=MESH)
    return lambda: pl.semaphore_wait(barrier, len(devices))


class BlkGather:
    def __init__(self, place, dst, send, recv):
        self.place, self.dst = place, dst
        b, across = place.b, place.across
        self.to_sib = remote(dst.at[b], dst.at[b], send.at[0], recv.at[0], place.in_page(place.sib))
        self.to_across = remote(dst.at[b], dst.at[b], send.at[1], recv.at[1], place.in_page(across))
        self.forward = remote(
            dst.at[across], dst.at[across], send.at[2], recv.at[2], place.in_page(place.sib)
        )

    def start(self):
        self.to_across.start()
        self.to_sib.start()

    def wait_sib(self):
        self.to_sib.wait_recv()

    def wait_across(self):
        self.to_across.wait_recv()
        self.forward.start()

    def wait_diag(self):
        self.forward.wait_recv()

    def finish(self):
        self.to_sib.wait_send()
        self.to_across.wait_send()
        self.forward.wait_send()


class BlkReduce:
    def __init__(self, place, parts, near, far, send, recv):
        self.place, self.parts, self.near, self.far = place, parts, near, far
        sib, across = place.sib, place.across
        self.sib_far = remote(
            parts.at[place.diag], near.at[1], send.at[0], recv.at[0], place.in_page(sib)
        )
        self.sib_near = remote(parts.at[sib], near.at[0], send.at[1], recv.at[1], place.in_page(sib))
        self.cross = remote(near.at[1], far, send.at[2], recv.at[2], place.in_page(across))

    def send_cross(self):
        self.sib_far.wait_recv()
        both = self.parts[self.place.across].astype(F32) + self.near[1].astype(F32)
        self.near[1] = both.astype(BF16)
        self.cross.start()

    def total(self, own):
        self.sib_near.wait_recv()
        partial = own + self.near[0].astype(F32)
        self.cross.wait_recv()
        return partial + self.far[...].astype(F32)

    def finish(self):
        self.sib_far.wait_send()
        self.sib_near.wait_send()
        self.cross.wait_send()


def vmem_call(kernel, outs, scratch, name, collective=None, smem=()):
    def run(*operands):
        params = dict(vmem_limit_bytes=VMEM_BYTES)
        if collective is not None:
            params.update(collective_id=collective, has_side_effects=True)
        return pl.pallas_call(
            kernel,
            name=name,
            out_shape=[jax.ShapeDtypeStruct(shape, kind) for shape, kind in outs],
            in_specs=[
                pl.BlockSpec(memory_space=pltpu.SMEM if i in smem else pltpu.VMEM)
                for i in range(len(operands))
            ],
            out_specs=[pl.BlockSpec(memory_space=pltpu.VMEM) for _ in outs],
            scratch_shapes=scratch,
            compiler_params=pltpu.CompilerParams(**params),
        )(*operands)

    return run


HEADS = 3
HEAD_COLS = 6 * HEAD_DIM
A_CHUNKS, B_CHUNKS, C_CHUNKS = (0, 1, 2), (3, 4), (5, 6)
CHUNKS = 7
VEC = 7
SPAN = 2 * FREQ


def centred(values):
    mean = jnp.mean(values, axis=-1, keepdims=True)
    centre = values - mean
    scale = lax.rsqrt(jnp.mean(centre * centre, axis=-1, keepdims=True) + 1e-12)
    return centre * scale, scale


def norm_back(grad_hat, hat, scale):
    first = jnp.mean(grad_hat, axis=-1, keepdims=True)
    second = jnp.mean(grad_hat * hat, axis=-1, keepdims=True)
    return scale * (grad_hat - first - hat * second)


def column_sum(values):
    return jnp.sum(values, axis=0, keepdims=True)


def block_rows(blk):
    return pl.ds(pl.multiple_of(blk * 128, 128), 128)


def layer_kernel(
    spread,
    lengths,
    w_qkv,
    w_relq,
    w_relk,
    w_out,
    w_up,
    w_down,
    hidden,
    cot,
    box,
    vec,
    out,
    grad_hid,
    sums,
    sum_c,
    vec_own,
    weights,
    grads,
    pair,
    line,
    cut,
    pack_a,
    pack_b,
    pack_vec,
    land_a,
    land_b,
    land_vec,
    all_vec,
    all_hid,
    all_box,
    all_out,
    vec_sum,
    table,
    feats,
    qkv,
    relq,
    relk,
    qrel,
    krel,
    probs,
    ctx,
    ctx_own,
    ctx_all,
    normed_all,
    act,
    slope,
    branch_all,
    g_middle,
    parts,
    near,
    far,
    g_attn_own,
    g_attn_cols,
    g_ctx_own,
    g_ctx,
    go_heads,
    g_scores,
    p_low,
    g_turned,
    g_qkv,
    gvec,
    gvec_all,
    gvec_page,
    ag_x,
    ag_z,
    rs_x,
    rs_z,
    in_swap,
    gather_sem,
    reduce_sem,
    mid_swap,
    out_swap,
):
    place = Place(spread)
    b = place.b
    peers = place.blk_peers()
    order = (b, place.sib, place.across, place.diag)
    partner = place.at(place.z, 1 - place.x)
    width = hidden.shape[1]
    tokens = BLK * hidden.shape[0]
    third = HEADS * HEAD_DIM
    ff_part = w_up.shape[1] // (GROUP * BLK)
    sends = []


    lower = place.z < 2
    outer = (place.z == 0) | (place.z == GRID_Z - 1)
    targets = (
        jnp.where(lower, 3, 0),
        jnp.where(lower, 2, 1),
        jnp.where(lower, 1 - place.z, 5 - place.z),
        place.z,
    )

    def start(copy):
        copy.start()
        sends.append(copy)
        return copy

    class Spread:
        def __init__(self, whole, index, sem_x, sem_z):
            self.whole, self.index, self.sem_x, self.sem_z = whole, index, sem_x, sem_z

        def _shard(self, z, x):
            return self.whole.at[z * GRID_X + x]

        def _along(self, z, slot, to):
            ref = self._shard(z, place.x)
            return copy_to(
                ref,
                ref,
                self.sem_z.at[0, self.index, slot],
                self.sem_z.at[1, self.index, z],
                place.at(to, place.x),
            )

        def _over(self, z, x):
            ref = self._shard(z, x)
            return copy_to(
                ref, ref, self.sem_x.at[0, self.index, z], self.sem_x.at[1, self.index, z], partner
            )

        def begin(self):
            z = place.z
            for slot, (here, to) in enumerate(((z < GRID_Z - 1, z + 1), (z > 0, z - 1))):
                start(Hop(here, functools.partial(self._along, z, slot, to)))

        def cross(self):
            self._over(place.z, place.x).start()

        def pass_on(self, distance):
            z = place.z
            for sign in (1, -1):
                source, to = z - sign * distance, z + sign
                inside = (source >= 0) & (source < GRID_Z)
                more = inside & (to >= 0) & (to < GRID_Z)

                @pl.when(inside)
                def _(source=source, to=to):
                    self._along(source, GRID_X, z).wait_recv()

                start(Hop(more, functools.partial(self._along, source, GRID_X + source, to)))

                @pl.when(inside)
                def _(source=source):
                    self._over(source, place.x).start()

        def settle(self):
            for z in range(GRID_Z):
                self._over(z, 1 - place.x).wait_recv()

        def finish(self):
            for z in range(GRID_Z):
                self._over(z, place.x).wait_send()

    class Sum:
        def __init__(self, index):
            self.index = index
            self.grad = grads.at[index]

        def _over(self, slot):
            return copy_to(
                self.grad.at[targets[slot] * GRID_X + 1 - place.x],
                pair.at[self.index, slot],
                rs_x.at[0, self.index, slot],
                rs_x.at[1, self.index, slot],
                partner,
            )

        def _along(self, slot, land, z):
            return copy_to(
                pair.at[self.index, slot],
                line.at[self.index, land],
                rs_z.at[0, self.index, slot],
                rs_z.at[1, self.index, land],
                place.at(z, place.x),
            )

        def begin(self):
            for slot in range(GRID_Z):
                self._over(slot).start()

        def pass_on(self):
            for slot in range(GRID_Z - 1):
                self._over(slot).wait_recv()
                mine = self.grad[targets[slot] * GRID_X + place.x].astype(F32)
                pair[self.index, slot] = (mine + pair[self.index, slot].astype(F32)).astype(BF16)

                def send(slot=slot):
                    self._along(slot, slot, targets[2]).start()

                if slot == 2:
                    send()
                else:
                    pl.when(outer)(send)

        def combine(self):
            @pl.when(jnp.logical_not(outer))
            def _():
                for slot in range(2):
                    self._along(slot, slot, place.z).wait_recv()
                    both = pair[self.index, slot].astype(F32) + line[self.index, slot].astype(F32)
                    pair[self.index, slot] = both.astype(BF16)
                    self._along(slot, 3, targets[slot]).start()

        def finish(self):
            for slot in range(GRID_Z):
                self._over(slot).wait_send()
            for slot in range(GRID_Z - 1):
                self._along(slot, slot, targets[2]).wait_send()

        def settle(self):
            index = self.index
            self._over(3).wait_recv()
            value = self.grad[place.hi].astype(F32) + pair[index, 3].astype(F32)
            for land in (2, 3):
                self._along(2, land, targets[2]).wait_recv()
                value = value + line[index, land].astype(F32)
            if index in C_CHUNKS:
                at = (index - C_CHUNKS[0]) * HEAD_COLS
                sum_c[:, at : at + HEAD_COLS] = value
                return []
            rows = value.shape[0] // BLK
            for blk in range(BLK):
                cut[index, blk] = value[blk * rows : (blk + 1) * rows, :].astype(BF16)
            sums[index, b] = cut[index, b]
            return [
                start(
                    remote(
                        cut.at[index, peer],
                        sums.at[index, b],
                        out_swap.at[0, index, slot],
                        out_swap.at[1, index, slot],
                        place.in_page(peer),
                    )
                )
                for slot, peer in enumerate(peers)
            ]

    def swap(sem, which, source_of, target):
        return [
            start(
                remote(
                    source_of(peer),
                    target.at[b],
                    sem.at[0, which, slot],
                    sem.at[1, which, slot],
                    place.in_page(peer),
                )
            )
            for slot, peer in enumerate(peers)
        ]

    def arrive(copies):
        for copy in copies:
            copy.wait_recv()

    def blk_gather(which, dst):
        return BlkGather(place, dst, gather_sem.at[0, which], gather_sem.at[1, which])

    def blk_reduce(which):
        return BlkReduce(
            place,
            parts.at[which],
            near.at[which],
            far.at[which],
            reduce_sem.at[0, which],
            reduce_sem.at[1, which],
        )

    all_met = greet(
        [place.in_page(peer) for peer in peers]
        + [partner]
        + [place.at(place.z_at(step), place.x) for step in range(1, GRID_Z)]
    )

    for half, index in enumerate(C_CHUNKS):
        weights[index, place.hi] = w_down[:, half * HEAD_COLS : (half + 1) * HEAD_COLS]
    for blk in range(BLK):
        for head in range(HEADS):
            at = blk * third + head * HEAD_DIM
            lanes = slice(at, at + HEAD_DIM)
            columns = [
                w_qkv[:, part * width + at : part * width + at + HEAD_DIM] for part in range(3)
            ]
            columns = columns + [w_relq[:, lanes], w_relk[:, lanes], w_out[:, lanes]]
            pack_a[blk, :, head * HEAD_COLS : (head + 1) * HEAD_COLS] = jnp.concatenate(
                columns, axis=1
            )
    chunk = [Spread(weights.at[index], index, ag_x, ag_z) for index in range(CHUNKS)]
    chunk.append(Spread(all_vec, VEC, ag_x, ag_z))
    all_met()
    swap_a = swap(in_swap, 0, lambda peer: pack_a.at[peer], land_a)
    chunk[5].begin()
    chunk[5].cross()
    bias_part, plain_part = w_qkv.shape[1] // (GROUP * BLK), width // (GROUP * BLK)
    spot = place.hi * BLK + b

    def home(at):
        wide = at + spot * bias_part
        part = (wide >= width).astype(jnp.int32) + (wide >= 2 * width).astype(jnp.int32)
        rest = wide - part * width
        taker = sum((rest >= third * i).astype(jnp.int32) for i in range(1, BLK))
        rest = rest - third * taker
        head = sum((rest >= HEAD_DIM * i).astype(jnp.int32) for i in range(1, HEADS))
        bias_column = head * third + part * HEAD_DIM + (rest - HEAD_DIM * head)
        plain = at - (bias_part + ff_part)
        kind = sum((plain >= plain_part * i).astype(jnp.int32) for i in range(1, 6))
        plain_column = spot * plain_part + (plain - plain_part * kind)
        up_column = place.hi * ff_part + (at - bias_part)
        is_bias, is_up = at < bias_part, at < bias_part + ff_part
        row = jnp.where(is_bias, 0, jnp.where(is_up, 1, 2 + kind))
        column = jnp.where(is_bias, bias_column, jnp.where(is_up, up_column, plain_column))
        return row, column, jnp.where(is_bias, taker, jnp.where(is_up, b, -1))

    held = vec.shape[1]
    _, column, _ = home(lax.broadcasted_iota(jnp.int32, (held, 1), 0))
    spots = lax.broadcasted_iota(jnp.int32, (held, width), 1) == column
    spots = jnp.where(spots, 1.0, 0.0).astype(BF16)
    row, _, taker = home(lax.broadcasted_iota(jnp.int32, (1, held), 1))
    row_here = lax.broadcasted_iota(jnp.int32, (16, held), 0) == row
    for blk in range(BLK):
        taken = row_here & ((taker == blk) | (taker < 0))
        values = jnp.where(taken, jnp.broadcast_to(vec[...].astype(F32), (16, held)), 0.0)
        pack_vec[blk] = mm(values.astype(BF16), spots).astype(BF16)
    swap_vec = swap(in_swap, 1, lambda peer: pack_vec.at[peer], land_vec)

    for blk in range(BLK):
        pack_b[blk] = jnp.concatenate(
            [
                w_up[:, (page * BLK + blk) * ff_part : (page * BLK + blk + 1) * ff_part]
                for page in range(GROUP)
            ],
            axis=1,
        )
    swap_b = swap(in_swap, 2, lambda peer: pack_b.at[peer], land_b)
    all_hid[b] = hidden[...]
    all_box[b, 0:2, :] = box[...]
    gather_box = blk_gather(0, all_box)
    gather_hid = blk_gather(1, all_hid)
    gather_box.start()
    gather_hid.start()

    places = lax.broadcasted_iota(jnp.int32, (256, FREQ), 0).astype(F32)
    ladder = lax.broadcasted_iota(jnp.int32, (256, FREQ), 1).astype(F32)
    angles = places * jnp.exp(ladder * (-math.log(10000.0) / FREQ))
    cosines, sines, blank = jnp.cos(angles), jnp.sin(angles), jnp.zeros((256, FREQ), F32)
    table[0:256, :] = jnp.concatenate([cosines, blank, sines, blank], axis=1).astype(BF16)
    table[256:512, :] = jnp.concatenate([blank, cosines, blank, sines], axis=1).astype(BF16)

    land_a[b] = pack_a[b]
    arrive(swap_a)
    joined = jnp.concatenate([land_a[blk].astype(F32) for blk in range(BLK)], axis=0).astype(BF16)
    for head in range(HEADS):
        weights[head, place.hi] = joined[:, head * HEAD_COLS : (head + 1) * HEAD_COLS]
    land_vec[b] = pack_vec[b]
    arrive(swap_vec)
    all_vec[place.hi] = (
        land_vec[0].astype(F32)
        + land_vec[1].astype(F32)
        + land_vec[2].astype(F32)
        + land_vec[3].astype(F32)
    ).astype(BF16)
    chunk[VEC].begin()
    chunk[VEC].cross()
    chunk[5].pass_on(1)
    chunk[0].begin()
    chunk[0].cross()
    land_b[b] = pack_b[b]
    arrive(swap_b)
    joined = jnp.concatenate([land_b[blk].astype(F32) for blk in range(BLK)], axis=0).astype(BF16)
    for half, index in enumerate(B_CHUNKS):
        weights[index, place.hi] = joined[:, half * HEAD_COLS : (half + 1) * HEAD_COLS]
    gather_box.wait_across()
    gather_box.wait_sib()
    gather_box.wait_diag()
    slots = lax.broadcasted_iota(jnp.int32, (256, tokens // BLK), 0)
    for blk in range(BLK):
        hot = jnp.concatenate(
            [
                jnp.where(slots == all_box[blk][0:1, :], 1.0, 0.0),
                jnp.where(slots == all_box[blk][1:2, :], 1.0, 0.0),
            ],
            axis=0,
        ).astype(BF16)
        feats[blk * 128 : (blk + 1) * 128, :] = tmm(hot, table[...]).astype(BF16)
    chunk[5].pass_on(2)
    chunk[VEC].pass_on(1)
    chunk[0].pass_on(1)
    chunk[5].pass_on(3)
    chunk[VEC].pass_on(2)
    chunk[1].begin()
    chunk[1].cross()
    chunk[0].pass_on(2)
    chunk[VEC].pass_on(3)
    gather_hid.wait_across()
    chunk[1].pass_on(1)
    chunk[0].pass_on(3)
    chunk[2].begin()
    chunk[2].cross()
    gather_hid.wait_sib()
    gather_hid.wait_diag()
    chunk[VEC].settle()
    total = all_vec[0].astype(F32)
    for shard in range(1, GROUP):
        total = total + all_vec[shard].astype(F32)
    vec_sum[...] = total

    rows_whole = GROUP * weights.shape[2]
    whole = weights.reshape(CHUNKS, rows_whole, HEAD_COLS)
    hid = all_hid.reshape(tokens, width)
    usable = lax.broadcasted_iota(jnp.int32, (tokens, tokens), 1) < lengths[0]

    def head_forward(head):
        bias = vec_sum[0:1, head * 3 * HEAD_DIM : (head + 1) * 3 * HEAD_DIM]
        low = (mm(hid[...], whole[head, :, : 3 * HEAD_DIM]) + bias).astype(BF16)
        for part in range(3):
            qkv[3 * part + head] = low[:, part * HEAD_DIM : (part + 1) * HEAD_DIM]
        relq[head] = whole[head, :, 3 * HEAD_DIM : 4 * HEAD_DIM]
        relk[head] = whole[head, :, 4 * HEAD_DIM : 5 * HEAD_DIM]
        all_out[b, :, head * HEAD_DIM : (head + 1) * HEAD_DIM] = whole[
            head, :, 5 * HEAD_DIM : 6 * HEAD_DIM
        ]
        yield

        def turn(blk, carry):
            rows = pl.ds(pl.multiple_of(blk * 256, 256), 256)
            cos_part = feats[rows, :SPAN].astype(F32)
            sin_part = feats[rows, SPAN:].astype(F32)
            u = mm_t(qkv[head, rows, :], relq[head])
            u1, u2 = u[:, :SPAN], u[:, SPAN:]
            qrel[rows, :SPAN] = (u1 * cos_part + u2 * sin_part).astype(BF16)
            qrel[rows, SPAN:] = (u1 * sin_part - u2 * cos_part).astype(BF16)
            v = mm_t(qkv[3 + head, rows, :], relk[head])
            v1, v2 = v[:, :SPAN], v[:, SPAN:]
            krel[rows, :SPAN] = (v1 * cos_part - v2 * sin_part).astype(BF16)
            krel[rows, SPAN:] = (v1 * sin_part + v2 * cos_part).astype(BF16)
            return carry

        lax.fori_loop(0, tokens // 256, turn, 0)
        yield
        scores = mm_t(qrel[...], feats[...])
        scores = scores + mm_t(feats[...], krel[...])
        scores = scores + mm_t(qkv[head], qkv[3 + head])
        masked = jnp.where(usable, scores * 0.125, -1e30)
        raised = jnp.exp(masked - jnp.max(masked, axis=-1, keepdims=True))
        prob = raised / jnp.sum(raised, axis=-1, keepdims=True)
        probs[head] = prob
        found = mm(prob.astype(BF16), qkv[6 + head]).astype(BF16)
        for blk in range(BLK):
            ctx[blk, :, head * HEAD_DIM : (head + 1) * HEAD_DIM] = found[
                blk * 128 : (blk + 1) * 128, :
            ]
        yield

    def run(generator, events):
        at = 0
        for _ in generator:
            for event in events.get(at, ()):
                event()
            at += 1

    chunk[1].pass_on(2)
    chunk[0].settle()

    def later(call, *rest):
        return functools.partial(call, *rest)

    run(head_forward(0), {1: (later(chunk[2].pass_on, 1), later(chunk[1].pass_on, 3))})
    chunk[3].begin()
    chunk[3].cross()
    chunk[2].pass_on(2)
    chunk[1].settle()
    run(
        head_forward(1),
        {
            1: (later(chunk[3].pass_on, 1), later(chunk[2].pass_on, 3)),
            2: (chunk[4].begin, chunk[4].cross, later(chunk[3].pass_on, 2)),
        },
    )
    gather_out = blk_gather(2, all_out)
    chunk[2].settle()
    run(
        head_forward(2),
        {
            0: (gather_out.start, later(chunk[4].pass_on, 1)),
            1: (later(chunk[3].pass_on, 3), chunk[6].begin, chunk[6].cross),
            2: (later(chunk[4].pass_on, 2),),
        },
    )

    swap_ctx = swap(mid_swap, 0, lambda peer: ctx.at[peer], ctx_own)
    ctx_own[b] = ctx[b]
    gather_out.wait_across()
    gather_out.wait_sib()
    chunk[6].pass_on(1)
    chunk[4].pass_on(3)
    chunk[6].pass_on(2)
    gather_out.wait_diag()
    arrive(swap_ctx)
    own = jnp.concatenate([ctx_own[blk] for blk in range(BLK)], axis=1)
    attn = jnp.concatenate([mm(own, all_out[blk]) for blk in range(BLK)], axis=1) + vec_sum[2:3, :]
    hat_one, scale_one = centred(hidden[...].astype(F32) + attn)
    gain_one = vec_sum[3:4, :]
    normed = hat_one * gain_one + vec_sum[4:5, :]
    normed_all[b] = normed.astype(BF16)
    gather_normed = blk_gather(3, normed_all)
    gather_normed.start()
    chunk[6].pass_on(3)
    chunk[3].settle()
    chunk[4].settle()
    reduce_one = blk_reduce(0)

    def up(blk):
        for half, index in enumerate(B_CHUNKS):
            lanes = slice(half * HEAD_COLS, (half + 1) * HEAD_COLS)
            middle = mm(normed_all[blk], whole[index]) + vec_sum[1:2, lanes]
            gate = 0.5 * (1.0 + lax.erf(middle * math.sqrt(0.5)))
            act[blk, :, lanes] = (middle * gate).astype(BF16)
            bell = jnp.exp(-0.5 * middle * middle) * (1.0 / math.sqrt(2.0 * math.pi))
            slope[blk, :, lanes] = gate + middle * bell

    def down(blk):
        return jnp.concatenate([mm(act[blk], whole[index]) for index in C_CHUNKS], axis=1)

    up(b)
    gather_normed.wait_sib()
    up(place.sib)
    gather_normed.wait_across()
    up(place.across)
    gather_normed.wait_diag()
    up(place.diag)
    chunk[5].settle()
    chunk[6].settle()
    parts[0, place.diag] = down(place.diag).astype(BF16)
    reduce_one.sib_far.start()
    parts[0, place.across] = down(place.across).astype(BF16)
    parts[0, place.sib] = down(place.sib).astype(BF16)
    reduce_one.sib_near.start()
    own_branch = down(b)
    reduce_one.send_cross()
    branch = reduce_one.total(own_branch) + vec_sum[5:6, :]

    hat_two, scale_two = centred(normed + branch)
    gain_two = vec_sum[6:7, :]
    cot_wide = cot[...].astype(F32)
    g_two = norm_back(cot_wide * gain_two, hat_two, scale_two)
    branch_all[b] = g_two.astype(BF16)
    gather_branch = blk_gather(4, branch_all)
    gather_branch.start()
    out[...] = (hat_two * gain_two + vec_sum[7:8, :]).astype(BF16)
    gvec[6:7, :] = column_sum(cot_wide * hat_two)
    gvec[7:8, :] = column_sum(cot_wide)
    gvec[5:6, :] = column_sum(branch_all[b].astype(F32))
    gvec[8:16, :] = jnp.zeros((8, width), F32)
    reduce_two = blk_reduce(1)

    def back(blk):
        slab = mm_t(branch_all[blk, :, :HEAD_COLS], whole[C_CHUNKS[0]])
        slab = slab + mm_t(branch_all[blk, :, HEAD_COLS:], whole[C_CHUNKS[1]])
        low = (slab * slope[blk]).astype(BF16)
        g_middle[blk] = low
        part = mm_t(low[:, :HEAD_COLS], whole[B_CHUNKS[0]])
        return part + mm_t(low[:, HEAD_COLS:], whole[B_CHUNKS[1]])

    own_normed = back(b)
    gather_branch.wait_sib()
    parts[1, place.sib] = back(place.sib).astype(BF16)
    reduce_two.sib_near.start()
    gather_branch.wait_across()
    parts[1, place.across] = back(place.across).astype(BF16)
    gather_branch.wait_diag()
    parts[1, place.diag] = back(place.diag).astype(BF16)
    reduce_two.sib_far.start()

    act_rows = act.reshape(tokens, act.shape[2])
    branch_rows = branch_all.reshape(tokens, width)
    normed_rows = normed_all.reshape(tokens, width)
    middle_rows = g_middle.reshape(tokens, act.shape[2])
    flat_grads = grads.reshape(CHUNKS, rows_whole, HEAD_COLS)

    def weight_grad(indices, left, right):
        def step(at, carry):
            cols = pl.ds(pl.multiple_of(at * 256, 256), 256)
            both = tmm(left[:, cols], right[...]).astype(BF16)
            for half, index in enumerate(indices):
                flat_grads[index, cols, :] = both[:, half * HEAD_COLS : (half + 1) * HEAD_COLS]
            return carry

        lax.fori_loop(0, rows_whole // 256, step, 0)

    summed = [Sum(index) for index in range(CHUNKS)]
    weight_grad(C_CHUNKS, act_rows, branch_rows)
    summed[5].begin()
    summed[6].begin()
    reduce_two.send_cross()
    weight_grad(B_CHUNKS, normed_rows, middle_rows)
    summed[3].begin()
    summed[4].begin()
    gvec[1:2, :] = column_sum(middle_rows[...].astype(F32))
    g_normed = g_two + reduce_two.total(own_normed)

    g_one = norm_back(g_normed * gain_one, hat_one, scale_one)
    g_attn = g_one.astype(BF16)
    for blk in range(BLK):
        g_attn_own[blk] = g_attn[:, blk * third : (blk + 1) * third]
    wide = mm_t(g_attn_own[0], all_out[0])
    for blk in range(1, BLK):
        wide = wide + mm_t(g_attn_own[blk], all_out[blk])
    for blk in range(BLK):
        g_ctx_own[blk] = wide[:, blk * third : (blk + 1) * third].astype(BF16)
    swap_back = swap(mid_swap, 1, lambda peer: g_ctx_own.at[peer], g_ctx)
    g_ctx[b] = g_ctx_own[b]
    gvec[3:4, :] = column_sum(g_normed * hat_one)
    gvec[4:5, :] = column_sum(g_normed)
    gvec[2:3, :] = column_sum(g_attn.astype(F32))
    summed[5].pass_on()
    arrive(swap_back)
    swap_attn = swap(mid_swap, 2, lambda peer: g_attn_own.at[peer], g_attn_cols)
    g_attn_cols[b] = g_attn_own[b]
    ctx_all[b] = ctx[...]
    gather_ctx = blk_gather(6, ctx_all)
    gather_ctx.start()

    g_ctx_rows = g_ctx.reshape(tokens, third)
    ctx_rows = ctx.reshape(tokens, third)

    def head_backward(head):
        lanes = slice(head * HEAD_DIM, (head + 1) * HEAD_DIM)
        go_heads[...] = g_ctx_rows[:, lanes]
        go = go_heads[...]
        delta = jnp.sum(
            go.astype(F32) * ctx_rows[:, lanes].astype(F32), axis=-1, keepdims=True
        )
        prob = probs[head]
        p_low[...] = prob.astype(BF16)
        g_scores[...] = (prob * (mm_t(go, qkv[6 + head]) - delta)).astype(BF16)
        cos_part = feats[:, :SPAN].astype(F32)
        sin_part = feats[:, SPAN:].astype(F32)
        turned = 0.125 * mm(g_scores[...], feats[...])
        a1, a2 = turned[:, :SPAN], turned[:, SPAN:]
        g_turned[0, head, :, :SPAN] = (a1 * cos_part + a2 * sin_part).astype(BF16)
        g_turned[0, head, :, SPAN:] = (a1 * sin_part - a2 * cos_part).astype(BF16)
        gq = 0.125 * mm(g_scores[...], qkv[3 + head]) + mm(g_turned[0, head], relq[head])
        turned = 0.125 * tmm(g_scores[...], feats[...])
        b1, b2 = turned[:, :SPAN], turned[:, SPAN:]
        g_turned[1, head, :, :SPAN] = (b1 * cos_part + b2 * sin_part).astype(BF16)
        g_turned[1, head, :, SPAN:] = (b2 * cos_part - b1 * sin_part).astype(BF16)
        gk = 0.125 * tmm(g_scores[...], qkv[head]) + mm(g_turned[1, head], relk[head])
        g_value = tmm(p_low[...], go)
        g_qkv[head] = jnp.concatenate([gq, gk, g_value], axis=1).astype(BF16)
        gvec[0:1, head * third : (head + 1) * third] = column_sum(g_qkv[head].astype(F32))

    def head_grads(head):
        lanes = slice(head * HEAD_DIM, (head + 1) * HEAD_DIM)
        for at in range(rows_whole // 256):
            cols = slice(at * 256, (at + 1) * 256)
            flat_grads[head, cols, :] = jnp.concatenate(
                [
                    tmm(hid[:, cols], g_qkv[head]),
                    tmm(g_turned[0, head, :, cols], qkv[head]),
                    tmm(g_turned[1, head, :, cols], qkv[3 + head]),
                    tmm(ctx_flat(at), g_attn_cols_rows[:, lanes]),
                ],
                axis=1,
            ).astype(BF16)

    g_attn_cols_rows = g_attn_cols.reshape(tokens, third)

    def ctx_flat(at):
        pieces, start_col = [], at * 256
        while start_col < (at + 1) * 256:
            owner = start_col // third
            stop = min((owner + 1) * third, (at + 1) * 256)
            pieces.append(
                ctx_all.reshape(BLK, tokens, third)[
                    owner, :, start_col - owner * third : stop - owner * third
                ]
            )
            start_col = stop
        return jnp.concatenate(pieces, axis=1)

    finals = []

    def settle(index):
        finals.extend(summed[index].settle())

    gvec[0:1, 3 * third :] = jnp.zeros((1, width - 3 * third), F32)
    head_backward(0)
    summed[5].combine()
    head_backward(1)
    gather_ctx.wait_across()
    summed[6].pass_on()
    head_backward(2)
    gvec_all[place.hi] = gvec[...].astype(BF16)
    vec_back = Spread(gvec_all, VEC, rs_x, rs_z)
    vec_back.begin()
    vec_back.cross()
    arrive(swap_attn)
    gather_ctx.wait_sib()
    gather_ctx.wait_diag()
    head_grads(0)
    summed[0].begin()
    summed[6].combine()
    vec_back.pass_on(1)
    head_grads(1)
    summed[1].begin()
    vec_back.pass_on(2)
    summed[3].pass_on()
    head_grads(2)
    summed[2].begin()
    vec_back.pass_on(3)
    settle(5)
    reduce_hid = blk_reduce(2)

    def part_hid(blk):
        total = mm_t(g_qkv[0, block_rows(blk), :], whole[0, :, :third])
        for head in range(1, HEADS):
            total = total + mm_t(g_qkv[head, block_rows(blk), :], whole[head, :, :third])
        return total

    parts[2, place.diag] = part_hid(place.diag).astype(BF16)
    reduce_hid.sib_far.start()
    parts[2, place.across] = part_hid(place.across).astype(BF16)
    reduce_hid.send_cross()
    parts[2, place.sib] = part_hid(place.sib).astype(BF16)
    reduce_hid.sib_near.start()
    own_hid = part_hid(b) + g_one
    summed[3].combine()
    settle(6)
    summed[4].pass_on()
    grad_hid[...] = reduce_hid.total(own_hid).astype(BF16)
    settle(3)
    summed[4].combine()
    summed[0].pass_on()
    settle(4)
    vec_back.settle()
    total = gvec_all[0].astype(F32)
    for shard in range(1, GROUP):
        total = total + gvec_all[shard].astype(F32)
    gvec_page[b] = total
    gather_vec = blk_gather(5, gvec_page)
    gather_vec.start()
    summed[0].combine()
    summed[1].pass_on()
    gather_vec.wait_across()
    gather_vec.wait_sib()
    gather_vec.wait_diag()

    _, column, taker = home(lax.broadcasted_iota(jnp.int32, (1, held), 1))
    places = lax.broadcasted_iota(jnp.int32, (width, held), 0) == column
    places = jnp.where(places, 1.0, 0.0)
    plain = gvec_page[0] + gvec_page[1] + gvec_page[2] + gvec_page[3]
    plain_row = lax.broadcasted_iota(jnp.int32, (16, width), 0)
    plain = jnp.where(plain_row < 2, 0.0, plain)
    bias_all = jnp.concatenate([gvec_page[blk][0:1, :] for blk in range(BLK)], axis=0)
    stacked = jnp.concatenate([plain, bias_all, gvec_page[b][1:2, :], bias_all[0:3, :]], axis=0)
    picked = jnp.dot(stacked, places, preferred_element_type=F32, precision=lax.Precision.HIGHEST)
    own_bias = jnp.zeros((1, held), F32)
    for blk in range(BLK):
        own_bias = own_bias + jnp.where(taker == blk, picked[16 + blk : 17 + blk, :], 0.0)
    vec_own[...] = jnp.concatenate([own_bias, picked[20:21, :], picked[2:8, :]], axis=0)

    settle(0)
    summed[1].combine()
    summed[2].pass_on()
    settle(1)
    summed[2].combine()
    settle(2)
    arrive(finals)
    for part in chunk + summed + [vec_back]:
        part.finish()
    for copy in sends:
        copy.wait_send()
    for reduce in (reduce_one, reduce_two, reduce_hid):
        reduce.finish()
    for gather in (gather_box, gather_hid, gather_out, gather_normed, gather_branch, gather_ctx, gather_vec):
        gather.finish()


def finish_kernel(
    out_in,
    hid_in,
    sums,
    sum_c,
    vec,
    out,
    grad_hid,
    g_qkv,
    g_bias,
    g_relq,
    g_relk,
    g_out,
    g_out_bias,
    g_gain_one,
    g_shift_one,
    g_up,
    g_up_bias,
    g_down,
    g_down_bias,
    g_gain_two,
    g_shift_two,
):
    out[...] = out_in[...]
    grad_hid[...] = hid_in[...]
    g_down[...] = sum_c[...]
    width = sum_c.shape[1]
    pieces = [
        [sums[head, blk].astype(F32) for blk in range(BLK)] for head in range(HEADS)
    ]

    def gathered(part):
        lanes = slice(part * HEAD_DIM, (part + 1) * HEAD_DIM)
        return jnp.concatenate(
            [pieces[head][blk][:, lanes] for blk in range(BLK) for head in range(HEADS)], axis=1
        )

    for part in range(3):
        g_qkv[:, part * width : (part + 1) * width] = gathered(part)
    g_relq[...] = gathered(3)
    g_relk[...] = gathered(4)
    g_out[...] = gathered(5)
    per_chunk = GROUP // len(B_CHUNKS)
    part = HEAD_COLS // per_chunk
    for half, index in enumerate(B_CHUNKS):
        wide = [sums[index, blk].astype(F32) for blk in range(BLK)]
        columns = jnp.concatenate(
            [
                wide[blk][:, page * part : (page + 1) * part]
                for page in range(per_chunk)
                for blk in range(BLK)
            ],
            axis=1,
        )
        g_up[:, half * columns.shape[1] : (half + 1) * columns.shape[1]] = columns
    for row, target in enumerate(
        (g_bias, g_up_bias, g_out_bias, g_gain_one, g_shift_one, g_down_bias, g_gain_two, g_shift_two)
    ):
        first = 0 if row == 0 else g_bias.shape[1]
        if row > 1:
            first = first + g_up_bias.shape[1] + (row - 2) * target.shape[1]
        target[...] = vec[row : row + 1, first : first + target.shape[1]]


def on_device(
    hidden,
    boxes,
    lengths,
    w_qkv,
    b_qkv,
    w_relq,
    w_relk,
    w_out,
    b_out,
    ln1_gain,
    ln1_bias,
    w_up,
    b_up,
    w_down,
    b_down,
    ln2_gain,
    ln2_bias,
    cotangent,
):
    page_count = lax.axis_size("pages")
    spread = page_count // GROUP
    b = lax.axis_index("blk")
    hi = lax.axis_index("pages") // spread
    _, tok, width = hidden.shape
    third = 3 * HEAD_DIM
    groups = [[h * spread + low for low in range(spread)] for h in range(GROUP)]

    def grow(rows):
        if spread == 1:
            return rows
        rows = lax.all_gather(rows, "blk", axis=0, tiled=True)
        rows = lax.all_gather(rows, "pages", axis=0, tiled=True, axis_index_groups=groups)
        count = rows.shape[0] // BLK
        return lax.dynamic_slice_in_dim(rows, b * count, count, 0)

    def shrink(rows):
        if spread == 1:
            return rows
        rows = lax.all_gather(rows, "blk", axis=0, tiled=True)
        rows = lax.psum_scatter(
            rows, "pages", scatter_dimension=0, tiled=True, axis_index_groups=groups
        )
        count = rows.shape[0] // BLK
        return lax.dynamic_slice_in_dim(rows, b * count, count, 0)

    w_qkv, w_relq, w_relk, w_out, w_up, w_down = map(
        grow, (w_qkv, w_relq, w_relk, w_out, w_up, w_down)
    )
    b_qkv, b_up, b_out, ln1_gain, ln1_bias, b_down, ln2_gain, ln2_bias = map(
        grow, (b_qkv, b_up, b_out, ln1_gain, ln1_bias, b_down, ln2_gain, ln2_bias)
    )
    rows = w_qkv.shape[0]
    shard = BLK * rows
    ff_part = w_up.shape[1] // (GROUP * BLK)

    vec = jnp.concatenate([b_qkv, b_up, b_out, ln1_gain, ln1_bias, b_down, ln2_gain, ln2_bias])
    vec = jnp.pad(vec, (0, 384 - vec.shape[0]))[None]
    box = boxes[0].T
    tokens = BLK * tok
    sem = pltpu.SemaphoreType.DMA

    def held(*shape, kind=BF16):
        return pltpu.VMEM(shape, kind)

    outs = [
        ((tok, width), BF16),
        ((tok, width), BF16),
        ((5, BLK, rows, HEAD_COLS), BF16),
        ((shard, width), F32),
        ((8, 384), F32),
    ]
    scratch = dict(
        weights=held(CHUNKS, GROUP, shard, HEAD_COLS),
        grads=held(CHUNKS, GROUP, shard, HEAD_COLS),
        pair=held(CHUNKS, GRID_Z, shard, HEAD_COLS),
        line=held(CHUNKS, GRID_Z, shard, HEAD_COLS),
        cut=held(5, BLK, rows, HEAD_COLS),
        pack_a=held(BLK, rows, 3 * HEAD_COLS),
        pack_b=held(BLK, rows, GROUP * ff_part),
        pack_vec=held(BLK, 16, width),
        land_a=held(BLK, rows, 3 * HEAD_COLS),
        land_b=held(BLK, rows, GROUP * ff_part),
        land_vec=held(BLK, 16, width),
        all_vec=held(GROUP, 16, width),
        all_hid=held(BLK, tok, width),
        all_box=held(BLK, 8, tok, kind=jnp.int32),
        all_out=held(BLK, GROUP * shard, third),
        vec_sum=held(16, width, kind=F32),
        table=held(512, width),
        feats=held(tokens, width),
        qkv=held(9, tokens, HEAD_DIM),
        relq=held(3, width, HEAD_DIM),
        relk=held(3, width, HEAD_DIM),
        qrel=held(tokens, width),
        krel=held(tokens, width),
        probs=held(3, tokens, tokens, kind=F32),
        ctx=held(BLK, tok, third),
        ctx_own=held(BLK, tok, third),
        ctx_all=held(BLK, BLK, tok, third),
        normed_all=held(BLK, tok, width),
        act=held(BLK, tok, GROUP * ff_part),
        slope=held(BLK, tok, GROUP * ff_part, kind=F32),
        branch_all=held(BLK, tok, width),
        g_middle=held(BLK, tok, GROUP * ff_part),
        parts=held(3, BLK, tok, width),
        near=held(3, 2, tok, width),
        far=held(3, tok, width),
        g_attn_own=held(BLK, tok, third),
        g_attn_cols=held(BLK, tok, third),
        g_ctx_own=held(BLK, tok, third),
        g_ctx=held(BLK, tok, third),
        go_heads=held(tokens, HEAD_DIM),
        g_scores=held(tokens, tokens),
        p_low=held(tokens, tokens),
        g_turned=held(2, HEADS, tokens, width),
        g_qkv=held(3, tokens, third),
        gvec=held(16, width, kind=F32),
        gvec_all=held(GROUP, 16, width),
        gvec_page=held(BLK, 16, width, kind=F32),
        ag_x=sem((2, CHUNKS + 1, 4)),
        ag_z=sem((2, CHUNKS + 1, 6)),
        rs_x=sem((2, CHUNKS + 1, 4)),
        rs_z=sem((2, CHUNKS + 1, 6)),
        in_swap=sem((2, 3, 3)),
        gather_sem=sem((2, 7, 3)),
        reduce_sem=sem((2, 3, 3)),
        mid_swap=sem((2, 3, 3)),
        out_swap=sem((2, 5, 3)),
    )
    out, grad_hid, sums, sum_c, vec_own = vmem_call(
        functools.partial(layer_kernel, spread),
        outs,
        list(scratch.values()),
        "layer",
        collective=1,
        smem=(0,),
    )(
        lengths,
        w_qkv,
        w_relq,
        w_relk,
        w_out,
        w_up,
        w_down,
        hidden[0],
        cotangent[0],
        box,
        vec,
    )

    square = ((rows, BLK * third), F32)
    plain = ((1, rows), F32)
    results = vmem_call(
        finish_kernel,
        [
            ((tok, width), BF16),
            ((tok, width), BF16),
            ((rows, 3 * BLK * third), F32),
            ((1, 3 * rows), F32),
            square,
            square,
            square,
            plain,
            plain,
            plain,
            ((rows, GROUP * BLK * ff_part), F32),
            ((1, ff_part), F32),
            ((shard, width), F32),
            plain,
            plain,
            plain,
        ],
        [],
        "finish",
    )(out, grad_hid, sums, sum_c, vec_own)
    flat = [part[0] if part.shape[0] == 1 else part for part in results[2:]]
    return (results[0][None], results[1][None]) + tuple(shrink(part) for part in flat)


def solution(mesh):
    rows = P(("pages", "blk"), None)
    vector = P(("pages", "blk"))
    tokens = P("pages", "blk", None)
    return jax.shard_map(
        on_device,
        mesh=mesh,
        in_specs=(
            tokens,
            tokens,
            P("pages"),
            rows,
            vector,
            rows,
            rows,
            rows,
            vector,
            vector,
            vector,
            rows,
            vector,
            rows,
            vector,
            vector,
            vector,
            tokens,
        ),
        out_specs=(
            tokens,
            tokens,
            rows,
            vector,
            rows,
            rows,
            rows,
            vector,
            vector,
            vector,
            rows,
            vector,
            rows,
            vector,
            vector,
            vector,
        ),
        check_vma=False,
    )
```

```python
import functools
import math

import jax
import jax.numpy as jnp
from jax import lax
from jax.experimental import pallas as pl
from jax.experimental.pallas import tpu as pltpu
from jax.sharding import PartitionSpec as P

HEAD_DIM = 64
FREQ = 192
GRID_Z = 4
GRID_X = 2
GROUP = GRID_Z * GRID_X
BLK = 4
MESH = pl.DeviceIdType.MESH
F32 = jnp.float32
BF16 = jnp.bfloat16
VMEM_BYTES = 56 << 20


def mm(left, right):
    return jnp.dot(left, right, preferred_element_type=F32)


def mm_t(left, right):
    return lax.dot_general(left, right, (((1,), (1,)), ((), ())), preferred_element_type=F32)


def tmm(left, right):
    return lax.dot_general(left, right, (((0,), (0,)), ((), ())), preferred_element_type=F32)


class Place:
    def __init__(self, spread):
        pages = lax.axis_index("pages")
        self.spread = spread
        self.hi = pages // spread
        self.lo = pages % spread
        self.z = self.hi // GRID_X
        self.x = self.hi % GRID_X
        self.b = lax.axis_index("blk")
        self.pages = pages
        self.sib = self.b + 1 - 2 * (self.b % 2)
        self.across = (self.b + 2) % BLK
        self.diag = (self.sib + 2) % BLK

    def at(self, z, x):
        return ((z * GRID_X + x) * self.spread + self.lo, self.b)

    def in_page(self, b):
        return (self.pages, b)

    def blk_peers(self):
        return (self.sib, self.across, self.diag)

    def z_at(self, step):
        return (self.z + step) % GRID_Z


def copy_to(src, dst, send, recv, device):
    return pltpu.make_async_remote_copy(
        src_ref=src, dst_ref=dst, send_sem=send, recv_sem=recv, device_id=device, device_id_type=MESH
    )


def remote(src, dst, send, recv, device):
    return copy_to(src, dst, send, recv, device)


class Hop:
    def __init__(self, here, make):
        self.here, self.make = here, make

    def start(self):
        @pl.when(self.here)
        def _():
            self.make().start()

    def wait_send(self):
        @pl.when(self.here)
        def _():
            self.make().wait_send()


def greet(devices):
    barrier = pltpu.get_barrier_semaphore()
    for device in devices:
        pl.semaphore_signal(barrier, inc=1, device_id=device, device_id_type=MESH)
    return lambda: pl.semaphore_wait(barrier, len(devices))


class BlkGather:
    def __init__(self, place, dst, send, recv):
        self.place, self.dst = place, dst
        b, across = place.b, place.across
        self.to_sib = remote(dst.at[b], dst.at[b], send.at[0], recv.at[0], place.in_page(place.sib))
        self.to_across = remote(dst.at[b], dst.at[b], send.at[1], recv.at[1], place.in_page(across))
        self.forward = remote(
            dst.at[across], dst.at[across], send.at[2], recv.at[2], place.in_page(place.sib)
        )

    def start(self):
        self.to_across.start()
        self.to_sib.start()

    def wait_sib(self):
        self.to_sib.wait_recv()

    def wait_across(self):
        self.to_across.wait_recv()
        self.forward.start()

    def wait_diag(self):
        self.forward.wait_recv()

    def finish(self):
        self.to_sib.wait_send()
        self.to_across.wait_send()
        self.forward.wait_send()


class BlkReduce:
    def __init__(self, place, parts, near, far, send, recv):
        self.place, self.parts, self.near, self.far = place, parts, near, far
        sib, across = place.sib, place.across
        self.sib_far = remote(
            parts.at[place.diag], near.at[1], send.at[0], recv.at[0], place.in_page(sib)
        )
        self.sib_near = remote(parts.at[sib], near.at[0], send.at[1], recv.at[1], place.in_page(sib))
        self.cross = remote(near.at[1], far, send.at[2], recv.at[2], place.in_page(across))

    def send_cross(self):
        self.sib_far.wait_recv()
        both = self.parts[self.place.across].astype(F32) + self.near[1].astype(F32)
        self.near[1] = both.astype(BF16)
        self.cross.start()

    def total(self, own):
        self.sib_near.wait_recv()
        partial = own + self.near[0].astype(F32)
        self.cross.wait_recv()
        return partial + self.far[...].astype(F32)

    def finish(self):
        self.sib_far.wait_send()
        self.sib_near.wait_send()
        self.cross.wait_send()


def vmem_call(kernel, outs, scratch, name, collective=None, smem=()):
    def run(*operands):
        params = dict(vmem_limit_bytes=VMEM_BYTES)
        if collective is not None:
            params.update(collective_id=collective, has_side_effects=True)
        return pl.pallas_call(
            kernel,
            name=name,
            out_shape=[jax.ShapeDtypeStruct(shape, kind) for shape, kind in outs],
            in_specs=[
                pl.BlockSpec(memory_space=pltpu.SMEM if i in smem else pltpu.VMEM)
                for i in range(len(operands))
            ],
            out_specs=[pl.BlockSpec(memory_space=pltpu.VMEM) for _ in outs],
            scratch_shapes=scratch,
            compiler_params=pltpu.CompilerParams(**params),
        )(*operands)

    return run


HEADS = 3
HEAD_COLS = 6 * HEAD_DIM
A_CHUNKS, B_CHUNKS, C_CHUNKS = (0, 1, 2), (3, 4), (5, 6)
CHUNKS = 7
VEC = 7
SPAN = 2 * FREQ


def centred(values):
    mean = jnp.mean(values, axis=-1, keepdims=True)
    centre = values - mean
    scale = lax.rsqrt(jnp.mean(centre * centre, axis=-1, keepdims=True) + 1e-12)
    return centre * scale, scale


def norm_back(grad_hat, hat, scale):
    first = jnp.mean(grad_hat, axis=-1, keepdims=True)
    second = jnp.mean(grad_hat * hat, axis=-1, keepdims=True)
    return scale * (grad_hat - first - hat * second)


def column_sum(values):
    return jnp.sum(values, axis=0, keepdims=True)


def block_rows(blk):
    return pl.ds(pl.multiple_of(blk * 128, 128), 128)


def layer_kernel(
    spread,
    lengths,
    w_qkv,
    w_relq,
    w_relk,
    w_out,
    w_up,
    w_down,
    hidden,
    cot,
    box,
    vec,
    out,
    grad_hid,
    sums,
    sum_c,
    vec_own,
    weights,
    grads,
    pair,
    line,
    beside,
    cut,
    pack_a,
    pack_b,
    pack_vec,
    land_a,
    land_b,
    land_vec,
    all_vec,
    all_hid,
    all_box,
    all_out_a,
    all_out_b,
    vec_sum,
    table,
    feats,
    qkv,
    relq,
    relk,
    qrel,
    krel,
    probs,
    ctx,
    ctx_own,
    ctx_all,
    normed_all,
    act,
    slope,
    branch_all,
    g_middle,
    parts,
    near,
    far,
    g_attn_own,
    g_attn_cols,
    g_ctx_own,
    g_ctx,
    go_heads,
    g_scores,
    p_low,
    g_turned,
    g_qkv,
    gvec,
    gvec_all,
    gvec_page,
    ag_x,
    ag_z,
    rs_x,
    rs_z,
    in_swap,
    gather_sem,
    reduce_sem,
    mid_swap,
    out_swap,
):
    place = Place(spread)
    b = place.b
    peers = place.blk_peers()
    order = (b, place.sib, place.across, place.diag)
    partner = place.at(place.z, 1 - place.x)
    width = hidden.shape[1]
    tokens = BLK * hidden.shape[0]
    third = HEADS * HEAD_DIM
    ff_part = w_up.shape[1] // (GROUP * BLK)
    sends = []


    lower = place.z < 2
    outer = (place.z == 0) | (place.z == GRID_Z - 1)
    targets = (
        jnp.where(lower, 3, 0),
        jnp.where(lower, 2, 1),
        jnp.where(lower, 1 - place.z, 5 - place.z),
        place.z,
    )
    mate = targets[2]

    def start(copy):
        copy.start()
        sends.append(copy)
        return copy

    class Spread:
        def __init__(self, whole, index, sem_x, sem_z):
            self.whole, self.index, self.sem_x, self.sem_z = whole, index, sem_x, sem_z
            self.halved = index != VEC

        def _shard(self, z, x, part=None):
            if part is None or not self.halved:
                return self.whole.at[z * GRID_X + x]
            rows = self.whole.shape[1] // 2
            return self.whole.at[z * GRID_X + x, part * rows : (part + 1) * rows]

        def _along(self, z, slot, to):
            ref = self._shard(z, place.x)
            return copy_to(
                ref,
                ref,
                self.sem_z.at[0, self.index, slot],
                self.sem_z.at[1, self.index, z],
                place.at(to, place.x),
            )

        def _over(self, z, x, part=None):
            ref = self._shard(z, x, part)
            return copy_to(
                ref, ref, self.sem_x.at[0, self.index, z], self.sem_x.at[1, self.index, z], partner
            )

        def _beside(self):
            ref = self._shard(place.z, 1 - place.x, 1)
            return copy_to(
                ref,
                ref,
                self.sem_z.at[0, self.index, GRID_X + place.z],
                self.sem_z.at[1, self.index, GRID_Z],
                place.at(mate, place.x),
            )

        def relay(self):
            self._over(place.z, 1 - place.x).wait_recv()
            if self.halved:
                self._beside().start()

        def begin(self):
            z = place.z
            for slot, (here, to) in enumerate(((z < GRID_Z - 1, z + 1), (z > 0, z - 1))):
                start(Hop(here, functools.partial(self._along, z, slot, to)))

        def cross(self):
            self._over(place.z, place.x).start()

        def pass_on(self, distance):
            z = place.z
            for sign in (1, -1):
                source, to = z - sign * distance, z + sign
                inside = (source >= 0) & (source < GRID_Z)
                more = inside & (to >= 0) & (to < GRID_Z)

                @pl.when(inside)
                def _(source=source, to=to):
                    self._along(source, GRID_X, z).wait_recv()

                start(Hop(more, functools.partial(self._along, source, GRID_X + source, to)))

                if distance > 1:

                    @pl.when(inside)
                    def _(source=source):
                        self._over(source, place.x).start()

                else:

                    @pl.when(inside & (source == mate))
                    def _(source=source):
                        self._over(source, place.x, 0).start()

                    @pl.when(inside & (source != mate))
                    def _(source=source):
                        self._over(source, place.x).start()

        def settle(self):
            for slot in range(2):
                self._over(targets[slot], 1 - place.x).wait_recv()
            self._over(mate, 1 - place.x, 0).wait_recv()
            if self.halved:
                self._beside().wait_recv()

        def finish(self):
            for slot in (0, 1, 3):
                self._over(targets[slot], place.x).wait_send()
            self._over(mate, place.x, 0).wait_send()
            if self.halved:
                self._beside().wait_send()

    half_rows = grads.shape[2] // 2

    class Sum:
        def __init__(self, index):
            self.index = index
            self.grad = grads.at[index]

        def _over(self, slot):
            shard = targets[min(slot, 3)] * GRID_X + 1 - place.x
            src, dst = self.grad.at[shard], pair.at[self.index, min(slot, 3)]
            if slot >= 9:
                rows = slice(half_rows, None) if slot == 4 else slice(0, half_rows)
                src, dst = src.at[rows], dst.at[rows]
            return copy_to(
                src, dst, rs_x.at[0, self.index, slot], rs_x.at[1, self.index, slot], partner
            )

        def _beside(self):
            return copy_to(
                self.grad.at[mate * GRID_X + 1 - place.x, half_rows:],
                beside.at[self.index],
                rs_z.at[0, self.index, 3],
                rs_z.at[1, self.index, 4],
                place.at(mate, place.x),
            )

        def _along(self, slot, land, z):
            return copy_to(
                pair.at[self.index, slot],
                line.at[self.index, land],
                rs_z.at[0, self.index, slot],
                rs_z.at[1, self.index, land],
                place.at(z, place.x),
            )

        def begin(self):
            for slot in range(GRID_Z):
                self._over(slot).start()

        def relay(self):
            return


        def pass_on(self):
            for slot in range(GRID_Z - 1):
                self._over(slot).wait_recv()
                shard = targets[slot] * GRID_X + place.x
                if slot < 9:
                    both = self.grad[shard].astype(F32) + pair[self.index, slot].astype(F32)
                    pair[self.index, slot] = both.astype(BF16)
                else:
                    mine = self.grad[shard, :half_rows].astype(F32)
                    both = mine + pair[self.index, slot, :half_rows].astype(F32)
                    pair[self.index, slot, :half_rows] = both.astype(BF16)
                    pair[self.index, slot, half_rows:] = self.grad[shard, half_rows:]

                def send(slot=slot):
                    self._along(slot, slot, targets[2]).start()

                if slot == 2:
                    send()
                else:
                    pl.when(outer)(send)

        def combine(self):
            @pl.when(jnp.logical_not(outer))
            def _():
                for slot in range(2):
                    self._along(slot, slot, place.z).wait_recv()
                    both = pair[self.index, slot].astype(F32) + line[self.index, slot].astype(F32)
                    pair[self.index, slot] = both.astype(BF16)
                    self._along(slot, 3, targets[slot]).start()

        def finish(self):
            for slot in range(GRID_Z):
                self._over(slot).wait_send()
            for slot in range(GRID_Z - 1):
                self._along(slot, slot, targets[2]).wait_send()

        def settle(self):
            index = self.index
            self._over(3).wait_recv()
            value = self.grad[place.hi].astype(F32) + pair[index, 3].astype(F32)
            for land in (2, 3):
                self._along(2, land, targets[2]).wait_recv()
                value = value + line[index, land].astype(F32)
            if index in C_CHUNKS:
                at = (index - C_CHUNKS[0]) * HEAD_COLS
                sum_c[:, at : at + HEAD_COLS] = value
                return []
            rows = value.shape[0] // BLK
            for blk in range(BLK):
                cut[index, blk] = value[blk * rows : (blk + 1) * rows, :].astype(BF16)
            sums[index, b] = cut[index, b]
            return [
                start(
                    remote(
                        cut.at[index, peer],
                        sums.at[index, b],
                        out_swap.at[0, index, slot],
                        out_swap.at[1, index, slot],
                        place.in_page(peer),
                    )
                )
                for slot, peer in enumerate(peers)
            ]

    def swap(sem, which, source_of, target):
        return [
            start(
                remote(
                    source_of(peer),
                    target.at[b],
                    sem.at[0, which, slot],
                    sem.at[1, which, slot],
                    place.in_page(peer),
                )
            )
            for slot, peer in enumerate(peers)
        ]

    def arrive(copies):
        for copy in copies:
            copy.wait_recv()

    def blk_gather(which, dst):
        return BlkGather(place, dst, gather_sem.at[0, which], gather_sem.at[1, which])

    def blk_reduce(which):
        return BlkReduce(
            place,
            parts.at[which],
            near.at[which],
            far.at[which],
            reduce_sem.at[0, which],
            reduce_sem.at[1, which],
        )

    all_met = greet(
        [place.in_page(peer) for peer in peers]
        + [partner]
        + [place.at(place.z_at(step), place.x) for step in range(1, GRID_Z)]
    )

    for half, index in enumerate(C_CHUNKS):
        weights[index, place.hi] = w_down[:, half * HEAD_COLS : (half + 1) * HEAD_COLS]
    for blk in range(BLK):
        for head in range(HEADS):
            at = blk * third + head * HEAD_DIM
            lanes = slice(at, at + HEAD_DIM)
            columns = [
                w_qkv[:, part * width + at : part * width + at + HEAD_DIM] for part in range(3)
            ]
            columns = columns + [w_relq[:, lanes], w_relk[:, lanes], w_out[:, lanes]]
            pack_a[blk, :, head * HEAD_COLS : (head + 1) * HEAD_COLS] = jnp.concatenate(
                columns, axis=1
            )
    chunk = [Spread(weights.at[index], index, ag_x, ag_z) for index in range(CHUNKS)]
    chunk.append(Spread(all_vec, VEC, ag_x, ag_z))
    all_met()
    swap_a = swap(in_swap, 0, lambda peer: pack_a.at[peer], land_a)
    chunk[5].begin()
    chunk[5].cross()
    bias_part, plain_part = w_qkv.shape[1] // (GROUP * BLK), width // (GROUP * BLK)
    spot = place.hi * BLK + b

    def home(at):
        wide = at + spot * bias_part
        part = (wide >= width).astype(jnp.int32) + (wide >= 2 * width).astype(jnp.int32)
        rest = wide - part * width
        taker = sum((rest >= third * i).astype(jnp.int32) for i in range(1, BLK))
        rest = rest - third * taker
        head = sum((rest >= HEAD_DIM * i).astype(jnp.int32) for i in range(1, HEADS))
        bias_column = head * third + part * HEAD_DIM + (rest - HEAD_DIM * head)
        plain = at - (bias_part + ff_part)
        kind = sum((plain >= plain_part * i).astype(jnp.int32) for i in range(1, 6))
        plain_column = spot * plain_part + (plain - plain_part * kind)
        up_column = place.hi * ff_part + (at - bias_part)
        is_bias, is_up = at < bias_part, at < bias_part + ff_part
        row = jnp.where(is_bias, 0, jnp.where(is_up, 1, 2 + kind))
        column = jnp.where(is_bias, bias_column, jnp.where(is_up, up_column, plain_column))
        return row, column, jnp.where(is_bias, taker, jnp.where(is_up, b, -1))

    held = vec.shape[1]
    _, column, _ = home(lax.broadcasted_iota(jnp.int32, (held, 1), 0))
    spots = lax.broadcasted_iota(jnp.int32, (held, width), 1) == column
    spots = jnp.where(spots, 1.0, 0.0).astype(BF16)
    row, _, taker = home(lax.broadcasted_iota(jnp.int32, (1, held), 1))
    row_here = lax.broadcasted_iota(jnp.int32, (16, held), 0) == row
    for blk in range(BLK):
        taken = row_here & ((taker == blk) | (taker < 0))
        values = jnp.where(taken, jnp.broadcast_to(vec[...].astype(F32), (16, held)), 0.0)
        pack_vec[blk] = mm(values.astype(BF16), spots).astype(BF16)
    swap_vec = swap(in_swap, 1, lambda peer: pack_vec.at[peer], land_vec)

    for blk in range(BLK):
        pack_b[blk] = jnp.concatenate(
            [
                w_up[:, (page * BLK + blk) * ff_part : (page * BLK + blk + 1) * ff_part]
                for page in range(GROUP)
            ],
            axis=1,
        )
    swap_b = swap(in_swap, 2, lambda peer: pack_b.at[peer], land_b)
    all_hid[b] = hidden[...]
    all_box[b, 0:2, :] = box[...]
    gather_box = blk_gather(0, all_box)
    gather_hid = blk_gather(1, all_hid)
    gather_box.start()
    gather_hid.start()

    places = lax.broadcasted_iota(jnp.int32, (256, FREQ), 0).astype(F32)
    ladder = lax.broadcasted_iota(jnp.int32, (256, FREQ), 1).astype(F32)
    angles = places * jnp.exp(ladder * (-math.log(10000.0) / FREQ))
    cosines, sines, blank = jnp.cos(angles), jnp.sin(angles), jnp.zeros((256, FREQ), F32)
    table[0:256, :] = jnp.concatenate([cosines, blank, sines, blank], axis=1).astype(BF16)
    table[256:512, :] = jnp.concatenate([blank, cosines, blank, sines], axis=1).astype(BF16)

    land_a[b] = pack_a[b]
    arrive(swap_a)
    joined = jnp.concatenate([land_a[blk].astype(F32) for blk in range(BLK)], axis=0).astype(BF16)
    for head in range(HEADS):
        weights[head, place.hi] = joined[:, head * HEAD_COLS : (head + 1) * HEAD_COLS]
    chunk[0].begin()
    chunk[0].cross()
    land_vec[b] = pack_vec[b]
    arrive(swap_vec)
    all_vec[place.hi] = (
        land_vec[0].astype(F32)
        + land_vec[1].astype(F32)
        + land_vec[2].astype(F32)
        + land_vec[3].astype(F32)
    ).astype(BF16)
    chunk[VEC].begin()
    chunk[VEC].cross()
    chunk[5].pass_on(1)
    land_b[b] = pack_b[b]
    arrive(swap_b)
    joined = jnp.concatenate([land_b[blk].astype(F32) for blk in range(BLK)], axis=0).astype(BF16)
    for half, index in enumerate(B_CHUNKS):
        weights[index, place.hi] = joined[:, half * HEAD_COLS : (half + 1) * HEAD_COLS]
    chunk[5].relay()
    chunk[5].pass_on(2)
    chunk[0].pass_on(1)
    chunk[1].begin()
    chunk[1].cross()
    gather_box.wait_across()
    gather_hid.wait_across()
    chunk[VEC].pass_on(1)
    gather_box.wait_sib()
    gather_box.wait_diag()
    slots = lax.broadcasted_iota(jnp.int32, (256, tokens // BLK), 0)
    for blk in range(BLK):
        hot = jnp.concatenate(
            [
                jnp.where(slots == all_box[blk][0:1, :], 1.0, 0.0),
                jnp.where(slots == all_box[blk][1:2, :], 1.0, 0.0),
            ],
            axis=0,
        ).astype(BF16)
        feats[blk * 128 : (blk + 1) * 128, :] = tmm(hot, table[...]).astype(BF16)
    chunk[5].pass_on(3)
    chunk[0].relay()
    chunk[0].pass_on(2)
    chunk[VEC].relay()
    chunk[VEC].pass_on(2)
    chunk[1].pass_on(1)
    chunk[2].begin()
    chunk[2].cross()
    chunk[0].pass_on(3)
    chunk[VEC].pass_on(3)
    gather_hid.wait_sib()
    gather_hid.wait_diag()
    chunk[1].relay()
    chunk[1].pass_on(2)
    chunk[VEC].settle()
    total = all_vec[0].astype(F32)
    for shard in range(1, GROUP):
        total = total + all_vec[shard].astype(F32)
    vec_sum[...] = total

    rows_whole = GROUP * weights.shape[2]
    whole = weights.reshape(CHUNKS, rows_whole, HEAD_COLS)
    hid = all_hid.reshape(tokens, width)
    usable = lax.broadcasted_iota(jnp.int32, (tokens, tokens), 1) < lengths[0]

    gather_out = [blk_gather(2, all_out_a), blk_gather(7, all_out_b)]

    def head_forward(head):
        out_part = whole[head, :, 5 * HEAD_DIM : 6 * HEAD_DIM]
        if head == 2:
            all_out_b[b] = out_part
            gather_out[1].start()
        else:
            all_out_a[b, :, head * HEAD_DIM : (head + 1) * HEAD_DIM] = out_part
        if head == 1:
            gather_out[0].start()
        bias = vec_sum[0:1, head * 3 * HEAD_DIM : (head + 1) * 3 * HEAD_DIM]
        low = (mm(hid[...], whole[head, :, : 3 * HEAD_DIM]) + bias).astype(BF16)
        for part in range(3):
            qkv[3 * part + head] = low[:, part * HEAD_DIM : (part + 1) * HEAD_DIM]
        relq[head] = whole[head, :, 3 * HEAD_DIM : 4 * HEAD_DIM]
        relk[head] = whole[head, :, 4 * HEAD_DIM : 5 * HEAD_DIM]
        yield

        def turn(blk, carry):
            rows = pl.ds(pl.multiple_of(blk * 256, 256), 256)
            cos_part = feats[rows, :SPAN].astype(F32)
            sin_part = feats[rows, SPAN:].astype(F32)
            u = mm_t(qkv[head, rows, :], relq[head])
            u1, u2 = u[:, :SPAN], u[:, SPAN:]
            qrel[rows, :SPAN] = (u1 * cos_part + u2 * sin_part).astype(BF16)
            qrel[rows, SPAN:] = (u1 * sin_part - u2 * cos_part).astype(BF16)
            v = mm_t(qkv[3 + head, rows, :], relk[head])
            v1, v2 = v[:, :SPAN], v[:, SPAN:]
            krel[rows, :SPAN] = (v1 * cos_part - v2 * sin_part).astype(BF16)
            krel[rows, SPAN:] = (v1 * sin_part + v2 * cos_part).astype(BF16)
            return carry

        lax.fori_loop(0, tokens // 256, turn, 0)
        yield
        scores = mm_t(qrel[...], feats[...])
        scores = scores + mm_t(feats[...], krel[...])
        scores = scores + mm_t(qkv[head], qkv[3 + head])
        masked = jnp.where(usable, scores * 0.125, -1e30)
        raised = jnp.exp(masked - jnp.max(masked, axis=-1, keepdims=True))
        prob = raised / jnp.sum(raised, axis=-1, keepdims=True)
        probs[head] = prob
        found = mm(prob.astype(BF16), qkv[6 + head]).astype(BF16)
        for blk in range(BLK):
            ctx[blk, :, head * HEAD_DIM : (head + 1) * HEAD_DIM] = found[
                blk * 128 : (blk + 1) * 128, :
            ]
        yield

    def run(generator, events):
        at = 0
        for _ in generator:
            for event in events.get(at, ()):
                event()
            at += 1

    chunk[2].pass_on(1)
    chunk[3].begin()
    chunk[3].cross()
    chunk[0].settle()

    def later(call, *rest):
        return functools.partial(call, *rest)

    run(head_forward(0), {0: (later(chunk[1].pass_on, 3),)})
    chunk[2].relay()
    chunk[2].pass_on(2)
    chunk[1].settle()
    run(
        head_forward(1),
        {
            0: (later(chunk[3].pass_on, 1), chunk[4].begin, chunk[4].cross),
            1: (later(chunk[2].pass_on, 3),),
        },
    )
    chunk[3].relay()
    chunk[3].pass_on(2)
    chunk[4].pass_on(1)
    chunk[6].begin()
    chunk[6].cross()
    chunk[2].settle()
    run(
        head_forward(2),
        {
            0: (gather_out[0].wait_across,),
            1: (later(chunk[3].pass_on, 3),),
        },
    )

    swap_ctx = swap(mid_swap, 0, lambda peer: ctx.at[peer], ctx_own)
    ctx_own[b] = ctx[b]
    chunk[4].relay()
    chunk[4].pass_on(2)
    chunk[6].pass_on(1)
    gather_out[1].wait_across()
    for gather in gather_out:
        gather.wait_sib()
        gather.wait_diag()
    arrive(swap_ctx)
    own = jnp.concatenate([ctx_own[blk] for blk in range(BLK)], axis=1)
    attn = jnp.concatenate(
        [mm(own, part[blk]) for blk in range(BLK) for part in (all_out_a, all_out_b)], axis=1
    )
    attn = attn + vec_sum[2:3, :]
    hat_one, scale_one = centred(hidden[...].astype(F32) + attn)
    gain_one = vec_sum[3:4, :]
    normed = hat_one * gain_one + vec_sum[4:5, :]
    normed_all[b] = normed.astype(BF16)
    gather_normed = blk_gather(3, normed_all)
    gather_normed.start()
    chunk[4].pass_on(3)
    chunk[6].relay()
    chunk[6].pass_on(2)
    chunk[3].settle()
    chunk[4].settle()
    reduce_one = blk_reduce(0)

    def up(blk):
        for half, index in enumerate(B_CHUNKS):
            lanes = slice(half * HEAD_COLS, (half + 1) * HEAD_COLS)
            middle = mm(normed_all[blk], whole[index]) + vec_sum[1:2, lanes]
            gate = 0.5 * (1.0 + lax.erf(middle * math.sqrt(0.5)))
            act[blk, :, lanes] = (middle * gate).astype(BF16)
            bell = jnp.exp(-0.5 * middle * middle) * (1.0 / math.sqrt(2.0 * math.pi))
            slope[blk, :, lanes] = gate + middle * bell

    def down(blk):
        return jnp.concatenate([mm(act[blk], whole[index]) for index in C_CHUNKS], axis=1)

    up(b)
    chunk[6].pass_on(3)
    gather_normed.wait_sib()
    up(place.sib)
    gather_normed.wait_across()
    up(place.across)
    gather_normed.wait_diag()
    up(place.diag)
    chunk[5].settle()
    chunk[6].settle()
    parts[0, place.diag] = down(place.diag).astype(BF16)
    reduce_one.sib_far.start()
    parts[0, place.across] = down(place.across).astype(BF16)
    parts[0, place.sib] = down(place.sib).astype(BF16)
    reduce_one.sib_near.start()
    own_branch = down(b)
    reduce_one.send_cross()
    branch = reduce_one.total(own_branch) + vec_sum[5:6, :]

    hat_two, scale_two = centred(normed + branch)
    gain_two = vec_sum[6:7, :]
    cot_wide = cot[...].astype(F32)
    g_two = norm_back(cot_wide * gain_two, hat_two, scale_two)
    branch_all[b] = g_two.astype(BF16)
    gather_branch = blk_gather(4, branch_all)
    gather_branch.start()
    out[...] = (hat_two * gain_two + vec_sum[7:8, :]).astype(BF16)
    gvec[6:7, :] = column_sum(cot_wide * hat_two)
    gvec[7:8, :] = column_sum(cot_wide)
    gvec[5:6, :] = column_sum(branch_all[b].astype(F32))
    gvec[8:16, :] = jnp.zeros((8, width), F32)
    reduce_two = blk_reduce(1)

    def back(blk):
        slab = mm_t(branch_all[blk, :, :HEAD_COLS], whole[C_CHUNKS[0]])
        slab = slab + mm_t(branch_all[blk, :, HEAD_COLS:], whole[C_CHUNKS[1]])
        low = (slab * slope[blk]).astype(BF16)
        g_middle[blk] = low
        part = mm_t(low[:, :HEAD_COLS], whole[B_CHUNKS[0]])
        return part + mm_t(low[:, HEAD_COLS:], whole[B_CHUNKS[1]])

    own_normed = back(b)
    gather_branch.wait_sib()
    parts[1, place.sib] = back(place.sib).astype(BF16)
    reduce_two.sib_near.start()
    gather_branch.wait_across()
    parts[1, place.across] = back(place.across).astype(BF16)
    gather_branch.wait_diag()
    parts[1, place.diag] = back(place.diag).astype(BF16)
    reduce_two.sib_far.start()

    act_rows = act.reshape(tokens, act.shape[2])
    branch_rows = branch_all.reshape(tokens, width)
    normed_rows = normed_all.reshape(tokens, width)
    middle_rows = g_middle.reshape(tokens, act.shape[2])
    flat_grads = grads.reshape(CHUNKS, rows_whole, HEAD_COLS)

    def weight_grad(indices, left, right):
        def step(at, carry):
            cols = pl.ds(pl.multiple_of(at * 256, 256), 256)
            both = tmm(left[:, cols], right[...]).astype(BF16)
            for half, index in enumerate(indices):
                flat_grads[index, cols, :] = both[:, half * HEAD_COLS : (half + 1) * HEAD_COLS]
            return carry

        lax.fori_loop(0, rows_whole // 256, step, 0)

    summed = [Sum(index) for index in range(CHUNKS)]
    weight_grad(C_CHUNKS, act_rows, branch_rows)
    summed[5].begin()
    summed[6].begin()
    reduce_two.send_cross()
    weight_grad(B_CHUNKS, normed_rows, middle_rows)
    summed[3].begin()
    summed[4].begin()
    gvec[1:2, :] = column_sum(middle_rows[...].astype(F32))
    for index in (5, 6, 3, 4):
        summed[index].relay()
    g_normed = g_two + reduce_two.total(own_normed)

    g_one = norm_back(g_normed * gain_one, hat_one, scale_one)
    g_attn = g_one.astype(BF16)
    for blk in range(BLK):
        g_attn_own[blk] = g_attn[:, blk * third : (blk + 1) * third]
    wide = jnp.zeros(g_one.shape, F32)
    for blk in range(BLK):
        wide = wide + mm_t(g_attn_own[blk, :, : 2 * HEAD_DIM], all_out_a[blk])
        wide = wide + mm_t(g_attn_own[blk, :, 2 * HEAD_DIM :], all_out_b[blk])
    for blk in range(BLK):
        g_ctx_own[blk] = wide[:, blk * third : (blk + 1) * third].astype(BF16)
    swap_back = swap(mid_swap, 1, lambda peer: g_ctx_own.at[peer], g_ctx)
    g_ctx[b] = g_ctx_own[b]
    gvec[3:4, :] = column_sum(g_normed * hat_one)
    gvec[4:5, :] = column_sum(g_normed)
    gvec[2:3, :] = column_sum(g_attn.astype(F32))
    summed[5].pass_on()
    arrive(swap_back)
    swap_attn = swap(mid_swap, 2, lambda peer: g_attn_own.at[peer], g_attn_cols)
    g_attn_cols[b] = g_attn_own[b]
    ctx_all[b] = ctx[...]
    gather_ctx = blk_gather(6, ctx_all)
    gather_ctx.start()

    g_ctx_rows = g_ctx.reshape(tokens, third)
    ctx_rows = ctx.reshape(tokens, third)

    def head_backward(head):
        lanes = slice(head * HEAD_DIM, (head + 1) * HEAD_DIM)
        go_heads[...] = g_ctx_rows[:, lanes]
        go = go_heads[...]
        delta = jnp.sum(
            go.astype(F32) * ctx_rows[:, lanes].astype(F32), axis=-1, keepdims=True
        )
        prob = probs[head]
        p_low[...] = prob.astype(BF16)
        g_scores[...] = (prob * (mm_t(go, qkv[6 + head]) - delta)).astype(BF16)
        cos_part = feats[:, :SPAN].astype(F32)
        sin_part = feats[:, SPAN:].astype(F32)
        turned = 0.125 * mm(g_scores[...], feats[...])
        a1, a2 = turned[:, :SPAN], turned[:, SPAN:]
        g_turned[0, head, :, :SPAN] = (a1 * cos_part + a2 * sin_part).astype(BF16)
        g_turned[0, head, :, SPAN:] = (a1 * sin_part - a2 * cos_part).astype(BF16)
        gq = 0.125 * mm(g_scores[...], qkv[3 + head]) + mm(g_turned[0, head], relq[head])
        turned = 0.125 * tmm(g_scores[...], feats[...])
        b1, b2 = turned[:, :SPAN], turned[:, SPAN:]
        g_turned[1, head, :, :SPAN] = (b1 * cos_part + b2 * sin_part).astype(BF16)
        g_turned[1, head, :, SPAN:] = (b2 * cos_part - b1 * sin_part).astype(BF16)
        gk = 0.125 * tmm(g_scores[...], qkv[head]) + mm(g_turned[1, head], relk[head])
        g_value = tmm(p_low[...], go)
        g_qkv[head] = jnp.concatenate([gq, gk, g_value], axis=1).astype(BF16)
        gvec[0:1, head * third : (head + 1) * third] = column_sum(g_qkv[head].astype(F32))

    def head_grads(head):
        lanes = slice(head * HEAD_DIM, (head + 1) * HEAD_DIM)
        for at in range(rows_whole // 256):
            cols = slice(at * 256, (at + 1) * 256)
            flat_grads[head, cols, :] = jnp.concatenate(
                [
                    tmm(hid[:, cols], g_qkv[head]),
                    tmm(g_turned[0, head, :, cols], qkv[head]),
                    tmm(g_turned[1, head, :, cols], qkv[3 + head]),
                    tmm(ctx_flat(at), g_attn_cols_rows[:, lanes]),
                ],
                axis=1,
            ).astype(BF16)

    g_attn_cols_rows = g_attn_cols.reshape(tokens, third)

    def ctx_flat(at):
        pieces, start_col = [], at * 256
        while start_col < (at + 1) * 256:
            owner = start_col // third
            stop = min((owner + 1) * third, (at + 1) * 256)
            pieces.append(
                ctx_all.reshape(BLK, tokens, third)[
                    owner, :, start_col - owner * third : stop - owner * third
                ]
            )
            start_col = stop
        return jnp.concatenate(pieces, axis=1)

    finals = []

    def settle(index):
        finals.extend(summed[index].settle())

    gvec[0:1, 3 * third :] = jnp.zeros((1, width - 3 * third), F32)
    head_backward(0)
    head_backward(1)
    gather_ctx.wait_across()
    head_backward(2)
    gvec_all[place.hi] = gvec[...].astype(BF16)
    vec_back = Spread(gvec_all, VEC, rs_x, rs_z)
    vec_back.begin()
    vec_back.cross()
    arrive(swap_attn)
    gather_ctx.wait_sib()
    gather_ctx.wait_diag()
    head_grads(0)
    summed[0].begin()
    summed[6].pass_on()
    summed[5].combine()
    vec_back.pass_on(1)
    head_grads(1)
    summed[1].begin()
    summed[0].relay()
    vec_back.relay()
    vec_back.pass_on(2)
    head_grads(2)
    summed[2].begin()
    summed[1].relay()
    summed[3].pass_on()
    summed[6].combine()
    vec_back.pass_on(3)
    settle(5)
    summed[2].relay()
    reduce_hid = blk_reduce(2)

    def part_hid(blk):
        total = mm_t(g_qkv[0, block_rows(blk), :], whole[0, :, :third])
        for head in range(1, HEADS):
            total = total + mm_t(g_qkv[head, block_rows(blk), :], whole[head, :, :third])
        return total

    parts[2, place.diag] = part_hid(place.diag).astype(BF16)
    reduce_hid.sib_far.start()
    parts[2, place.across] = part_hid(place.across).astype(BF16)
    reduce_hid.send_cross()
    parts[2, place.sib] = part_hid(place.sib).astype(BF16)
    reduce_hid.sib_near.start()
    own_hid = part_hid(b) + g_one
    summed[3].combine()
    settle(6)
    summed[4].pass_on()
    grad_hid[...] = reduce_hid.total(own_hid).astype(BF16)
    settle(3)
    summed[4].combine()
    summed[0].pass_on()
    settle(4)
    vec_back.settle()
    total = gvec_all[0].astype(F32)
    for shard in range(1, GROUP):
        total = total + gvec_all[shard].astype(F32)
    gvec_page[b] = total
    gather_vec = blk_gather(5, gvec_page)
    gather_vec.start()
    summed[0].combine()
    summed[1].pass_on()
    gather_vec.wait_across()
    gather_vec.wait_sib()
    gather_vec.wait_diag()

    _, column, taker = home(lax.broadcasted_iota(jnp.int32, (1, held), 1))
    places = lax.broadcasted_iota(jnp.int32, (width, held), 0) == column
    places = jnp.where(places, 1.0, 0.0)
    plain = gvec_page[0] + gvec_page[1] + gvec_page[2] + gvec_page[3]
    plain_row = lax.broadcasted_iota(jnp.int32, (16, width), 0)
    plain = jnp.where(plain_row < 2, 0.0, plain)
    bias_all = jnp.concatenate([gvec_page[blk][0:1, :] for blk in range(BLK)], axis=0)
    stacked = jnp.concatenate([plain, bias_all, gvec_page[b][1:2, :], bias_all[0:3, :]], axis=0)
    picked = jnp.dot(stacked, places, preferred_element_type=F32, precision=lax.Precision.HIGHEST)
    own_bias = jnp.zeros((1, held), F32)
    for blk in range(BLK):
        own_bias = own_bias + jnp.where(taker == blk, picked[16 + blk : 17 + blk, :], 0.0)
    vec_own[...] = jnp.concatenate([own_bias, picked[20:21, :], picked[2:8, :]], axis=0)

    settle(0)
    summed[1].combine()
    summed[2].pass_on()
    settle(1)
    summed[2].combine()
    settle(2)
    arrive(finals)
    for part in chunk + summed + [vec_back]:
        part.finish()
    for copy in sends:
        copy.wait_send()
    for reduce in (reduce_one, reduce_two, reduce_hid):
        reduce.finish()
    for gather in (gather_box, gather_hid, *gather_out, gather_normed, gather_branch, gather_ctx, gather_vec):
        gather.finish()


def finish_kernel(
    out_in,
    hid_in,
    sums,
    sum_c,
    vec,
    out,
    grad_hid,
    g_qkv,
    g_bias,
    g_relq,
    g_relk,
    g_out,
    g_out_bias,
    g_gain_one,
    g_shift_one,
    g_up,
    g_up_bias,
    g_down,
    g_down_bias,
    g_gain_two,
    g_shift_two,
):
    out[...] = out_in[...]
    grad_hid[...] = hid_in[...]
    g_down[...] = sum_c[...]
    width = sum_c.shape[1]
    pieces = [
        [sums[head, blk].astype(F32) for blk in range(BLK)] for head in range(HEADS)
    ]

    def gathered(part):
        lanes = slice(part * HEAD_DIM, (part + 1) * HEAD_DIM)
        return jnp.concatenate(
            [pieces[head][blk][:, lanes] for blk in range(BLK) for head in range(HEADS)], axis=1
        )

    for part in range(3):
        g_qkv[:, part * width : (part + 1) * width] = gathered(part)
    g_relq[...] = gathered(3)
    g_relk[...] = gathered(4)
    g_out[...] = gathered(5)
    per_chunk = GROUP // len(B_CHUNKS)
    part = HEAD_COLS // per_chunk
    for half, index in enumerate(B_CHUNKS):
        wide = [sums[index, blk].astype(F32) for blk in range(BLK)]
        columns = jnp.concatenate(
            [
                wide[blk][:, page * part : (page + 1) * part]
                for page in range(per_chunk)
                for blk in range(BLK)
            ],
            axis=1,
        )
        g_up[:, half * columns.shape[1] : (half + 1) * columns.shape[1]] = columns
    for row, target in enumerate(
        (g_bias, g_up_bias, g_out_bias, g_gain_one, g_shift_one, g_down_bias, g_gain_two, g_shift_two)
    ):
        first = 0 if row == 0 else g_bias.shape[1]
        if row > 1:
            first = first + g_up_bias.shape[1] + (row - 2) * target.shape[1]
        target[...] = vec[row : row + 1, first : first + target.shape[1]]


def on_device(
    hidden,
    boxes,
    lengths,
    w_qkv,
    b_qkv,
    w_relq,
    w_relk,
    w_out,
    b_out,
    ln1_gain,
    ln1_bias,
    w_up,
    b_up,
    w_down,
    b_down,
    ln2_gain,
    ln2_bias,
    cotangent,
):
    page_count = lax.axis_size("pages")
    spread = page_count // GROUP
    b = lax.axis_index("blk")
    hi = lax.axis_index("pages") // spread
    _, tok, width = hidden.shape
    third = 3 * HEAD_DIM
    groups = [[h * spread + low for low in range(spread)] for h in range(GROUP)]

    def grow(rows):
        if spread == 1:
            return rows
        rows = lax.all_gather(rows, "blk", axis=0, tiled=True)
        rows = lax.all_gather(rows, "pages", axis=0, tiled=True, axis_index_groups=groups)
        count = rows.shape[0] // BLK
        return lax.dynamic_slice_in_dim(rows, b * count, count, 0)

    def shrink(rows):
        if spread == 1:
            return rows
        rows = lax.all_gather(rows, "blk", axis=0, tiled=True)
        rows = lax.psum_scatter(
            rows, "pages", scatter_dimension=0, tiled=True, axis_index_groups=groups
        )
        count = rows.shape[0] // BLK
        return lax.dynamic_slice_in_dim(rows, b * count, count, 0)

    w_qkv, w_relq, w_relk, w_out, w_up, w_down = map(
        grow, (w_qkv, w_relq, w_relk, w_out, w_up, w_down)
    )
    b_qkv, b_up, b_out, ln1_gain, ln1_bias, b_down, ln2_gain, ln2_bias = map(
        grow, (b_qkv, b_up, b_out, ln1_gain, ln1_bias, b_down, ln2_gain, ln2_bias)
    )
    rows = w_qkv.shape[0]
    shard = BLK * rows
    ff_part = w_up.shape[1] // (GROUP * BLK)

    vec = jnp.concatenate([b_qkv, b_up, b_out, ln1_gain, ln1_bias, b_down, ln2_gain, ln2_bias])
    vec = jnp.pad(vec, (0, 384 - vec.shape[0]))[None]
    box = boxes[0].T
    tokens = BLK * tok
    sem = pltpu.SemaphoreType.DMA

    def held(*shape, kind=BF16):
        return pltpu.VMEM(shape, kind)

    outs = [
        ((tok, width), BF16),
        ((tok, width), BF16),
        ((5, BLK, rows, HEAD_COLS), BF16),
        ((shard, width), F32),
        ((8, 384), F32),
    ]
    scratch = dict(
        weights=held(CHUNKS, GROUP, shard, HEAD_COLS),
        grads=held(CHUNKS, GROUP, shard, HEAD_COLS),
        pair=held(CHUNKS, GRID_Z, shard, HEAD_COLS),
        line=held(CHUNKS, GRID_Z, shard, HEAD_COLS),
        beside=held(CHUNKS, shard // 2, HEAD_COLS),
        cut=held(5, BLK, rows, HEAD_COLS),
        pack_a=held(BLK, rows, 3 * HEAD_COLS),
        pack_b=held(BLK, rows, GROUP * ff_part),
        pack_vec=held(BLK, 16, width),
        land_a=held(BLK, rows, 3 * HEAD_COLS),
        land_b=held(BLK, rows, GROUP * ff_part),
        land_vec=held(BLK, 16, width),
        all_vec=held(GROUP, 16, width),
        all_hid=held(BLK, tok, width),
        all_box=held(BLK, 8, tok, kind=jnp.int32),
        all_out_a=held(BLK, GROUP * shard, 2 * HEAD_DIM),
        all_out_b=held(BLK, GROUP * shard, HEAD_DIM),
        vec_sum=held(16, width, kind=F32),
        table=held(512, width),
        feats=held(tokens, width),
        qkv=held(9, tokens, HEAD_DIM),
        relq=held(3, width, HEAD_DIM),
        relk=held(3, width, HEAD_DIM),
        qrel=held(tokens, width),
        krel=held(tokens, width),
        probs=held(3, tokens, tokens, kind=F32),
        ctx=held(BLK, tok, third),
        ctx_own=held(BLK, tok, third),
        ctx_all=held(BLK, BLK, tok, third),
        normed_all=held(BLK, tok, width),
        act=held(BLK, tok, GROUP * ff_part),
        slope=held(BLK, tok, GROUP * ff_part, kind=F32),
        branch_all=held(BLK, tok, width),
        g_middle=held(BLK, tok, GROUP * ff_part),
        parts=held(3, BLK, tok, width),
        near=held(3, 2, tok, width),
        far=held(3, tok, width),
        g_attn_own=held(BLK, tok, third),
        g_attn_cols=held(BLK, tok, third),
        g_ctx_own=held(BLK, tok, third),
        g_ctx=held(BLK, tok, third),
        go_heads=held(tokens, HEAD_DIM),
        g_scores=held(tokens, tokens),
        p_low=held(tokens, tokens),
        g_turned=held(2, HEADS, tokens, width),
        g_qkv=held(3, tokens, third),
        gvec=held(16, width, kind=F32),
        gvec_all=held(GROUP, 16, width),
        gvec_page=held(BLK, 16, width, kind=F32),
        ag_x=sem((2, CHUNKS + 1, 4)),
        ag_z=sem((2, CHUNKS + 1, 6)),
        rs_x=sem((2, CHUNKS + 1, 5)),
        rs_z=sem((2, CHUNKS + 1, 6)),
        in_swap=sem((2, 3, 3)),
        gather_sem=sem((2, 8, 3)),
        reduce_sem=sem((2, 3, 3)),
        mid_swap=sem((2, 3, 3)),
        out_swap=sem((2, 5, 3)),
    )
    out, grad_hid, sums, sum_c, vec_own = vmem_call(
        functools.partial(layer_kernel, spread),
        outs,
        list(scratch.values()),
        "layer",
        collective=1,
        smem=(0,),
    )(
        lengths,
        w_qkv,
        w_relq,
        w_relk,
        w_out,
        w_up,
        w_down,
        hidden[0],
        cotangent[0],
        box,
        vec,
    )

    square = ((rows, BLK * third), F32)
    plain = ((1, rows), F32)
    results = vmem_call(
        finish_kernel,
        [
            ((tok, width), BF16),
            ((tok, width), BF16),
            ((rows, 3 * BLK * third), F32),
            ((1, 3 * rows), F32),
            square,
            square,
            square,
            plain,
            plain,
            plain,
            ((rows, GROUP * BLK * ff_part), F32),
            ((1, ff_part), F32),
            ((shard, width), F32),
            plain,
            plain,
            plain,
        ],
        [],
        "finish",
    )(out, grad_hid, sums, sum_c, vec_own)
    flat = [part[0] if part.shape[0] == 1 else part for part in results[2:]]
    return (results[0][None], results[1][None]) + tuple(shrink(part) for part in flat)


def solution(mesh):
    rows = P(("pages", "blk"), None)
    vector = P(("pages", "blk"))
    tokens = P("pages", "blk", None)
    return jax.shard_map(
        on_device,
        mesh=mesh,
        in_specs=(
            tokens,
            tokens,
            P("pages"),
            rows,
            vector,
            rows,
            rows,
            rows,
            vector,
            vector,
            vector,
            rows,
            vector,
            rows,
            vector,
            vector,
            vector,
            tokens,
        ),
        out_specs=(
            tokens,
            tokens,
            rows,
            vector,
            rows,
            rows,
            rows,
            vector,
            vector,
            vector,
            rows,
            vector,
            rows,
            vector,
            vector,
            vector,
        ),
        check_vma=False,
    )
```

```python
import functools
import math

import jax
import jax.numpy as jnp
from jax import lax
from jax.experimental import pallas as pl
from jax.experimental.pallas import tpu as pltpu
from jax.sharding import PartitionSpec as P

HEAD_DIM = 64
FREQ = 192
GRID_Z = 4
GRID_X = 2
GROUP = GRID_Z * GRID_X
BLK = 4
MESH = pl.DeviceIdType.MESH
F32 = jnp.float32
BF16 = jnp.bfloat16
VMEM_BYTES = 56 << 20


def mm(left, right):
    return jnp.dot(left, right, preferred_element_type=F32)


def mm_t(left, right):
    return lax.dot_general(left, right, (((1,), (1,)), ((), ())), preferred_element_type=F32)


def tmm(left, right):
    return lax.dot_general(left, right, (((0,), (0,)), ((), ())), preferred_element_type=F32)


class Place:
    def __init__(self, spread):
        pages = lax.axis_index("pages")
        self.spread = spread
        self.hi = pages // spread
        self.lo = pages % spread
        self.z = self.hi // GRID_X
        self.x = self.hi % GRID_X
        self.b = lax.axis_index("blk")
        self.pages = pages
        self.sib = self.b + 1 - 2 * (self.b % 2)
        self.across = (self.b + 2) % BLK
        self.diag = (self.sib + 2) % BLK

    def at(self, z, x):
        return ((z * GRID_X + x) * self.spread + self.lo, self.b)

    def in_page(self, b):
        return (self.pages, b)

    def blk_peers(self):
        return (self.sib, self.across, self.diag)

    def z_at(self, step):
        return (self.z + step) % GRID_Z


def copy_to(src, dst, send, recv, device):
    return pltpu.make_async_remote_copy(
        src_ref=src, dst_ref=dst, send_sem=send, recv_sem=recv, device_id=device, device_id_type=MESH
    )


def remote(src, dst, send, recv, device):
    return copy_to(src, dst, send, recv, device)


class Hop:
    def __init__(self, here, make):
        self.here, self.make = here, make

    def start(self):
        @pl.when(self.here)
        def _():
            self.make().start()

    def wait_send(self):
        @pl.when(self.here)
        def _():
            self.make().wait_send()


def greet(devices):
    barrier = pltpu.get_barrier_semaphore()
    for device in devices:
        pl.semaphore_signal(barrier, inc=1, device_id=device, device_id_type=MESH)
    return lambda: pl.semaphore_wait(barrier, len(devices))


class BlkGather:
    def __init__(self, place, dst, send, recv):
        self.place, self.dst = place, dst
        b, across = place.b, place.across
        self.to_sib = remote(dst.at[b], dst.at[b], send.at[0], recv.at[0], place.in_page(place.sib))
        self.to_across = remote(dst.at[b], dst.at[b], send.at[1], recv.at[1], place.in_page(across))
        self.forward = remote(
            dst.at[across], dst.at[across], send.at[2], recv.at[2], place.in_page(place.sib)
        )

    def start(self):
        self.to_across.start()
        self.to_sib.start()

    def wait_sib(self):
        self.to_sib.wait_recv()

    def wait_across(self):
        self.to_across.wait_recv()
        self.forward.start()

    def wait_diag(self):
        self.forward.wait_recv()

    def finish(self):
        self.to_sib.wait_send()
        self.to_across.wait_send()
        self.forward.wait_send()


class BlkReduce:
    def __init__(self, place, parts, near, far, send, recv):
        self.place, self.parts, self.near, self.far = place, parts, near, far
        sib, across = place.sib, place.across
        self.sib_far = remote(
            parts.at[place.diag], near.at[1], send.at[0], recv.at[0], place.in_page(sib)
        )
        self.sib_near = remote(parts.at[sib], near.at[0], send.at[1], recv.at[1], place.in_page(sib))
        self.cross = remote(near.at[1], far, send.at[2], recv.at[2], place.in_page(across))

    def send_cross(self):
        self.sib_far.wait_recv()
        both = self.parts[self.place.across].astype(F32) + self.near[1].astype(F32)
        self.near[1] = both.astype(BF16)
        self.cross.start()

    def total(self, own):
        self.sib_near.wait_recv()
        partial = own + self.near[0].astype(F32)
        self.cross.wait_recv()
        return partial + self.far[...].astype(F32)

    def finish(self):
        self.sib_far.wait_send()
        self.sib_near.wait_send()
        self.cross.wait_send()


def vmem_call(kernel, outs, scratch, name, collective=None, smem=()):
    def run(*operands):
        params = dict(vmem_limit_bytes=VMEM_BYTES)
        if collective is not None:
            params.update(collective_id=collective, has_side_effects=True)
        return pl.pallas_call(
            kernel,
            name=name,
            out_shape=[jax.ShapeDtypeStruct(shape, kind) for shape, kind in outs],
            in_specs=[
                pl.BlockSpec(memory_space=pltpu.SMEM if i in smem else pltpu.VMEM)
                for i in range(len(operands))
            ],
            out_specs=[pl.BlockSpec(memory_space=pltpu.VMEM) for _ in outs],
            scratch_shapes=scratch,
            compiler_params=pltpu.CompilerParams(**params),
        )(*operands)

    return run


HEADS = 3
HEAD_COLS = 6 * HEAD_DIM
A_CHUNKS, B_CHUNKS, C_CHUNKS = (0, 1, 2), (3, 4), (5, 6)
CHUNKS = 7
VEC = 7
SPAN = 2 * FREQ


def centred(values):
    mean = jnp.mean(values, axis=-1, keepdims=True)
    centre = values - mean
    scale = lax.rsqrt(jnp.mean(centre * centre, axis=-1, keepdims=True) + 1e-12)
    return centre * scale, scale


def norm_back(grad_hat, hat, scale):
    first = jnp.mean(grad_hat, axis=-1, keepdims=True)
    second = jnp.mean(grad_hat * hat, axis=-1, keepdims=True)
    return scale * (grad_hat - first - hat * second)


def column_sum(values):
    return jnp.sum(values, axis=0, keepdims=True)


def block_rows(blk):
    return pl.ds(pl.multiple_of(blk * 128, 128), 128)


def layer_kernel(
    spread,
    lengths,
    w_qkv,
    w_relq,
    w_relk,
    w_out,
    w_up,
    w_down,
    hidden,
    cot,
    box,
    vec,
    out,
    grad_hid,
    sums,
    sum_c,
    vec_own,
    weights,
    grads,
    pair,
    line,
    beside,
    cut,
    pack_a,
    pack_b,
    pack_vec,
    land_a,
    land_b,
    land_vec,
    all_vec,
    all_hid,
    all_box,
    all_out_a,
    all_out_b,
    vec_sum,
    table,
    feats,
    qkv,
    relq,
    relk,
    qrel,
    krel,
    probs,
    ctx,
    ctx_own,
    ctx_all,
    normed_all,
    act,
    slope,
    branch_all,
    g_middle,
    parts,
    near,
    far,
    g_attn_own,
    g_attn_cols,
    g_ctx_own,
    g_ctx,
    go_heads,
    g_scores,
    p_low,
    g_turned,
    g_qkv,
    gvec,
    gvec_all,
    gvec_page,
    ag_x,
    ag_z,
    rs_x,
    rs_z,
    in_swap,
    gather_sem,
    reduce_sem,
    mid_swap,
    out_swap,
):
    place = Place(spread)
    b = place.b
    peers = place.blk_peers()
    order = (b, place.sib, place.across, place.diag)
    partner = place.at(place.z, 1 - place.x)
    width = hidden.shape[1]
    tokens = BLK * hidden.shape[0]
    third = HEADS * HEAD_DIM
    ff_part = w_up.shape[1] // (GROUP * BLK)
    sends = []


    lower = place.z < 2
    outer = (place.z == 0) | (place.z == GRID_Z - 1)
    targets = (
        jnp.where(lower, 3, 0),
        jnp.where(lower, 2, 1),
        jnp.where(lower, 1 - place.z, 5 - place.z),
        place.z,
    )
    mate = targets[2]

    def start(copy):
        copy.start()
        sends.append(copy)
        return copy

    class Spread:
        def __init__(self, whole, index, sem_x, sem_z):
            self.whole, self.index, self.sem_x, self.sem_z = whole, index, sem_x, sem_z
            self.halved = index != VEC

        def _shard(self, z, x, part=None):
            if part is None or not self.halved:
                return self.whole.at[z * GRID_X + x]
            rows = self.whole.shape[1] // 2
            return self.whole.at[z * GRID_X + x, part * rows : (part + 1) * rows]

        def _along(self, z, slot, to):
            ref = self._shard(z, place.x)
            return copy_to(
                ref,
                ref,
                self.sem_z.at[0, self.index, slot],
                self.sem_z.at[1, self.index, z],
                place.at(to, place.x),
            )

        def _over(self, z, x, part=None):
            ref = self._shard(z, x, part)
            return copy_to(
                ref, ref, self.sem_x.at[0, self.index, z], self.sem_x.at[1, self.index, z], partner
            )

        def _beside(self):
            ref = self._shard(place.z, 1 - place.x, 1)
            return copy_to(
                ref,
                ref,
                self.sem_z.at[0, self.index, GRID_X + place.z],
                self.sem_z.at[1, self.index, GRID_Z],
                place.at(mate, place.x),
            )

        def relay(self):
            self._over(place.z, 1 - place.x).wait_recv()
            if self.halved:
                self._beside().start()

        def begin(self):
            z = place.z
            for slot, (here, to) in enumerate(((z < GRID_Z - 1, z + 1), (z > 0, z - 1))):
                start(Hop(here, functools.partial(self._along, z, slot, to)))

        def cross(self):
            self._over(place.z, place.x).start()

        def pass_on(self, distance):
            z = place.z
            for sign in (1, -1):
                source, to = z - sign * distance, z + sign
                inside = (source >= 0) & (source < GRID_Z)
                more = inside & (to >= 0) & (to < GRID_Z)

                @pl.when(inside)
                def _(source=source, to=to):
                    self._along(source, GRID_X, z).wait_recv()

                start(Hop(more, functools.partial(self._along, source, GRID_X + source, to)))

                if distance > 1:

                    @pl.when(inside)
                    def _(source=source):
                        self._over(source, place.x).start()

                else:

                    @pl.when(inside & (source == mate))
                    def _(source=source):
                        self._over(source, place.x, 0).start()

                    @pl.when(inside & (source != mate))
                    def _(source=source):
                        self._over(source, place.x).start()

        def settle(self):
            for slot in range(2):
                self._over(targets[slot], 1 - place.x).wait_recv()
            self._over(mate, 1 - place.x, 0).wait_recv()
            if self.halved:
                self._beside().wait_recv()

        def finish(self):
            for slot in (0, 1, 3):
                self._over(targets[slot], place.x).wait_send()
            self._over(mate, place.x, 0).wait_send()
            if self.halved:
                self._beside().wait_send()

    half_rows = grads.shape[2] // 2

    class Sum:
        def __init__(self, index):
            self.index = index
            self.grad = grads.at[index]

        def _over(self, slot):
            shard = targets[min(slot, 3)] * GRID_X + 1 - place.x
            src, dst = self.grad.at[shard], pair.at[self.index, min(slot, 3)]
            if slot >= 9:
                rows = slice(half_rows, None) if slot == 4 else slice(0, half_rows)
                src, dst = src.at[rows], dst.at[rows]
            return copy_to(
                src, dst, rs_x.at[0, self.index, slot], rs_x.at[1, self.index, slot], partner
            )

        def _beside(self):
            return copy_to(
                self.grad.at[mate * GRID_X + 1 - place.x, half_rows:],
                beside.at[self.index],
                rs_z.at[0, self.index, 3],
                rs_z.at[1, self.index, 4],
                place.at(mate, place.x),
            )

        def _along(self, slot, land, z):
            return copy_to(
                pair.at[self.index, slot],
                line.at[self.index, land],
                rs_z.at[0, self.index, slot],
                rs_z.at[1, self.index, land],
                place.at(z, place.x),
            )

        def begin(self):
            for slot in range(GRID_Z):
                self._over(slot).start()

        def relay(self):
            return


        def pass_on(self):
            for slot in range(GRID_Z - 1):
                self._over(slot).wait_recv()
                shard = targets[slot] * GRID_X + place.x
                if slot < 9:
                    both = self.grad[shard].astype(F32) + pair[self.index, slot].astype(F32)
                    pair[self.index, slot] = both.astype(BF16)
                else:
                    mine = self.grad[shard, :half_rows].astype(F32)
                    both = mine + pair[self.index, slot, :half_rows].astype(F32)
                    pair[self.index, slot, :half_rows] = both.astype(BF16)
                    pair[self.index, slot, half_rows:] = self.grad[shard, half_rows:]

                def send(slot=slot):
                    self._along(slot, slot, targets[2]).start()

                if slot == 2:
                    send()
                else:
                    pl.when(outer)(send)

        def combine(self):
            @pl.when(jnp.logical_not(outer))
            def _():
                for slot in range(2):
                    self._along(slot, slot, place.z).wait_recv()
                    both = pair[self.index, slot].astype(F32) + line[self.index, slot].astype(F32)
                    pair[self.index, slot] = both.astype(BF16)
                    self._along(slot, 3, targets[slot]).start()

        def finish(self):
            for slot in range(GRID_Z):
                self._over(slot).wait_send()
            for slot in range(GRID_Z - 1):
                self._along(slot, slot, targets[2]).wait_send()

        def settle(self):
            index = self.index
            self._over(3).wait_recv()
            value = self.grad[place.hi].astype(F32) + pair[index, 3].astype(F32)
            for land in (2, 3):
                self._along(2, land, targets[2]).wait_recv()
                value = value + line[index, land].astype(F32)
            if index in C_CHUNKS:
                at = (index - C_CHUNKS[0]) * HEAD_COLS
                sum_c[:, at : at + HEAD_COLS] = value
                return []
            rows = value.shape[0] // BLK
            for blk in range(BLK):
                cut[index, blk] = value[blk * rows : (blk + 1) * rows, :].astype(BF16)
            sums[index, b] = cut[index, b]
            return [
                start(
                    remote(
                        cut.at[index, peer],
                        sums.at[index, b],
                        out_swap.at[0, index, slot],
                        out_swap.at[1, index, slot],
                        place.in_page(peer),
                    )
                )
                for slot, peer in enumerate(peers)
            ]

    def swap(sem, which, source_of, target):
        return [
            start(
                remote(
                    source_of(peer),
                    target.at[b],
                    sem.at[0, which, slot],
                    sem.at[1, which, slot],
                    place.in_page(peer),
                )
            )
            for slot, peer in enumerate(peers)
        ]

    def arrive(copies):
        for copy in copies:
            copy.wait_recv()

    def blk_gather(which, dst):
        return BlkGather(place, dst, gather_sem.at[0, which], gather_sem.at[1, which])

    def blk_reduce(which):
        return BlkReduce(
            place,
            parts.at[which],
            near.at[which],
            far.at[which],
            reduce_sem.at[0, which],
            reduce_sem.at[1, which],
        )

    all_met = greet(
        [place.in_page(peer) for peer in peers]
        + [partner]
        + [place.at(place.z_at(step), place.x) for step in range(1, GRID_Z)]
    )

    for half, index in enumerate(C_CHUNKS):
        weights[index, place.hi] = w_down[:, half * HEAD_COLS : (half + 1) * HEAD_COLS]
    for blk in range(BLK):
        for head in range(HEADS):
            at = blk * third + head * HEAD_DIM
            lanes = slice(at, at + HEAD_DIM)
            columns = [
                w_qkv[:, part * width + at : part * width + at + HEAD_DIM] for part in range(3)
            ]
            columns = columns + [w_relq[:, lanes], w_relk[:, lanes], w_out[:, lanes]]
            pack_a[blk, :, head * HEAD_COLS : (head + 1) * HEAD_COLS] = jnp.concatenate(
                columns, axis=1
            )
    chunk = [Spread(weights.at[index], index, ag_x, ag_z) for index in range(CHUNKS)]
    chunk.append(Spread(all_vec, VEC, ag_x, ag_z))
    all_met()
    swap_a = swap(in_swap, 0, lambda peer: pack_a.at[peer], land_a)
    chunk[5].begin()
    chunk[5].cross()
    bias_part, plain_part = w_qkv.shape[1] // (GROUP * BLK), width // (GROUP * BLK)
    spot = place.hi * BLK + b

    def folded(rows):
        return jnp.concatenate([rows[0:8, : width // 2], rows[0:8, width // 2 :]], axis=0)

    def unfolded(rows):
        return jnp.concatenate([rows[0:8], rows[8:16]], axis=1)

    def home(at):
        wide = at + spot * bias_part
        part = (wide >= width).astype(jnp.int32) + (wide >= 2 * width).astype(jnp.int32)
        rest = wide - part * width
        taker = sum((rest >= third * i).astype(jnp.int32) for i in range(1, BLK))
        rest = rest - third * taker
        head = sum((rest >= HEAD_DIM * i).astype(jnp.int32) for i in range(1, HEADS))
        bias_column = head * third + part * HEAD_DIM + (rest - HEAD_DIM * head)
        plain = at - (bias_part + ff_part)
        kind = sum((plain >= plain_part * i).astype(jnp.int32) for i in range(1, 6))
        plain_column = spot * plain_part + (plain - plain_part * kind)
        up_column = place.hi * ff_part + (at - bias_part)
        is_bias, is_up = at < bias_part, at < bias_part + ff_part
        row = jnp.where(is_bias, 0, jnp.where(is_up, 1, 2 + kind))
        column = jnp.where(is_bias, bias_column, jnp.where(is_up, up_column, plain_column))
        return row, column, jnp.where(is_bias, taker, jnp.where(is_up, b, -1))

    held = vec.shape[1]
    _, column, _ = home(lax.broadcasted_iota(jnp.int32, (held, 1), 0))
    spots = lax.broadcasted_iota(jnp.int32, (held, width), 1) == column
    spots = jnp.where(spots, 1.0, 0.0).astype(BF16)
    row, _, taker = home(lax.broadcasted_iota(jnp.int32, (1, held), 1))
    row_here = lax.broadcasted_iota(jnp.int32, (16, held), 0) == row
    for blk in range(BLK):
        taken = row_here & ((taker == blk) | (taker < 0))
        values = jnp.where(taken, jnp.broadcast_to(vec[...].astype(F32), (16, held)), 0.0)
        pack_vec[blk] = folded(mm(values.astype(BF16), spots)).astype(BF16)
    swap_vec = swap(in_swap, 1, lambda peer: pack_vec.at[peer], land_vec)

    for blk in range(BLK):
        pack_b[blk] = jnp.concatenate(
            [
                w_up[:, (page * BLK + blk) * ff_part : (page * BLK + blk + 1) * ff_part]
                for page in range(GROUP)
            ],
            axis=1,
        )
    swap_b = swap(in_swap, 2, lambda peer: pack_b.at[peer], land_b)
    all_hid[b] = hidden[...]
    all_box[b, 0:2, :] = box[...]
    gather_box = blk_gather(0, all_box)
    gather_hid = blk_gather(1, all_hid)
    gather_box.start()
    gather_hid.start()

    places = lax.broadcasted_iota(jnp.int32, (256, FREQ), 0).astype(F32)
    ladder = lax.broadcasted_iota(jnp.int32, (256, FREQ), 1).astype(F32)
    angles = places * jnp.exp(ladder * (-math.log(10000.0) / FREQ))
    cosines, sines, blank = jnp.cos(angles), jnp.sin(angles), jnp.zeros((256, FREQ), F32)
    table[0:256, :] = jnp.concatenate([cosines, blank, sines, blank], axis=1).astype(BF16)
    table[256:512, :] = jnp.concatenate([blank, cosines, blank, sines], axis=1).astype(BF16)

    land_a[b] = pack_a[b]
    arrive(swap_a)
    joined = jnp.concatenate([land_a[blk].astype(F32) for blk in range(BLK)], axis=0).astype(BF16)
    for head in range(HEADS):
        weights[head, place.hi] = joined[:, head * HEAD_COLS : (head + 1) * HEAD_COLS]
    chunk[0].begin()
    chunk[0].cross()
    land_vec[b] = pack_vec[b]
    arrive(swap_vec)
    all_vec[place.hi] = (
        land_vec[0].astype(F32)
        + land_vec[1].astype(F32)
        + land_vec[2].astype(F32)
        + land_vec[3].astype(F32)
    ).astype(BF16)
    chunk[VEC].begin()
    chunk[VEC].cross()
    chunk[5].pass_on(1)
    land_b[b] = pack_b[b]
    arrive(swap_b)
    joined = jnp.concatenate([land_b[blk].astype(F32) for blk in range(BLK)], axis=0).astype(BF16)
    for half, index in enumerate(B_CHUNKS):
        weights[index, place.hi] = joined[:, half * HEAD_COLS : (half + 1) * HEAD_COLS]
    chunk[5].relay()
    chunk[5].pass_on(2)
    chunk[0].pass_on(1)
    chunk[1].begin()
    chunk[1].cross()
    gather_box.wait_across()
    gather_hid.wait_across()
    chunk[VEC].pass_on(1)
    gather_box.wait_sib()
    gather_box.wait_diag()
    slots = lax.broadcasted_iota(jnp.int32, (256, tokens // BLK), 0)
    for blk in range(BLK):
        hot = jnp.concatenate(
            [
                jnp.where(slots == all_box[blk][0:1, :], 1.0, 0.0),
                jnp.where(slots == all_box[blk][1:2, :], 1.0, 0.0),
            ],
            axis=0,
        ).astype(BF16)
        feats[blk * 128 : (blk + 1) * 128, :] = tmm(hot, table[...]).astype(BF16)
    chunk[5].pass_on(3)
    chunk[0].relay()
    chunk[0].pass_on(2)
    chunk[VEC].relay()
    chunk[VEC].pass_on(2)
    chunk[1].pass_on(1)
    chunk[2].begin()
    chunk[2].cross()
    chunk[0].pass_on(3)
    chunk[VEC].pass_on(3)
    gather_hid.wait_sib()
    gather_hid.wait_diag()
    chunk[1].relay()
    chunk[1].pass_on(2)
    chunk[VEC].settle()
    total = all_vec[0].astype(F32)
    for shard in range(1, GROUP):
        total = total + all_vec[shard].astype(F32)
    vec_sum[...] = unfolded(total)

    rows_whole = GROUP * weights.shape[2]
    whole = weights.reshape(CHUNKS, rows_whole, HEAD_COLS)
    hid = all_hid.reshape(tokens, width)
    usable = lax.broadcasted_iota(jnp.int32, (tokens, tokens), 1) < lengths[0]

    gather_out = [blk_gather(2, all_out_a), blk_gather(7, all_out_b)]

    def head_forward(head):
        out_part = whole[head, :, 5 * HEAD_DIM : 6 * HEAD_DIM]
        if head == 2:
            all_out_b[b] = out_part
            gather_out[1].start()
        else:
            all_out_a[b, :, head * HEAD_DIM : (head + 1) * HEAD_DIM] = out_part
        if head == 1:
            gather_out[0].start()
        bias = vec_sum[0:1, head * 3 * HEAD_DIM : (head + 1) * 3 * HEAD_DIM]
        low = (mm(hid[...], whole[head, :, : 3 * HEAD_DIM]) + bias).astype(BF16)
        for part in range(3):
            qkv[3 * part + head] = low[:, part * HEAD_DIM : (part + 1) * HEAD_DIM]
        relq[head] = whole[head, :, 3 * HEAD_DIM : 4 * HEAD_DIM]
        relk[head] = whole[head, :, 4 * HEAD_DIM : 5 * HEAD_DIM]
        yield

        def turn(blk, carry):
            rows = pl.ds(pl.multiple_of(blk * 256, 256), 256)
            cos_part = feats[rows, :SPAN].astype(F32)
            sin_part = feats[rows, SPAN:].astype(F32)
            u = mm_t(qkv[head, rows, :], relq[head])
            u1, u2 = u[:, :SPAN], u[:, SPAN:]
            qrel[rows, :SPAN] = (u1 * cos_part + u2 * sin_part).astype(BF16)
            qrel[rows, SPAN:] = (u1 * sin_part - u2 * cos_part).astype(BF16)
            v = mm_t(qkv[3 + head, rows, :], relk[head])
            v1, v2 = v[:, :SPAN], v[:, SPAN:]
            krel[rows, :SPAN] = (v1 * cos_part - v2 * sin_part).astype(BF16)
            krel[rows, SPAN:] = (v1 * sin_part + v2 * cos_part).astype(BF16)
            return carry

        lax.fori_loop(0, tokens // 256, turn, 0)
        yield
        scores = mm_t(qrel[...], feats[...])
        scores = scores + mm_t(feats[...], krel[...])
        scores = scores + mm_t(qkv[head], qkv[3 + head])
        masked = jnp.where(usable, scores * 0.125, -1e30)
        raised = jnp.exp(masked - jnp.max(masked, axis=-1, keepdims=True))
        prob = raised / jnp.sum(raised, axis=-1, keepdims=True)
        probs[head] = prob
        found = mm(prob.astype(BF16), qkv[6 + head]).astype(BF16)
        for blk in range(BLK):
            ctx[blk, :, head * HEAD_DIM : (head + 1) * HEAD_DIM] = found[
                blk * 128 : (blk + 1) * 128, :
            ]
        yield

    def run(generator, events):
        at = 0
        for _ in generator:
            for event in events.get(at, ()):
                event()
            at += 1

    chunk[2].pass_on(1)
    chunk[3].begin()
    chunk[3].cross()
    chunk[0].settle()

    def later(call, *rest):
        return functools.partial(call, *rest)

    run(head_forward(0), {0: (later(chunk[1].pass_on, 3),)})
    chunk[2].relay()
    chunk[2].pass_on(2)
    chunk[1].settle()
    run(
        head_forward(1),
        {
            0: (later(chunk[3].pass_on, 1), chunk[4].begin, chunk[4].cross),
            1: (later(chunk[2].pass_on, 3),),
        },
    )
    chunk[3].relay()
    chunk[3].pass_on(2)
    chunk[4].pass_on(1)
    chunk[6].begin()
    chunk[6].cross()
    chunk[2].settle()
    run(
        head_forward(2),
        {
            0: (gather_out[0].wait_across,),
            1: (later(chunk[3].pass_on, 3),),
        },
    )

    swap_ctx = swap(mid_swap, 0, lambda peer: ctx.at[peer], ctx_own)
    ctx_own[b] = ctx[b]
    chunk[4].relay()
    chunk[4].pass_on(2)
    chunk[6].pass_on(1)
    gather_out[1].wait_across()
    for gather in gather_out:
        gather.wait_sib()
        gather.wait_diag()
    arrive(swap_ctx)
    own = jnp.concatenate([ctx_own[blk] for blk in range(BLK)], axis=1)
    attn = jnp.concatenate(
        [mm(own, part[blk]) for blk in range(BLK) for part in (all_out_a, all_out_b)], axis=1
    )
    attn = attn + vec_sum[2:3, :]
    hat_one, scale_one = centred(hidden[...].astype(F32) + attn)
    gain_one = vec_sum[3:4, :]
    normed = hat_one * gain_one + vec_sum[4:5, :]
    normed_all[b] = normed.astype(BF16)
    gather_normed = blk_gather(3, normed_all)
    gather_normed.start()
    chunk[4].pass_on(3)
    chunk[6].relay()
    chunk[6].pass_on(2)
    chunk[3].settle()
    chunk[4].settle()
    reduce_one = blk_reduce(0)

    def up(blk):
        for half, index in enumerate(B_CHUNKS):
            lanes = slice(half * HEAD_COLS, (half + 1) * HEAD_COLS)
            middle = mm(normed_all[blk], whole[index]) + vec_sum[1:2, lanes]
            gate = 0.5 * (1.0 + lax.erf(middle * math.sqrt(0.5)))
            act[blk, :, lanes] = (middle * gate).astype(BF16)
            bell = jnp.exp(-0.5 * middle * middle) * (1.0 / math.sqrt(2.0 * math.pi))
            slope[blk, :, lanes] = gate + middle * bell

    def down(blk):
        return jnp.concatenate([mm(act[blk], whole[index]) for index in C_CHUNKS], axis=1)

    up(b)
    chunk[6].pass_on(3)
    gather_normed.wait_sib()
    up(place.sib)
    gather_normed.wait_across()
    up(place.across)
    gather_normed.wait_diag()
    up(place.diag)
    chunk[5].settle()
    chunk[6].settle()
    parts[0, place.diag] = down(place.diag).astype(BF16)
    reduce_one.sib_far.start()
    parts[0, place.across] = down(place.across).astype(BF16)
    parts[0, place.sib] = down(place.sib).astype(BF16)
    reduce_one.sib_near.start()
    own_branch = down(b)
    reduce_one.send_cross()
    branch = reduce_one.total(own_branch) + vec_sum[5:6, :]

    hat_two, scale_two = centred(normed + branch)
    gain_two = vec_sum[6:7, :]
    cot_wide = cot[...].astype(F32)
    g_two = norm_back(cot_wide * gain_two, hat_two, scale_two)
    branch_all[b] = g_two.astype(BF16)
    gather_branch = blk_gather(4, branch_all)
    gather_branch.start()
    out[...] = (hat_two * gain_two + vec_sum[7:8, :]).astype(BF16)
    gvec[6:7, :] = column_sum(cot_wide * hat_two)
    gvec[7:8, :] = column_sum(cot_wide)
    gvec[5:6, :] = column_sum(branch_all[b].astype(F32))
    reduce_two = blk_reduce(1)

    def back(blk):
        slab = mm_t(branch_all[blk, :, :HEAD_COLS], whole[C_CHUNKS[0]])
        slab = slab + mm_t(branch_all[blk, :, HEAD_COLS:], whole[C_CHUNKS[1]])
        low = (slab * slope[blk]).astype(BF16)
        g_middle[blk] = low
        part = mm_t(low[:, :HEAD_COLS], whole[B_CHUNKS[0]])
        return part + mm_t(low[:, HEAD_COLS:], whole[B_CHUNKS[1]])

    own_normed = back(b)
    gather_branch.wait_sib()
    parts[1, place.sib] = back(place.sib).astype(BF16)
    reduce_two.sib_near.start()
    gather_branch.wait_across()
    parts[1, place.across] = back(place.across).astype(BF16)
    gather_branch.wait_diag()
    parts[1, place.diag] = back(place.diag).astype(BF16)
    reduce_two.sib_far.start()

    act_rows = act.reshape(tokens, act.shape[2])
    branch_rows = branch_all.reshape(tokens, width)
    normed_rows = normed_all.reshape(tokens, width)
    middle_rows = g_middle.reshape(tokens, act.shape[2])
    flat_grads = grads.reshape(CHUNKS, rows_whole, HEAD_COLS)

    def weight_grad(indices, left, right):
        def step(at, carry):
            cols = pl.ds(pl.multiple_of(at * 256, 256), 256)
            both = tmm(left[:, cols], right[...]).astype(BF16)
            for half, index in enumerate(indices):
                flat_grads[index, cols, :] = both[:, half * HEAD_COLS : (half + 1) * HEAD_COLS]
            return carry

        lax.fori_loop(0, rows_whole // 256, step, 0)

    summed = [Sum(index) for index in range(CHUNKS)]
    weight_grad(C_CHUNKS, act_rows, branch_rows)
    summed[5].begin()
    summed[6].begin()
    reduce_two.send_cross()
    weight_grad(B_CHUNKS, normed_rows, middle_rows)
    summed[3].begin()
    summed[4].begin()
    gvec[1:2, :] = column_sum(middle_rows[...].astype(F32))
    for index in (5, 6, 3, 4):
        summed[index].relay()
    g_normed = g_two + reduce_two.total(own_normed)

    g_one = norm_back(g_normed * gain_one, hat_one, scale_one)
    g_attn = g_one.astype(BF16)
    for blk in range(BLK):
        g_attn_own[blk] = g_attn[:, blk * third : (blk + 1) * third]
    wide = jnp.zeros(g_one.shape, F32)
    for blk in range(BLK):
        wide = wide + mm_t(g_attn_own[blk, :, : 2 * HEAD_DIM], all_out_a[blk])
        wide = wide + mm_t(g_attn_own[blk, :, 2 * HEAD_DIM :], all_out_b[blk])
    for blk in range(BLK):
        g_ctx_own[blk] = wide[:, blk * third : (blk + 1) * third].astype(BF16)
    swap_back = swap(mid_swap, 1, lambda peer: g_ctx_own.at[peer], g_ctx)
    g_ctx[b] = g_ctx_own[b]
    gvec[3:4, :] = column_sum(g_normed * hat_one)
    gvec[4:5, :] = column_sum(g_normed)
    gvec[2:3, :] = column_sum(g_attn.astype(F32))
    summed[5].pass_on()
    arrive(swap_back)
    swap_attn = swap(mid_swap, 2, lambda peer: g_attn_own.at[peer], g_attn_cols)
    g_attn_cols[b] = g_attn_own[b]
    ctx_all[b] = ctx[...]
    gather_ctx = blk_gather(6, ctx_all)
    gather_ctx.start()

    g_ctx_rows = g_ctx.reshape(tokens, third)
    ctx_rows = ctx.reshape(tokens, third)

    def head_backward(head):
        lanes = slice(head * HEAD_DIM, (head + 1) * HEAD_DIM)
        go_heads[...] = g_ctx_rows[:, lanes]
        go = go_heads[...]
        delta = jnp.sum(
            go.astype(F32) * ctx_rows[:, lanes].astype(F32), axis=-1, keepdims=True
        )
        prob = probs[head]
        p_low[...] = prob.astype(BF16)
        g_scores[...] = (prob * (mm_t(go, qkv[6 + head]) - delta)).astype(BF16)
        cos_part = feats[:, :SPAN].astype(F32)
        sin_part = feats[:, SPAN:].astype(F32)
        turned = 0.125 * mm(g_scores[...], feats[...])
        a1, a2 = turned[:, :SPAN], turned[:, SPAN:]
        g_turned[0, head, :, :SPAN] = (a1 * cos_part + a2 * sin_part).astype(BF16)
        g_turned[0, head, :, SPAN:] = (a1 * sin_part - a2 * cos_part).astype(BF16)
        gq = 0.125 * mm(g_scores[...], qkv[3 + head]) + mm(g_turned[0, head], relq[head])
        turned = 0.125 * tmm(g_scores[...], feats[...])
        b1, b2 = turned[:, :SPAN], turned[:, SPAN:]
        g_turned[1, head, :, :SPAN] = (b1 * cos_part + b2 * sin_part).astype(BF16)
        g_turned[1, head, :, SPAN:] = (b2 * cos_part - b1 * sin_part).astype(BF16)
        gk = 0.125 * tmm(g_scores[...], qkv[head]) + mm(g_turned[1, head], relk[head])
        g_value = tmm(p_low[...], go)
        g_qkv[head] = jnp.concatenate([gq, gk, g_value], axis=1).astype(BF16)
        gvec[0:1, head * third : (head + 1) * third] = column_sum(g_qkv[head].astype(F32))

    def head_grads(head):
        lanes = slice(head * HEAD_DIM, (head + 1) * HEAD_DIM)
        for at in range(rows_whole // 256):
            cols = slice(at * 256, (at + 1) * 256)
            flat_grads[head, cols, :] = jnp.concatenate(
                [
                    tmm(hid[:, cols], g_qkv[head]),
                    tmm(g_turned[0, head, :, cols], qkv[head]),
                    tmm(g_turned[1, head, :, cols], qkv[3 + head]),
                    tmm(ctx_flat(at), g_attn_cols_rows[:, lanes]),
                ],
                axis=1,
            ).astype(BF16)

    g_attn_cols_rows = g_attn_cols.reshape(tokens, third)

    def ctx_flat(at):
        pieces, start_col = [], at * 256
        while start_col < (at + 1) * 256:
            owner = start_col // third
            stop = min((owner + 1) * third, (at + 1) * 256)
            pieces.append(
                ctx_all.reshape(BLK, tokens, third)[
                    owner, :, start_col - owner * third : stop - owner * third
                ]
            )
            start_col = stop
        return jnp.concatenate(pieces, axis=1)

    finals = []

    def settle(index):
        finals.extend(summed[index].settle())

    gvec[0:1, 3 * third :] = jnp.zeros((1, width - 3 * third), F32)
    head_backward(0)
    head_backward(1)
    gather_ctx.wait_across()
    head_backward(2)
    gvec_all[place.hi] = folded(gvec[...]).astype(BF16)
    vec_back = Spread(gvec_all, VEC, rs_x, rs_z)
    vec_back.begin()
    vec_back.cross()
    arrive(swap_attn)
    gather_ctx.wait_sib()
    gather_ctx.wait_diag()
    head_grads(0)
    summed[0].begin()
    summed[6].pass_on()
    vec_back.pass_on(1)
    head_grads(1)
    summed[5].combine()
    summed[1].begin()
    summed[0].relay()
    vec_back.relay()
    vec_back.pass_on(2)
    head_grads(2)
    summed[2].begin()
    summed[1].relay()
    summed[3].pass_on()
    summed[6].combine()
    vec_back.pass_on(3)
    summed[2].relay()
    reduce_hid = blk_reduce(2)

    def part_hid(blk):
        total = mm_t(g_qkv[0, block_rows(blk), :], whole[0, :, :third])
        for head in range(1, HEADS):
            total = total + mm_t(g_qkv[head, block_rows(blk), :], whole[head, :, :third])
        return total

    parts[2, place.diag] = part_hid(place.diag).astype(BF16)
    reduce_hid.sib_far.start()
    parts[2, place.across] = part_hid(place.across).astype(BF16)
    reduce_hid.send_cross()
    parts[2, place.sib] = part_hid(place.sib).astype(BF16)
    reduce_hid.sib_near.start()
    own_hid = part_hid(b) + g_one
    summed[3].combine()
    summed[4].pass_on()
    grad_hid[...] = reduce_hid.total(own_hid).astype(BF16)
    summed[4].combine()
    summed[0].pass_on()
    vec_back.settle()
    total = gvec_all[0].astype(F32)
    for shard in range(1, GROUP):
        total = total + gvec_all[shard].astype(F32)
    gvec_page[b] = unfolded(total)
    gather_vec = blk_gather(5, gvec_page)
    gather_vec.start()
    summed[0].combine()
    summed[1].pass_on()
    gather_vec.wait_across()
    gather_vec.wait_sib()
    gather_vec.wait_diag()

    _, column, taker = home(lax.broadcasted_iota(jnp.int32, (1, held), 1))
    places = lax.broadcasted_iota(jnp.int32, (width, held), 0) == column
    places = jnp.where(places, 1.0, 0.0)
    plain = gvec_page[0] + gvec_page[1] + gvec_page[2] + gvec_page[3]
    plain_row = lax.broadcasted_iota(jnp.int32, (8, width), 0)
    plain = jnp.where(plain_row < 2, 0.0, plain)
    bias_all = jnp.concatenate([gvec_page[blk][0:1, :] for blk in range(BLK)], axis=0)
    stacked = jnp.concatenate([plain, bias_all, gvec_page[b][1:2, :], bias_all[0:3, :]], axis=0)
    picked = jnp.dot(stacked, places, preferred_element_type=F32, precision=lax.Precision.HIGHEST)
    own_bias = jnp.zeros((1, held), F32)
    for blk in range(BLK):
        own_bias = own_bias + jnp.where(taker == blk, picked[8 + blk : 9 + blk, :], 0.0)
    vec_own[...] = jnp.concatenate([own_bias, picked[12:13, :], picked[2:8, :]], axis=0)

    settle(5)
    settle(6)
    summed[1].combine()
    summed[2].pass_on()
    settle(3)
    settle(4)
    summed[2].combine()
    settle(0)
    settle(1)
    settle(2)
    arrive(finals)
    for part in chunk + summed + [vec_back]:
        part.finish()
    for copy in sends:
        copy.wait_send()
    for reduce in (reduce_one, reduce_two, reduce_hid):
        reduce.finish()
    for gather in (gather_box, gather_hid, *gather_out, gather_normed, gather_branch, gather_ctx, gather_vec):
        gather.finish()


def finish_kernel(
    out_in,
    hid_in,
    sums,
    sum_c,
    vec,
    out,
    grad_hid,
    g_qkv,
    g_bias,
    g_relq,
    g_relk,
    g_out,
    g_out_bias,
    g_gain_one,
    g_shift_one,
    g_up,
    g_up_bias,
    g_down,
    g_down_bias,
    g_gain_two,
    g_shift_two,
):
    out[...] = out_in[...]
    grad_hid[...] = hid_in[...]
    g_down[...] = sum_c[...]
    width = sum_c.shape[1]
    pieces = [
        [sums[head, blk].astype(F32) for blk in range(BLK)] for head in range(HEADS)
    ]

    def gathered(part):
        lanes = slice(part * HEAD_DIM, (part + 1) * HEAD_DIM)
        return jnp.concatenate(
            [pieces[head][blk][:, lanes] for blk in range(BLK) for head in range(HEADS)], axis=1
        )

    for part in range(3):
        g_qkv[:, part * width : (part + 1) * width] = gathered(part)
    g_relq[...] = gathered(3)
    g_relk[...] = gathered(4)
    g_out[...] = gathered(5)
    per_chunk = GROUP // len(B_CHUNKS)
    part = HEAD_COLS // per_chunk
    for half, index in enumerate(B_CHUNKS):
        wide = [sums[index, blk].astype(F32) for blk in range(BLK)]
        columns = jnp.concatenate(
            [
                wide[blk][:, page * part : (page + 1) * part]
                for page in range(per_chunk)
                for blk in range(BLK)
            ],
            axis=1,
        )
        g_up[:, half * columns.shape[1] : (half + 1) * columns.shape[1]] = columns
    for row, target in enumerate(
        (g_bias, g_up_bias, g_out_bias, g_gain_one, g_shift_one, g_down_bias, g_gain_two, g_shift_two)
    ):
        first = 0 if row == 0 else g_bias.shape[1]
        if row > 1:
            first = first + g_up_bias.shape[1] + (row - 2) * target.shape[1]
        target[...] = vec[row : row + 1, first : first + target.shape[1]]


def on_device(
    hidden,
    boxes,
    lengths,
    w_qkv,
    b_qkv,
    w_relq,
    w_relk,
    w_out,
    b_out,
    ln1_gain,
    ln1_bias,
    w_up,
    b_up,
    w_down,
    b_down,
    ln2_gain,
    ln2_bias,
    cotangent,
):
    page_count = lax.axis_size("pages")
    spread = page_count // GROUP
    b = lax.axis_index("blk")
    hi = lax.axis_index("pages") // spread
    _, tok, width = hidden.shape
    third = 3 * HEAD_DIM
    groups = [[h * spread + low for low in range(spread)] for h in range(GROUP)]

    def grow(rows):
        if spread == 1:
            return rows
        rows = lax.all_gather(rows, "blk", axis=0, tiled=True)
        rows = lax.all_gather(rows, "pages", axis=0, tiled=True, axis_index_groups=groups)
        count = rows.shape[0] // BLK
        return lax.dynamic_slice_in_dim(rows, b * count, count, 0)

    def shrink(rows):
        if spread == 1:
            return rows
        rows = lax.all_gather(rows, "blk", axis=0, tiled=True)
        rows = lax.psum_scatter(
            rows, "pages", scatter_dimension=0, tiled=True, axis_index_groups=groups
        )
        count = rows.shape[0] // BLK
        return lax.dynamic_slice_in_dim(rows, b * count, count, 0)

    w_qkv, w_relq, w_relk, w_out, w_up, w_down = map(
        grow, (w_qkv, w_relq, w_relk, w_out, w_up, w_down)
    )
    b_qkv, b_up, b_out, ln1_gain, ln1_bias, b_down, ln2_gain, ln2_bias = map(
        grow, (b_qkv, b_up, b_out, ln1_gain, ln1_bias, b_down, ln2_gain, ln2_bias)
    )
    rows = w_qkv.shape[0]
    shard = BLK * rows
    ff_part = w_up.shape[1] // (GROUP * BLK)

    vec = jnp.concatenate([b_qkv, b_up, b_out, ln1_gain, ln1_bias, b_down, ln2_gain, ln2_bias])
    vec = jnp.pad(vec, (0, 384 - vec.shape[0]))[None]
    box = boxes[0].T
    tokens = BLK * tok
    sem = pltpu.SemaphoreType.DMA

    def held(*shape, kind=BF16):
        return pltpu.VMEM(shape, kind)

    outs = [
        ((tok, width), BF16),
        ((tok, width), BF16),
        ((5, BLK, rows, HEAD_COLS), BF16),
        ((shard, width), F32),
        ((8, 384), F32),
    ]
    scratch = dict(
        weights=held(CHUNKS, GROUP, shard, HEAD_COLS),
        grads=held(CHUNKS, GROUP, shard, HEAD_COLS),
        pair=held(CHUNKS, GRID_Z, shard, HEAD_COLS),
        line=held(CHUNKS, GRID_Z, shard, HEAD_COLS),
        beside=held(CHUNKS, shard // 2, HEAD_COLS),
        cut=held(5, BLK, rows, HEAD_COLS),
        pack_a=held(BLK, rows, 3 * HEAD_COLS),
        pack_b=held(BLK, rows, GROUP * ff_part),
        pack_vec=held(BLK, 16, width // 2),
        land_a=held(BLK, rows, 3 * HEAD_COLS),
        land_b=held(BLK, rows, GROUP * ff_part),
        land_vec=held(BLK, 16, width // 2),
        all_vec=held(GROUP, 16, width // 2),
        all_hid=held(BLK, tok, width),
        all_box=held(BLK, 8, tok, kind=jnp.int32),
        all_out_a=held(BLK, GROUP * shard, 2 * HEAD_DIM),
        all_out_b=held(BLK, GROUP * shard, HEAD_DIM),
        vec_sum=held(8, width, kind=F32),
        table=held(512, width),
        feats=held(tokens, width),
        qkv=held(9, tokens, HEAD_DIM),
        relq=held(3, width, HEAD_DIM),
        relk=held(3, width, HEAD_DIM),
        qrel=held(tokens, width),
        krel=held(tokens, width),
        probs=held(3, tokens, tokens, kind=F32),
        ctx=held(BLK, tok, third),
        ctx_own=held(BLK, tok, third),
        ctx_all=held(BLK, BLK, tok, third),
        normed_all=held(BLK, tok, width),
        act=held(BLK, tok, GROUP * ff_part),
        slope=held(BLK, tok, GROUP * ff_part, kind=F32),
        branch_all=held(BLK, tok, width),
        g_middle=held(BLK, tok, GROUP * ff_part),
        parts=held(3, BLK, tok, width),
        near=held(3, 2, tok, width),
        far=held(3, tok, width),
        g_attn_own=held(BLK, tok, third),
        g_attn_cols=held(BLK, tok, third),
        g_ctx_own=held(BLK, tok, third),
        g_ctx=held(BLK, tok, third),
        go_heads=held(tokens, HEAD_DIM),
        g_scores=held(tokens, tokens),
        p_low=held(tokens, tokens),
        g_turned=held(2, HEADS, tokens, width),
        g_qkv=held(3, tokens, third),
        gvec=held(8, width, kind=F32),
        gvec_all=held(GROUP, 16, width // 2),
        gvec_page=held(BLK, 8, width, kind=F32),
        ag_x=sem((2, CHUNKS + 1, 4)),
        ag_z=sem((2, CHUNKS + 1, 6)),
        rs_x=sem((2, CHUNKS + 1, 5)),
        rs_z=sem((2, CHUNKS + 1, 6)),
        in_swap=sem((2, 3, 3)),
        gather_sem=sem((2, 8, 3)),
        reduce_sem=sem((2, 3, 3)),
        mid_swap=sem((2, 3, 3)),
        out_swap=sem((2, 5, 3)),
    )
    out, grad_hid, sums, sum_c, vec_own = vmem_call(
        functools.partial(layer_kernel, spread),
        outs,
        list(scratch.values()),
        "layer",
        collective=1,
        smem=(0,),
    )(
        lengths,
        w_qkv,
        w_relq,
        w_relk,
        w_out,
        w_up,
        w_down,
        hidden[0],
        cotangent[0],
        box,
        vec,
    )

    square = ((rows, BLK * third), F32)
    plain = ((1, rows), F32)
    results = vmem_call(
        finish_kernel,
        [
            ((tok, width), BF16),
            ((tok, width), BF16),
            ((rows, 3 * BLK * third), F32),
            ((1, 3 * rows), F32),
            square,
            square,
            square,
            plain,
            plain,
            plain,
            ((rows, GROUP * BLK * ff_part), F32),
            ((1, ff_part), F32),
            ((shard, width), F32),
            plain,
            plain,
            plain,
        ],
        [],
        "finish",
    )(out, grad_hid, sums, sum_c, vec_own)
    flat = [part[0] if part.shape[0] == 1 else part for part in results[2:]]
    return (results[0][None], results[1][None]) + tuple(shrink(part) for part in flat)


def solution(mesh):
    rows = P(("pages", "blk"), None)
    vector = P(("pages", "blk"))
    tokens = P("pages", "blk", None)
    return jax.shard_map(
        on_device,
        mesh=mesh,
        in_specs=(
            tokens,
            tokens,
            P("pages"),
            rows,
            vector,
            rows,
            rows,
            rows,
            vector,
            vector,
            vector,
            rows,
            vector,
            rows,
            vector,
            vector,
            vector,
            tokens,
        ),
        out_specs=(
            tokens,
            tokens,
            rows,
            vector,
            rows,
            rows,
            rows,
            vector,
            vector,
            vector,
            rows,
            vector,
            rows,
            vector,
            vector,
            vector,
        ),
        check_vma=False,
    )
```
